128 devices in a mesh: row: 8 (over y, core), col: 16 (over x, z).
Axes of the slice: x: 4, y: 4, z: 4, core: 2. Of those that a mesh axis runs over, the one named last changes fastest.
Arguments:
- camera_jacobian: float32 [18, 8, 131072], P(None, None, ('row', 'col')), may hold values from -6 to 6
- point_jacobian: float32 [6, 8, 131072], P(None, None, ('row', 'col')), may hold values from -6 to 6
- residuals: float32 [2, 8, 131072], P(None, None, ('row', 'col')), may hold values from -6 to 6
- observed_camera: int32 [8, 131072], P(None, ('row', 'col')), may hold values from 0 to 49151, as said below
- track_length: int32 [131072], P(('row', 'col')), may hold values from 2 to 8
Outputs:
- camera_move: float32 [9, 49152], P(None, ('row', 'col'))
- point_move: float32 [3, 131072], P(None, ('row', 'col'))
The draws below stay inside these ranges and needn't reach their ends.
Inputs may be any that keep to these rules, and one draw needn't show every extreme that they name: `observed_camera`: the 8 cameras listed for one point are all different.
All inputs are finite; a program needn't handle non-finite values.
Results may differ from the reference program's by a relative error of at most 0.0003.
Values sent between devices are 32-bit elements; how exact they have to be, the bound alone decides.
No kernel may reach another device: no remote copies, remote signals or barrier semaphores. Data moves between devices by JAX's collectives and lax.ppermute only.
A program may use at most 128 MiB of HBM per device.

```python
import jax
import jax.numpy as jnp
from jax import lax

PT_DEV = 1024
TRACK = 8
ITERS = 2
NCAM = 49152
NPT = 131072
DEVICES = 128


def draw_observed_camera(key, part):
    key = jax.random.fold_in(key, 11)
    first_key, second_key = jax.random.split(key)
    window = NCAM // TRACK
    anchor = jax.random.randint(first_key, (1, NPT), 0, NCAM)
    offsets = jax.random.randint(second_key, (TRACK, NPT), 0, window)
    spaced = anchor + jnp.arange(TRACK, dtype=jnp.int32)[:, None] * window + offsets
    return (spaced % NCAM).astype(jnp.int32)


def with_ends(drawn, key, least, largest):
    extent = drawn.shape
    spot = [jax.random.randint(jax.random.fold_in(key, axis), (), 0, extent[axis]) for axis in range(len(extent))]
    drawn = drawn.at[tuple(spot)].set(least)
    longest = extent.index(max(extent))
    spot[longest] = (spot[longest] + 1) % extent[longest]
    return drawn.at[tuple(spot)].set(largest)


def steps_of(own_key, dims, cuts, least, largest):
    def one(axis_at, blocks):
        steps = jax.random.uniform(jax.random.fold_in(jax.random.fold_in(own_key, 6), axis_at), (blocks,), jnp.float32, least / len(cuts), largest / len(cuts))
        return jnp.repeat(jnp.exp(steps), dims[axis_at] // blocks).reshape((-1,) + (1,) * (len(dims) - axis_at - 1))

    loudness = one(*cuts[0])
    for cut in cuts[1:]:
        loudness = loudness * one(*cut)
    return loudness


def normal_values(rng, dims, deviation, most, shards=(), held_as=jnp.bfloat16):
    gain = steps_of(rng, dims, shards, -0.22, 0.18) if shards else 1.0
    drawn = jax.random.normal(rng, dims, jnp.float32) * deviation * gain
    return jnp.minimum(jnp.maximum(drawn, -most), most).astype(held_as)


def setup_inputs(seed: int = 0) -> dict:
    keys = jax.random.split(jax.random.key(seed), 6)
    camera_jacobian = normal_values(keys[0], (18, TRACK, NPT), 1.0, 6.0, ((2, 128),), jnp.float32)
    point_jacobian = normal_values(keys[1], (6, TRACK, NPT), 1.0, 6.0, ((2, 128),), jnp.float32)
    residuals = normal_values(keys[2], (2, TRACK, NPT), 1.0, 6.0, ((2, 128),), jnp.float32)
    observed_camera = draw_observed_camera(jax.random.fold_in(keys[5], 71), 0)
    track_length = with_ends(jax.random.randint(keys[4], (NPT,), 2, TRACK + 1), jax.random.fold_in(keys[4], 1), 2, TRACK).astype(jnp.int32)
    return dict(camera_jacobian=camera_jacobian, point_jacobian=point_jacobian, residuals=residuals, observed_camera=observed_camera, track_length=track_length)


damping = 1.0
block_pairs = [(leading, trailing) for leading in range(9) for trailing in range(leading, 9)]

def inverse_small(matrix):
    entries = [[matrix[row_at, col_at] for col_at in range(3)] for row_at in range(3)]
    cofactor = [[entries[(row_at + 1) % 3][(col_at + 1) % 3] * entries[(row_at + 2) % 3][(col_at + 2) % 3] - entries[(row_at + 1) % 3][(col_at + 2) % 3] * entries[(row_at + 2) % 3][(col_at + 1) % 3] for col_at in range(3)] for row_at in range(3)]
    determinant = entries[0][0] * cofactor[0][0] + entries[0][1] * cofactor[0][1] + entries[0][2] * cofactor[0][2]
    return jnp.stack([jnp.stack([cofactor[col_at][row_at] / determinant for col_at in range(3)]) for row_at in range(3)])

def block_inverse(matrix):
    factor = {}
    for col_at in range(9):
        pivot_value = matrix[col_at, col_at]
        for middle in range(col_at):
            pivot_value = pivot_value - factor[col_at, middle] * factor[col_at, middle]
        diagonal_root = jnp.sqrt(pivot_value)
        factor[col_at, col_at] = diagonal_root
        for row_at in range(col_at + 1, 9):
            running = matrix[row_at, col_at]
            for middle in range(col_at):
                running = running - factor[row_at, middle] * factor[col_at, middle]
            factor[row_at, col_at] = running / diagonal_root
    factor_inverse = {}
    for row_at in range(9):
        factor_inverse[row_at, row_at] = 1.0 / factor[row_at, row_at]
        for col_at in range(row_at):
            running = factor[row_at, col_at] * factor_inverse[col_at, col_at]
            for middle in range(col_at + 1, row_at):
                running = running + factor[row_at, middle] * factor_inverse[middle, col_at]
            factor_inverse[row_at, col_at] = -running / factor[row_at, row_at]
    result_rows = []
    for row_at in range(9):
        entries = []
        for col_at in range(9):
            running = factor_inverse[max(row_at, col_at), row_at] * factor_inverse[max(row_at, col_at), col_at]
            for middle in range(max(row_at, col_at) + 1, 9):
                running = running + factor_inverse[middle, row_at] * factor_inverse[middle, col_at]
            entries.append(running)
        result_rows.append(jnp.stack(entries))
    return jnp.stack(result_rows)

def assemble(packed):
    positions = {}
    for index_at, pair in enumerate(block_pairs):
        positions[pair[0], pair[1]] = index_at
        positions[pair[1], pair[0]] = index_at
    return jnp.stack([jnp.stack([packed[positions[row_at, col_at]] + (damping if row_at == col_at else 0.0) for col_at in range(9)]) for row_at in range(9)])

def apply_blocks(inverse_blocks, vector):
    return lax.optimization_barrier(jnp.sum(inverse_blocks * vector[None], axis=1))

def slot_basics(camera_jacobian, point_jacobian, residuals, track_length):
    tracks = camera_jacobian.shape[1]
    in_track = (jnp.arange(tracks, dtype=jnp.int32)[:, None] < track_length[None, :]).astype(jnp.float32)
    camera_blocks = camera_jacobian.reshape(2, 9, tracks, -1) * in_track
    point_blocks = point_jacobian.reshape(2, 3, tracks, -1) * in_track
    errors = residuals.reshape(2, tracks, -1) * in_track
    coupling = lax.optimization_barrier(jnp.sum(camera_blocks[:, :, None] * point_blocks[:, None], axis=0))
    point_system = lax.optimization_barrier(jnp.sum(point_blocks[:, :, None] * point_blocks[:, None], axis=(0, 3)))
    point_system = point_system + damping * jnp.eye(3, dtype=jnp.float32)[:, :, None]
    point_inverse = inverse_small(point_system)
    point_gradient = -lax.optimization_barrier(jnp.sum(point_blocks * errors[:, None], axis=(0, 2)))
    return (camera_blocks, errors, coupling, point_inverse, point_gradient)

def camera_terms(camera_blocks, errors, coupling, point_inverse, point_gradient):
    solved = lax.optimization_barrier(jnp.sum(point_inverse * point_gradient[None], axis=1))
    scaled = coupling[:, 0][:, None] * point_inverse[0][None, :, None, :]
    for middle in range(1, 3):
        scaled = scaled + coupling[:, middle][:, None] * point_inverse[middle][None, :, None, :]
    packed = []
    for leading, trailing in block_pairs:
        packed.append(lax.optimization_barrier(jnp.sum(camera_blocks[:, leading] * camera_blocks[:, trailing], axis=0)) - lax.optimization_barrier(jnp.sum(scaled[leading] * coupling[trailing], axis=0)))
    right_side = -lax.optimization_barrier(jnp.sum(camera_blocks * errors[:, None], axis=0)) - lax.optimization_barrier(jnp.sum(coupling * solved[None, :, None], axis=1))
    return jnp.concatenate([jnp.stack(packed), right_side], axis=0)

def slot_product(camera_blocks, coupling, point_inverse, gathered):
    projected = lax.optimization_barrier(jnp.sum(camera_blocks * gathered[None], axis=1))
    pulled = lax.optimization_barrier(jnp.sum(coupling * gathered[:, None], axis=(0, 2)))
    solved = lax.optimization_barrier(jnp.sum(point_inverse * pulled[None], axis=1))
    return lax.optimization_barrier(jnp.sum(camera_blocks * projected[:, None], axis=0)) - lax.optimization_barrier(jnp.sum(coupling * solved[None, :, None], axis=1))

def point_update(coupling, point_inverse, point_gradient, gathered):
    pulled = lax.optimization_barrier(jnp.sum(coupling * gathered[:, None], axis=(0, 2)))
    return lax.optimization_barrier(jnp.sum(point_inverse * (point_gradient - pulled)[None], axis=1))

def conjugate(right_side, inverse_blocks, product, curvature_sum, energy_sum):
    residual = right_side
    conditioned = apply_blocks(inverse_blocks, residual)
    direction = conditioned
    energy_now = energy_sum(jnp.sum(residual * conditioned))
    camera_step = jnp.zeros_like(right_side)
    taken = []
    for iteration in range(ITERS):
        curved, spread = product(direction)
        step_size = energy_now / curvature_sum(jnp.sum(direction * curved))
        camera_step = camera_step + step_size * direction
        taken.append((step_size, spread))
        if iteration + 1 < ITERS:
            residual = residual - step_size * curved
            conditioned = apply_blocks(inverse_blocks, residual)
            renewed = energy_sum(jnp.sum(residual * conditioned))
            direction = conditioned + renewed / energy_now * direction
            energy_now = renewed
    return (camera_step, taken)

def reference(camera_jacobian, point_jacobian, residuals, observed_camera, track_length):
    starts = jnp.arange(DEVICES, dtype=jnp.int32) * PT_DEV

    def block_of(start):
        return [lax.dynamic_slice_in_dim(array, start, PT_DEV, array.ndim - 1) for array in (camera_jacobian, point_jacobian, residuals, observed_camera, track_length)]

    def build_step(carry, start):
        camera_part, point_part, error_part, index_part, length_part = block_of(start)
        basics = slot_basics(camera_part, point_part, error_part, length_part)
        values = camera_terms(*basics).reshape(54, -1)
        return (carry.at[:, index_part.reshape(-1)].add(values), None)
    totals, unused = lax.scan(build_step, jnp.zeros((54, NCAM), jnp.float32), starts)

    def product(direction):

        def product_step(carry, start):
            camera_part, point_part, error_part, index_part, length_part = block_of(start)
            basics = slot_basics(camera_part, point_part, error_part, length_part)
            gathered = direction[:, index_part.reshape(-1)].reshape(9, TRACK, PT_DEV)
            contrib = slot_product(basics[0], basics[2], basics[3], gathered)
            return (carry.at[:, index_part.reshape(-1)].add(contrib.reshape(9, -1)), None)
        summed, unused_too = lax.scan(product_step, jnp.zeros((9, NCAM), jnp.float32), starts)
        return (damping * direction + summed, direction)

    def unchanged(value):
        return value
    camera_move, taken = conjugate(totals[45:], block_inverse(assemble(totals[:45])), product, unchanged, unchanged)

    def point_block(start):
        camera_part, point_part, error_part, index_part, length_part = block_of(start)
        basics = slot_basics(camera_part, point_part, error_part, length_part)
        gathered = camera_move[:, index_part.reshape(-1)].reshape(9, TRACK, PT_DEV)
        return point_update(basics[2], basics[3], basics[4], gathered)
    point_moves = lax.map(point_block, starts)
    return (camera_move, jnp.transpose(point_moves, (1, 0, 2)).reshape(3, NPT))
```

```python
import jax
import jax.numpy as jnp
from jax import lax
from jax.experimental import pallas as pl
from jax.experimental.pallas import tpu as pltpu
from jax.sharding import PartitionSpec as P

CAM_DEV = 384
TRACK = 8
PT_DEV = 1024
OWNERS = 128
LANES = 128
WIDTH = 21
GROUPS = 6
ROWS = 13
CAP = GROUPS * ROWS
SPAN = 80
FEW = 64
CAMERA_AT = 20
ENTRIES = 56
COUNT_AT = GROUPS * WIDTH
BLOCKS = TRACK * PT_DEV // LANES

F32 = jnp.float32
BF16 = jnp.bfloat16
PARAMS = pltpu.CompilerParams(vmem_limit_bytes=48 * 2**20)
block_pairs = [(leading, trailing) for leading in range(9) for trailing in range(leading, 9)]


def iota(shape, axis):
    return lax.broadcasted_iota(jnp.int32, shape, axis)


def two_parts(value):
    high = value.astype(BF16)
    low = (value - high.astype(F32)).astype(BF16)
    return high, low


def dot(left, right):
    return jnp.dot(left, right, preferred_element_type=F32)


def dot_lanes(left, right):
    return lax.dot_general(left, right, (((1,), (1,)), ((), ())), preferred_element_type=F32)


def total(value):
    return jnp.sum(jnp.sum(value, axis=0, keepdims=True), axis=1, keepdims=True)


def over_tracks(value):
    return jnp.sum(value, axis=0, keepdims=True)


def used_slots(length_ref, lanes):
    return iota((TRACK, LANES), 0) < length_ref[:, lanes]


def masked_points(point_ref, used, lanes):
    return [
        [jnp.where(used, point_ref[3 * i + a, :, lanes], 0.0) for a in range(3)] for i in range(2)
    ]


def times_inverse(inverse, vector):
    v00, v01, v02, v11, v12, v22 = inverse
    x, y, z = vector
    return [v00 * x + v01 * y + v02 * z, v01 * x + v11 * y + v12 * z, v02 * x + v12 * y + v22 * z]


def prepare_kernel(camera_ref, point_ref, error_ref, index_ref, length_ref, pay_ref, code_ref, route_ref, state_ref, root_ref, flag_ref):
    for chunk in range(PT_DEV // LANES):
        lanes = slice(chunk * LANES, (chunk + 1) * LANES)
        used = used_slots(length_ref, lanes)
        point = masked_points(point_ref, used, lanes)
        error = [jnp.where(used, error_ref[i, :, lanes], 0.0) for i in range(2)]

        def pair(a, b):
            return over_tracks(point[0][a] * point[0][b] + point[1][a] * point[1][b])

        s00, s01, s02 = 1.0 + pair(0, 0), pair(0, 1), pair(0, 2)
        s11, s12, s22 = 1.0 + pair(1, 1), pair(1, 2), 1.0 + pair(2, 2)
        c00 = s11 * s22 - s12 * s12
        c01 = s12 * s02 - s01 * s22
        c02 = s01 * s12 - s11 * s02
        c11 = s22 * s00 - s02 * s02
        c12 = s02 * s01 - s12 * s00
        c22 = s00 * s11 - s01 * s01
        determinant = s00 * c00 + s01 * c01 + s02 * c02
        inverse = [c / determinant for c in (c00, c01, c02, c11, c12, c22)]
        gradient = [
            -over_tracks(point[0][a] * error[0] + point[1][a] * error[1]) for a in range(3)
        ]
        for at, value in enumerate(inverse + gradient):
            state_ref[at : at + 1, lanes] = value
        solved = times_inverse(inverse, gradient)
        u0 = times_inverse(inverse, point[0])
        u1 = times_inverse(inverse, point[1])

        def along(left, right):
            return left[0] * right[0] + left[1] * right[1] + left[2] * right[2]

        camera = index_ref[:, lanes]
        owner = ((camera >> 7) * 171) >> 9
        local = camera - owner * CAM_DEV
        b01 = -along(u0, point[1])
        root0 = jnp.sqrt(1.0 - along(u0, point[0]))
        root1 = b01 / root0
        root2 = jnp.sqrt(1.0 - along(u1, point[1]) - root1 * root1)
        inverse0, inverse2 = 1.0 / root0, 1.0 / root2
        side0 = (error[0] + along(solved, point[0])) * inverse0
        side1 = (error[1] + along(solved, point[1]) - root1 * side0) * inverse2
        values = [root0 * camera_ref[j, :, lanes] + root1 * camera_ref[9 + j, :, lanes] for j in range(9)]
        values += [root2 * camera_ref[9 + j, :, lanes] for j in range(9)]
        values += [side0, side1, (local + 1).astype(F32)]
        for at, value in enumerate((inverse0, root1, inverse2)):
            root_ref[at * TRACK : (at + 1) * TRACK, lanes] = value
        for f in range(WIDTH):
            at = (chunk * WIDTH + f) * TRACK
            pay_ref[at : at + TRACK, :] = values[f]
        route_ref[0:TRACK, lanes] = jnp.where(used, owner, OWNERS)

    step = 256
    earlier = jnp.where(iota((step, step), 0) < iota((step, step), 1), 1.0, 0.0).astype(BF16)
    everything = jnp.ones((step, step), BF16)
    before = jnp.zeros((OWNERS, step), F32)
    names = iota((OWNERS, step), 0)
    for s in range(TRACK):
        for chunk in range(PT_DEV // step):
            lanes = slice(chunk * step, (chunk + 1) * step)
            chosen = names == route_ref[s : s + 1, lanes]
            hot = jnp.where(chosen, 1.0, 0.0).astype(BF16)
            rank = jnp.sum(
                jnp.where(chosen, dot(hot, earlier) + before, 0.0), axis=0, keepdims=True
            )
            before = before + dot(hot, everything)
            route_ref[TRACK + s : TRACK + s + 1, lanes] = rank.astype(jnp.int32)

    owner = route_ref[0:TRACK, :]
    rank = route_ref[TRACK : 2 * TRACK, :]
    fits = (owner < OWNERS) & (rank < CAP)
    row_at = (rank * 171) >> 10
    place = (rank - row_at * GROUPS) * (OWNERS * ROWS) + owner * ROWS + row_at
    code = jnp.where(fits, place, GROUPS * OWNERS * ROWS)
    for chunk in range(PT_DEV // LANES):
        code_ref[chunk * TRACK : (chunk + 1) * TRACK, :] = code[:, chunk * LANES : (chunk + 1) * LANES]
    most = jnp.max(jnp.max(before, axis=0, keepdims=True), axis=1, keepdims=True)
    lane = iota((OWNERS, LANES), 1)
    flag_ref[...] = jnp.where(lane > COUNT_AT, most, before[:, 0:LANES])


def dispatch_kernel(code_ref, pay_ref, flag_ref, out_ref, slot_ref, block_ref):
    rows = OWNERS * ROWS
    zeros = jnp.zeros((8, LANES), F32)
    slots_ref = slot_ref.reshape(BLOCKS * LANES, LANES)
    blocks_ref = block_ref.reshape(GROUPS * rows + 8, LANES)

    def clear(at, carry):
        for j in range(16):
            blocks_ref[pl.ds(pl.multiple_of(at * 128 + j * 8, 8), 8), :] = zeros
        return carry

    lax.fori_loop(0, GROUPS * rows // 128, clear, 0)
    within = iota((LANES, LANES), 1) % WIDTH
    for first in range(0, BLOCKS, GROUPS):
        blocks = []
        for block in range(first, first + GROUPS):
            chunk, s = divmod(block, TRACK)
            if block < BLOCKS:
                blocks.append(pay_ref[pl.ds(chunk * WIDTH * TRACK + s, WIDTH, stride=TRACK), :])
            else:
                blocks.append(jnp.zeros((WIDTH, LANES), F32))
        turned = jnp.transpose(jnp.concatenate(blocks + [zeros[0 : LANES - COUNT_AT]], axis=0))
        for block in range(first, min(first + GROUPS, BLOCKS)):
            slots_ref[block * LANES : (block + 1) * LANES, :] = jnp.take_along_axis(
                turned, within + (block - first) * WIDTH, axis=1, mode="promise_in_bounds"
            )

    def place(block, carry):
        for start in range(0, LANES, 32):
            columns = range(start, start + 32)
            codes = [code_ref[block, j] for j in columns]
            slots = [slot_ref[block, j] for j in columns]
            for code, slot in zip(codes, slots):
                block_ref[code] = slot
        return carry

    lax.fori_loop(0, BLOCKS, place, 0)
    group = iota((8, LANES), 1) // WIDTH

    def merge(at, carry):
        for j in range(8):
            start = pl.multiple_of(at * 64 + j * 8, 8)
            value = zeros
            for k in range(GROUPS):
                value = jnp.where(group == k, blocks_ref[pl.ds(k * rows + start, 8), :], value)
            out_ref[pl.ds(start, 8), :] = value
        return carry

    lax.fori_loop(0, rows // 64, merge, 0)
    lane = iota((OWNERS, LANES), 1)
    leading = pl.ds(0, OWNERS, stride=ROWS)
    out_ref[leading, :] = jnp.where(lane >= COUNT_AT, flag_ref[...], out_ref[leading, :])


def solve(factor, roots, vector):
    forward = []
    for i in range(9):
        value = vector[i]
        for j in range(i):
            value = value - factor[i, j] * forward[j]
        forward.append(value / roots[i])
    result = [None] * 9
    for i in reversed(range(9)):
        value = forward[i]
        for j in range(i + 1, 9):
            value = value - factor[j, i] * result[j]
        result[i] = value / roots[i]
    return result


def hot_cameras(feature_ref, hot_ref, block):
    names = iota((LANES, LANES), 0)
    for r in range(8):
        camera = feature_ref[pl.ds(CAMERA_AT * SPAN + block * 8 + r, 1), :].astype(jnp.int32) - 1
        hot = jnp.where(names == (camera & (LANES - 1)), 1.0, 0.0).astype(BF16)
        hot_ref[:, pl.ds(pl.multiple_of(block * PT_DEV + r * LANES, LANES), LANES)] = hot


def features_of(feature_ref, f, block):
    return feature_ref[pl.ds(pl.multiple_of(f * SPAN + block * 8, 8), 8), :]


def image_slots(vector, feature_ref, table_ref, image_ref, blocks):
    for j in range(9):
        for c in range(3):
            at = (3 * j + c) * 8
            table_ref[at : at + 8, :] = jnp.broadcast_to(vector[j][c : c + 1, :], (8, LANES))

    def one(block, carry):
        camera = features_of(feature_ref, CAMERA_AT, block).astype(jnp.int32) - 1
        third = camera >> 7
        lane = camera & (LANES - 1)
        images = [jnp.zeros((8, LANES), F32)] * 2
        for j in range(9):
            found = [
                jnp.take_along_axis(
                    table_ref[(3 * j + c) * 8 : (3 * j + c + 1) * 8, :],
                    lane,
                    axis=1,
                    mode="promise_in_bounds",
                )
                for c in range(3)
            ]
            value = jnp.where(third == 1, found[1], jnp.where(third == 2, found[2], found[0]))
            for i in range(2):
                images[i] = images[i] + features_of(feature_ref, 9 * i + j, block) * value
        for i in range(2):
            image_ref[pl.ds(pl.multiple_of(i * LANES + block * 8, 8), 8), :] = images[i]
        return carry

    lax.fori_loop(0, blocks, one, 0)


def keep_parts(part_ref, feature_ref, parts_ref, block, count):
    for r in range(8):
        lanes = pl.ds(pl.multiple_of(block * PT_DEV + r * LANES, LANES), LANES)
        camera = feature_ref[pl.ds(CAMERA_AT * SPAN + block * 8 + r, 1), :].astype(jnp.int32) - 1
        value = part_ref[pl.ds(r, count, stride=8), :]
        high = value.astype(BF16).astype(F32)
        both = jnp.concatenate([high, value - high], axis=0).astype(BF16)
        third = jnp.broadcast_to(camera >> 7, (16, LANES))
        for c in range(3):
            inside = jnp.where(third == c, 1.0, 0.0).astype(BF16)
            inside = jnp.concatenate([inside] * (count // 8), axis=0)
            parts_ref[2 * c * count : 2 * (c + 1) * count, lanes] = both * inside


def camera_sums(parts_ref, hot_ref, part_ref, sum_ref, count, many):
    few = FEW * LANES
    sum_ref[...] = dot_lanes(parts_ref[:, 0:few], hot_ref[:, 0:few])

    @pl.when(many)
    def _():
        sum_ref[...] += dot_lanes(parts_ref[:, few:], hot_ref[:, few:])

    part_ref[...] = jnp.zeros(part_ref.shape, F32)
    for c in range(3):
        at = 2 * c * count
        part_ref[pl.ds(c, count, stride=8), :] = (
            sum_ref[at : at + count, :] + sum_ref[at + count : at + 2 * count, :]
        )


def turn_in(got_ref, i):
    return jnp.transpose(got_ref[pl.ds(i, OWNERS, stride=2), :])


def turn_out(image_ref, out_ref):
    for i in range(2):
        out_ref[pl.ds(i, OWNERS, stride=2), :] = jnp.transpose(
            image_ref[i * LANES : (i + 1) * LANES, :]
        )


def first_camera_kernel(got_ref, feature_ref, factor_ref, first_ref, out_ref, flag_ref, hot_ref, parts_ref, table_ref, image_ref, sum_ref, part_ref):
    image_ref[...] = jnp.zeros((2 * LANES, LANES), F32)
    feature_ref[...] = jnp.zeros(feature_ref.shape, F32)

    def take_row(q):
        turned = jnp.transpose(got_ref[pl.ds(q, OWNERS, stride=ROWS), :])
        for k in range(GROUPS):
            feature_ref[pl.ds(q * GROUPS + k, WIDTH, stride=SPAN), :] = turned[
                k * WIDTH : (k + 1) * WIDTH, :
            ]
        return turned

    turned = take_row(0)
    flag_ref[...] = jnp.broadcast_to(
        jnp.max(turned[COUNT_AT + 1 : COUNT_AT + 2, :], axis=1, keepdims=True), (8, LANES)
    )
    most = jnp.max(turned[COUNT_AT : COUNT_AT + 1, :])
    many = most > FEW
    blocks = jnp.where(many, SPAN // 8, FEW // 8)
    few_rows = -(-FEW // GROUPS)
    for q in range(1, few_rows):
        take_row(q)

    @pl.when(many)
    def _():
        for q in range(few_rows, ROWS):
            take_row(q)

    part_ref[...] = jnp.zeros((ENTRIES * 8, LANES), F32)

    def gather_terms(block, carry):
        hot_cameras(feature_ref, hot_ref, block)
        f = [features_of(feature_ref, at, block) for at in range(20)]
        for at, (j, k) in enumerate(block_pairs):
            part_ref[at * 8 : (at + 1) * 8, :] = f[j] * f[k] + f[9 + j] * f[9 + k]
        for j in range(9):
            part_ref[(45 + j) * 8 : (46 + j) * 8, :] = -(f[j] * f[18] + f[9 + j] * f[19])
        keep_parts(part_ref, feature_ref, parts_ref, block, ENTRIES)
        return carry

    lax.fori_loop(0, blocks, gather_terms, 0)
    camera_sums(parts_ref, hot_ref, part_ref, sum_ref, ENTRIES, many)
    matrix = {}
    for at, (j, k) in enumerate(block_pairs):
        entry = part_ref[at * 8 : (at + 1) * 8, :]
        matrix[k, j] = entry + 1.0 if j == k else entry
    side = [part_ref[(45 + j) * 8 : (46 + j) * 8, :] for j in range(9)]
    factor, roots = {}, []
    for j in range(9):
        pivot = matrix[j, j]
        for m in range(j):
            pivot = pivot - factor[j, m] * factor[j, m]
        roots.append(jnp.sqrt(pivot))
        for i in range(j + 1, 9):
            running = matrix[i, j]
            for m in range(j):
                running = running - factor[i, m] * factor[j, m]
            factor[i, j] = running / roots[j]
    for at, (j, k) in enumerate(block_pairs):
        factor_ref[at * 8 : (at + 1) * 8, :] = roots[j] if j == k else factor[k, j]
    first = solve(factor, roots, side)
    energy = side[0] * first[0]
    for j in range(1, 9):
        energy = energy + side[j] * first[j]
    for j in range(9):
        first_ref[j * 8 : (j + 1) * 8, :] = first[j]
    first_ref[72:80, :] = energy
    first_ref[80:88, :] = jnp.broadcast_to(jnp.max(turned[COUNT_AT : COUNT_AT + 1, :], axis=1, keepdims=True), (8, LANES))
    image_slots(first, feature_ref, table_ref, image_ref, blocks)
    turn_out(image_ref, out_ref)


def pull_slots(got_ref, route_ref, point_ref, length_ref, state_ref, root_ref, value_ref, pulled_ref, curve_ref, back):
    images = []
    for i in range(2):
        images.append(turn_in(got_ref, i)[0:SPAN, :])
    high, low = two_parts(jnp.concatenate(images, axis=0))
    parts = jnp.concatenate([high, low], axis=1)
    owners = iota((OWNERS, PT_DEV), 0)
    ranks = iota((SPAN, PT_DEV), 0)
    for s in range(TRACK):
        hot = jnp.where(owners == route_ref[s : s + 1, :], 1.0, 0.0).astype(BF16)
        got = dot(parts, jnp.concatenate([hot, hot], axis=0))
        here = ranks == route_ref[TRACK + s : TRACK + s + 1, :]
        for i in range(2):
            value_ref[i * TRACK + s : i * TRACK + s + 1, :] = jnp.sum(
                jnp.where(here, got[i * SPAN : (i + 1) * SPAN, :], 0.0), axis=0, keepdims=True
            )
    curve = jnp.zeros((TRACK, LANES), F32)
    for chunk in range(PT_DEV // LANES):
        lanes = slice(chunk * LANES, (chunk + 1) * LANES)
        used = used_slots(length_ref, lanes)
        point = masked_points(point_ref, used, lanes)
        root = [root_ref[at * TRACK : (at + 1) * TRACK, lanes] for at in range(3)]
        image1 = value_ref[TRACK : 2 * TRACK, lanes] * root[2]
        image = [(value_ref[0:TRACK, lanes] - root[1] * image1) * root[0], image1]
        pulled = [over_tracks(point[0][a] * image[0] + point[1][a] * image[1]) for a in range(3)]
        inverse = [state_ref[at : at + 1, lanes] for at in range(6)]
        solved = times_inverse(inverse, pulled)
        for a in range(3):
            pulled_ref[a : a + 1, lanes] = pulled[a]
        result = [
            image[i] - (point[i][0] * solved[0] + point[i][1] * solved[1] + point[i][2] * solved[2])
            for i in range(2)
        ]
        if back:
            result0 = result[0] * root[0]
            value_ref[0:TRACK, lanes] = result0
            value_ref[TRACK : 2 * TRACK, lanes] = (result[1] - root[1] * result0) * root[2]
        else:
            curve = curve + image[0] * result[0] + image[1] * result[1]
    if not back:
        curve_ref[...] = curve


def first_point_kernel(got_ref, route_ref, point_ref, length_ref, state_ref, root_ref, pulled_ref, out_ref, value_ref, image_ref):
    pull_slots(got_ref, route_ref, point_ref, length_ref, state_ref, root_ref, value_ref, pulled_ref, None, True)
    owners = iota((OWNERS, PT_DEV), 0)
    ranks = iota((SPAN, PT_DEV), 0)
    sums = jnp.zeros((4 * SPAN, OWNERS), F32)
    for s in range(TRACK):
        hot = jnp.where(owners == route_ref[s : s + 1, :], 1.0, 0.0).astype(BF16)
        here = ranks == route_ref[TRACK + s : TRACK + s + 1, :]
        spread = []
        for i in range(2):
            value = value_ref[i * TRACK + s : i * TRACK + s + 1, :]
            spread.append(jnp.where(here, value, 0.0))
        high, low = two_parts(jnp.concatenate(spread, axis=0))
        sums = sums + dot_lanes(jnp.concatenate([high, low], axis=0), hot)
    sums = sums[0 : 2 * SPAN] + sums[2 * SPAN :]
    image_ref[...] = jnp.zeros((2 * LANES, LANES), F32)
    for i in range(2):
        image_ref[i * LANES : i * LANES + SPAN, :] = sums[i * SPAN : (i + 1) * SPAN, :]
    turn_out(image_ref, out_ref)


def second_point_kernel(got_ref, route_ref, point_ref, length_ref, state_ref, root_ref, pulled_ref, out_ref, scalar_ref, value_ref, curve_ref):
    pull_slots(got_ref, route_ref, point_ref, length_ref, state_ref, root_ref, value_ref, pulled_ref, curve_ref, False)
    out_ref[...] = jnp.broadcast_to(total(curve_ref[...]), (OWNERS, LANES))
    scalar_ref[...] = jnp.broadcast_to(
        jnp.sum(got_ref[pl.ds(0, OWNERS, stride=2), :], axis=0, keepdims=True), (8, LANES)
    )


def second_camera_kernel(got_ref, feature_ref, factor_ref, first_ref, second_ref, out_ref, hot_ref, parts_ref, table_ref, image_ref, sum_ref, wide_ref):
    for i in range(2):
        image_ref[i * LANES : (i + 1) * LANES, :] = turn_in(got_ref, i)
    many = jnp.max(first_ref[80:88, :]) > FEW
    blocks = jnp.where(many, SPAN // 8, FEW // 8)
    wide_ref[...] = jnp.zeros((LANES, LANES), F32)

    def gather_terms(block, carry):
        hot_cameras(feature_ref, hot_ref, block)
        back = [
            image_ref[pl.ds(pl.multiple_of(i * LANES + block * 8, 8), 8), :] for i in range(2)
        ]
        for j in range(9):
            wide_ref[j * 8 : (j + 1) * 8, :] = (
                features_of(feature_ref, j, block) * back[0]
                + features_of(feature_ref, 9 + j, block) * back[1]
            )
        keep_parts(wide_ref, feature_ref, parts_ref, block, 16)
        return carry

    lax.fori_loop(0, blocks, gather_terms, 0)
    camera_sums(parts_ref, hot_ref, wide_ref, sum_ref, 16, many)
    first = [first_ref[j * 8 : (j + 1) * 8, :] for j in range(9)]
    image = [first[j] + wide_ref[j * 8 : (j + 1) * 8, :] for j in range(9)]
    factor, roots = {}, []
    for at, (j, k) in enumerate(block_pairs):
        entry = factor_ref[at * 8 : (at + 1) * 8, :]
        if j == k:
            roots.append(entry)
        else:
            factor[k, j] = entry
    second = solve(factor, roots, image)
    for j in range(9):
        second_ref[j * 8 : (j + 1) * 8, :] = second[j]

    def inner(left, right):
        value = left[0] * right[0]
        for j in range(1, 9):
            value = value + left[j] * right[j]
        return value

    image_slots(second, feature_ref, table_ref, image_ref, blocks)
    scalars = [first_ref[72:80, :], inner(first, image), inner(image, second), inner(second, second)]
    for at, value in enumerate(scalars):
        image_ref[SPAN + at : SPAN + at + 1, :] = jnp.broadcast_to(total(value), (1, LANES))
    turn_out(image_ref, out_ref)


def finish_kernel(curve_ref, scalar_ref, first_ref, second_ref, state_ref, first_pulled_ref, second_pulled_ref, camera_out, point_out, camera_ref, point_ref, camera_sem, point_sem):
    own = jnp.sum(curve_ref[...], axis=0, keepdims=True)[:, 0:1]
    energy, curvature, crossed, square = [
        scalar_ref[0:1, SPAN + at : SPAN + at + 1] for at in range(4)
    ]
    step_size = energy / curvature
    renewed = step_size * step_size * crossed - energy
    ratio = 1.0 + renewed / energy
    second_step = renewed / (
        ratio * ratio * curvature
        - 2.0 * step_size * ratio * crossed
        + step_size * step_size * (square + own)
    )
    first_weight = step_size + second_step * ratio
    second_weight = -second_step * step_size
    for c in range(3):
        camera_ref[:, c * LANES : (c + 1) * LANES] = (
            first_weight * first_ref[pl.ds(c, 9, stride=8), :]
            + second_weight * second_ref[pl.ds(c, 9, stride=8), :]
        )
    camera_copy = pltpu.make_async_copy(camera_ref, camera_out, camera_sem)
    camera_copy.start()
    left = [
        state_ref[6 + a : 7 + a, :]
        - first_weight * first_pulled_ref[a : a + 1, :]
        - second_weight * second_pulled_ref[a : a + 1, :]
        for a in range(3)
    ]
    moved = times_inverse([state_ref[at : at + 1, :] for at in range(6)], left)
    for a in range(3):
        point_ref[a : a + 1, :] = moved[a]
    point_copy = pltpu.make_async_copy(point_ref, point_out, point_sem)
    point_copy.start()
    camera_copy.wait()
    point_copy.wait()


def call(kernel, outs, scratch, operands, in_scalar=0):
    specs = [
        pl.BlockSpec(memory_space=pltpu.SMEM if at < in_scalar else pltpu.VMEM)
        for at in range(len(operands))
    ]
    return pl.pallas_call(
        kernel,
        out_shape=[jax.ShapeDtypeStruct(shape, dtype) for shape, dtype in outs],
        in_specs=specs,
        out_specs=[pl.BlockSpec(memory_space=pltpu.VMEM)] * len(outs),
        scratch_shapes=[pltpu.VMEM(shape, dtype) for shape, dtype in scratch],
        compiler_params=PARAMS,
    )(*operands)


def exchange(rows):
    blocks = rows.reshape(OWNERS, 1, -1)
    blocks = lax.all_to_all(blocks, ("row", "col"), split_axis=0, concat_axis=0, tiled=True)
    return blocks.reshape(rows.shape)


def by_slots(camera_jacobian, point_jacobian, residuals, observed_camera, track_length):
    lengths = track_length.reshape(1, PT_DEV)
    pay, code, route, state, root, flag = call(
        prepare_kernel,
        [
            ((WIDTH * PT_DEV * TRACK // LANES, LANES), F32),
            ((BLOCKS, LANES), jnp.int32),
            ((2 * TRACK, PT_DEV), jnp.int32),
            ((16, PT_DEV), F32),
            ((3 * TRACK, PT_DEV), F32),
            ((OWNERS, LANES), F32),
        ],
        [],
        (camera_jacobian, point_jacobian, residuals, observed_camera, lengths),
    )
    (sent,) = call(
        dispatch_kernel,
        [((OWNERS * ROWS, LANES), F32)],
        [((BLOCKS, LANES, 1, LANES), F32), ((GROUPS * OWNERS * ROWS + 8, 1, LANES), F32)],
        (code, pay, flag),
        in_scalar=1,
    )
    hot = ((LANES, SPAN * LANES), BF16)
    table = ((27 * 8, LANES), F32)
    image = ((2 * LANES, LANES), F32)
    pair = ((2 * OWNERS, LANES), F32)
    features, factor, first, out, overflow = call(
        first_camera_kernel,
        [((WIDTH * SPAN, LANES), F32), ((45 * 8, LANES), F32), ((88, LANES), F32), pair, ((8, LANES), F32)],
        [hot, ((6 * ENTRIES, SPAN * LANES), BF16), table, image, ((6 * ENTRIES, LANES), F32), ((ENTRIES * 8, LANES), F32)],
        (exchange(sent),),
    )
    first_pulled, out = call(
        first_point_kernel,
        [((8, PT_DEV), F32), pair],
        [((2 * TRACK, PT_DEV), F32), image],
        (exchange(out), route, point_jacobian, lengths, state, root),
    )
    second, out = call(
        second_camera_kernel,
        [((72, LANES), F32), pair],
        [hot, ((96, SPAN * LANES), BF16), table, image, ((96, LANES), F32), ((LANES, LANES), F32)],
        (exchange(out), features, factor, first),
    )
    second_pulled, curve, scalars = call(
        second_point_kernel,
        [((8, PT_DEV), F32), ((OWNERS, LANES), F32), ((8, LANES), F32)],
        [((2 * TRACK, PT_DEV), F32), ((TRACK, LANES), F32)],
        (exchange(out), route, point_jacobian, lengths, state, root),
    )
    return overflow[0, 0], (exchange(curve), scalars, first, second, state, first_pulled, second_pulled)


def finish(*operands):
    shapes = [(9, CAM_DEV), (3, PT_DEV)]
    return tuple(
        pl.pallas_call(
            finish_kernel,
            out_shape=[jax.ShapeDtypeStruct(shape, F32) for shape in shapes],
            in_specs=[pl.BlockSpec(memory_space=pltpu.VMEM)] * len(operands),
            out_specs=[pl.BlockSpec(memory_space=pltpu.HBM)] * 2,
            scratch_shapes=[pltpu.VMEM(shape, F32) for shape in shapes]
            + [pltpu.SemaphoreType.DMA] * 2,
            compiler_params=PARAMS,
        )(*operands)
    )


damping = 1.0


def inverse_small(matrix):
    entries = [[matrix[row_at, col_at] for col_at in range(3)] for row_at in range(3)]
    cofactor = [
        [
            entries[(row_at + 1) % 3][(col_at + 1) % 3]
            * entries[(row_at + 2) % 3][(col_at + 2) % 3]
            - entries[(row_at + 1) % 3][(col_at + 2) % 3]
            * entries[(row_at + 2) % 3][(col_at + 1) % 3]
            for col_at in range(3)
        ]
        for row_at in range(3)
    ]
    determinant = (
        entries[0][0] * cofactor[0][0]
        + entries[0][1] * cofactor[0][1]
        + entries[0][2] * cofactor[0][2]
    )
    return jnp.stack(
        [
            jnp.stack([cofactor[col_at][row_at] / determinant for col_at in range(3)])
            for row_at in range(3)
        ]
    )


def block_inverse(matrix):
    factor = {}
    for col_at in range(9):
        pivot_value = matrix[col_at, col_at]
        for middle in range(col_at):
            pivot_value = pivot_value - factor[col_at, middle] * factor[col_at, middle]
        diagonal_root = jnp.sqrt(pivot_value)
        factor[col_at, col_at] = diagonal_root
        for row_at in range(col_at + 1, 9):
            running = matrix[row_at, col_at]
            for middle in range(col_at):
                running = running - factor[row_at, middle] * factor[col_at, middle]
            factor[row_at, col_at] = running / diagonal_root
    factor_inverse = {}
    for row_at in range(9):
        factor_inverse[row_at, row_at] = 1.0 / factor[row_at, row_at]
        for col_at in range(row_at):
            running = factor[row_at, col_at] * factor_inverse[col_at, col_at]
            for middle in range(col_at + 1, row_at):
                running = running + factor[row_at, middle] * factor_inverse[middle, col_at]
            factor_inverse[row_at, col_at] = -running / factor[row_at, row_at]
    result_rows = []
    for row_at in range(9):
        entries = []
        for col_at in range(9):
            running = (
                factor_inverse[max(row_at, col_at), row_at]
                * factor_inverse[max(row_at, col_at), col_at]
            )
            for middle in range(max(row_at, col_at) + 1, 9):
                running = running + factor_inverse[middle, row_at] * factor_inverse[middle, col_at]
            entries.append(running)
        result_rows.append(jnp.stack(entries))
    return jnp.stack(result_rows)


def assemble(packed):
    positions = {}
    for index_at, pair in enumerate(block_pairs):
        positions[pair[0], pair[1]] = index_at
        positions[pair[1], pair[0]] = index_at
    return jnp.stack(
        [
            jnp.stack(
                [
                    packed[positions[row_at, col_at]] + (damping if row_at == col_at else 0.0)
                    for col_at in range(9)
                ]
            )
            for row_at in range(9)
        ]
    )


def apply_blocks(inverse_blocks, vector):
    return jnp.sum(inverse_blocks * vector[None], axis=1)


def slot_basics(camera_jacobian, point_jacobian, residuals, track_length):
    tracks = camera_jacobian.shape[1]
    in_track = (jnp.arange(tracks, dtype=jnp.int32)[:, None] < track_length[None, :]).astype(
        jnp.float32
    )
    camera_blocks = camera_jacobian.reshape(2, 9, tracks, -1) * in_track
    point_blocks = point_jacobian.reshape(2, 3, tracks, -1) * in_track
    errors = residuals * in_track
    coupling = jnp.sum(camera_blocks[:, :, None] * point_blocks[:, None], axis=0)
    point_system = jnp.sum(point_blocks[:, :, None] * point_blocks[:, None], axis=(0, 3))
    point_system = point_system + damping * jnp.eye(3, dtype=jnp.float32)[:, :, None]
    point_inverse = inverse_small(point_system)
    point_gradient = -jnp.sum(point_blocks * errors[:, None], axis=(0, 2))
    return (camera_blocks, errors, coupling, point_inverse, point_gradient)


def camera_terms(camera_blocks, errors, coupling, point_inverse, point_gradient):
    solved = jnp.sum(point_inverse * point_gradient[None], axis=1)
    scaled = coupling[:, 0][:, None] * point_inverse[0][None, :, None, :]
    for middle in range(1, 3):
        scaled = scaled + coupling[:, middle][:, None] * point_inverse[middle][None, :, None, :]
    packed = []
    for leading, trailing in block_pairs:
        packed.append(
            jnp.sum(camera_blocks[:, leading] * camera_blocks[:, trailing], axis=0)
            - jnp.sum(scaled[leading] * coupling[trailing], axis=0)
        )
    right_side = -jnp.sum(camera_blocks * errors[:, None], axis=0) - jnp.sum(
        coupling * solved[None, :, None], axis=1
    )
    return jnp.concatenate([jnp.stack(packed), right_side], axis=0)


def slot_product(camera_blocks, coupling, point_inverse, gathered):
    projected = jnp.sum(camera_blocks * gathered[None], axis=1)
    pulled = jnp.sum(coupling * gathered[:, None], axis=(0, 2))
    solved = jnp.sum(point_inverse * pulled[None], axis=1)
    return jnp.sum(camera_blocks * projected[:, None], axis=0) - jnp.sum(
        coupling * solved[None, :, None], axis=1
    )


def by_dense(camera_jacobian, point_jacobian, residuals, observed_camera, track_length):
    camera_blocks, errors, coupling, point_inverse, point_gradient = slot_basics(
        camera_jacobian, point_jacobian, residuals, track_length
    )
    tracks, points = observed_camera.shape
    rows, cols = lax.axis_size("row"), lax.axis_size("col")
    cameras = CAM_DEV * rows * cols
    flat_cameras = observed_camera.reshape(-1)

    def into_cameras(values):
        width = values.shape[0]
        by_camera = (
            jnp.zeros((cameras, width), jnp.float32).at[flat_cameras].add(jnp.transpose(values))
        )
        return jnp.transpose(by_camera)

    def pick_slots(whole):
        slot_rows = jnp.transpose(whole)[flat_cameras]
        return jnp.transpose(slot_rows).reshape(9, tracks, points)

    def spread_out(value):
        copies = jnp.broadcast_to(value[:, None], (9, OWNERS, CAM_DEV)).reshape(9, cameras)
        return lax.all_to_all(copies, ("row", "col"), split_axis=1, concat_axis=1, tiled=True)

    term_values = camera_terms(
        camera_blocks, errors, coupling, point_inverse, point_gradient
    ).reshape(54, -1)
    local_terms = into_cameras(term_values).reshape(54, rows * cols, CAM_DEV)
    own_terms = jnp.sum(
        lax.all_to_all(local_terms, ("row", "col"), split_axis=1, concat_axis=1, tiled=True), axis=1
    )
    inverse_blocks = block_inverse(assemble(own_terms[:45]))
    right_side = own_terms[45:]

    first = apply_blocks(inverse_blocks, right_side)
    first_slots = pick_slots(spread_out(first))
    first_pulled = jnp.sum(coupling * first_slots[:, None], axis=(0, 2))
    contrib = slot_product(camera_blocks, coupling, point_inverse, first_slots)
    local_image = into_cameras(contrib.reshape(9, -1)).reshape(9, OWNERS, CAM_DEV)
    gathered_image = lax.all_to_all(
        local_image, ("row", "col"), split_axis=1, concat_axis=1, tiled=True
    )
    first_image = damping * first + jnp.sum(gathered_image, axis=1)

    second = apply_blocks(inverse_blocks, first_image)
    second_slots = pick_slots(spread_out(second))
    second_pulled = jnp.sum(coupling * second_slots[:, None], axis=(0, 2))
    projected = jnp.sum(camera_blocks * second_slots[None], axis=1)
    solved = jnp.sum(point_inverse * second_pulled[None], axis=1)
    own_sums = jnp.stack(
        [
            jnp.sum(right_side * first),
            jnp.sum(first * first_image),
            jnp.sum(first_image * second),
            jnp.sum(second * second)
            + jnp.sum(projected * projected)
            - jnp.sum(second_pulled * solved),
        ]
    )
    spread = jnp.broadcast_to(own_sums[None], (OWNERS, 4))
    energy, curvature, crossed, second_curvature = jnp.sum(exchange(spread), axis=0)
    step_size = energy / curvature
    renewed = step_size * step_size * crossed - energy
    ratio = 1.0 + renewed / energy
    second_step = renewed / (
        ratio * ratio * curvature
        - 2.0 * step_size * ratio * crossed
        + step_size * step_size * second_curvature
    )
    first_weight = step_size + second_step * ratio
    second_weight = -second_step * step_size
    camera_move = first_weight * first + second_weight * second
    pulled = first_weight * first_pulled + second_weight * second_pulled
    point_move = jnp.sum(point_inverse * (point_gradient - pulled)[None], axis=1)
    return (camera_move, point_move)


def on_device(camera_jacobian, point_jacobian, residuals, observed_camera, track_length):
    operands = (camera_jacobian, point_jacobian, residuals, observed_camera, track_length)
    overflow, kept = by_slots(*operands)
    return lax.cond(
        overflow > CAP,
        lambda given, unused: by_dense(*given),
        lambda unused, found: finish(*found),
        operands,
        kept,
    )


def solution(mesh):
    in_specs = (
        P(None, None, ("row", "col")),
        P(None, None, ("row", "col")),
        P(None, None, ("row", "col")),
        P(None, ("row", "col")),
        P(("row", "col")),
    )
    out_specs = (P(None, ("row", "col")), P(None, ("row", "col")))
    return jax.shard_map(
        on_device, mesh=mesh, in_specs=in_specs, out_specs=out_specs, check_vma=False
    )
```

```python
import jax
import jax.numpy as jnp
from jax import lax
from jax.experimental import pallas as pl
from jax.experimental.pallas import tpu as pltpu
from jax.sharding import PartitionSpec as P

CAM_DEV = 384
TRACK = 8
PT_DEV = 1024
OWNERS = 128
LANES = 128
WIDTH = 21
GROUPS = 6
ROWS = 13
CAP = GROUPS * ROWS
SPAN = 80
FEW = 64
CAMERA_AT = 20
ENTRIES = 56
COUNT_AT = GROUPS * WIDTH
BLOCKS = TRACK * PT_DEV // LANES

F32 = jnp.float32
BF16 = jnp.bfloat16
PARAMS = pltpu.CompilerParams(vmem_limit_bytes=48 * 2**20)
block_pairs = [(leading, trailing) for leading in range(9) for trailing in range(leading, 9)]


def iota(shape, axis):
    return lax.broadcasted_iota(jnp.int32, shape, axis)


def two_parts(value):
    high = value.astype(BF16)
    low = (value - high.astype(F32)).astype(BF16)
    return high, low


def dot(left, right):
    return jnp.dot(left, right, preferred_element_type=F32)


def dot_lanes(left, right):
    return lax.dot_general(left, right, (((1,), (1,)), ((), ())), preferred_element_type=F32)


def total(value):
    return jnp.sum(jnp.sum(value, axis=0, keepdims=True), axis=1, keepdims=True)


def over_tracks(value):
    return jnp.sum(value, axis=0, keepdims=True)


def used_slots(length_ref, lanes):
    return iota((TRACK, LANES), 0) < length_ref[:, lanes]


def masked_points(point_ref, used, lanes):
    return [
        [jnp.where(used, point_ref[3 * i + a, :, lanes], 0.0) for a in range(3)] for i in range(2)
    ]


def times_inverse(inverse, vector):
    v00, v01, v02, v11, v12, v22 = inverse
    x, y, z = vector
    return [v00 * x + v01 * y + v02 * z, v01 * x + v11 * y + v12 * z, v02 * x + v12 * y + v22 * z]


def owner_of(camera):
    return ((camera >> 7) * 171) >> 9


def prepare_kernel(camera_in, point_in, error_in, index_ref, length_ref, pay_ref, code_ref, route_ref, state_ref, root_ref, flag_ref, camera_ref, point_ref, error_ref, camera_sem, point_sem, error_sem):
    copies = [
        pltpu.make_async_copy(camera_in, camera_ref, camera_sem),
        pltpu.make_async_copy(point_in, point_ref, point_sem),
        pltpu.make_async_copy(error_in, error_ref, error_sem),
    ]
    for copy in copies:
        copy.start()
    used = iota((TRACK, PT_DEV), 0) < length_ref[...]
    route_ref[0:TRACK, :] = jnp.where(used, owner_of(index_ref[...]), OWNERS)

    step = 256
    upto = jnp.where(iota((step, step), 0) <= iota((step, step), 1), 1.0, 0.0).astype(BF16)
    before = jnp.zeros((OWNERS, step), F32)
    names = iota((OWNERS, step), 0)
    for s in range(TRACK):
        for chunk in range(PT_DEV // step):
            lanes = slice(chunk * step, (chunk + 1) * step)
            chosen = names == route_ref[s : s + 1, lanes]
            hot = jnp.where(chosen, 1.0, 0.0).astype(BF16)
            counts = dot(hot, upto)
            rank = jnp.sum(jnp.where(chosen, counts + before, 0.0), axis=0, keepdims=True) - 1.0
            before = before + jnp.broadcast_to(counts[:, step - 1 : step], (OWNERS, step))
            route_ref[TRACK + s : TRACK + s + 1, lanes] = rank.astype(jnp.int32)

    owner = route_ref[0:TRACK, :]
    rank = route_ref[TRACK : 2 * TRACK, :]
    fits = (owner < OWNERS) & (rank < CAP)
    row_at = (rank * 171) >> 10
    place = (rank - row_at * GROUPS) * (OWNERS * ROWS) + owner * ROWS + row_at
    code = jnp.where(fits, place, GROUPS * OWNERS * ROWS)
    for chunk in range(PT_DEV // LANES):
        code_ref[chunk * TRACK : (chunk + 1) * TRACK, :] = code[:, chunk * LANES : (chunk + 1) * LANES]
    most = jnp.max(jnp.max(before, axis=0, keepdims=True), axis=1, keepdims=True)
    lane = iota((OWNERS, LANES), 1)
    flag_ref[...] = jnp.where(lane > COUNT_AT, most, before[:, 0:LANES])
    for copy in copies:
        copy.wait()
    for chunk in range(PT_DEV // LANES):
        lanes = slice(chunk * LANES, (chunk + 1) * LANES)
        used = used_slots(length_ref, lanes)
        point = masked_points(point_ref, used, lanes)
        error = [jnp.where(used, error_ref[i, :, lanes], 0.0) for i in range(2)]

        def pair(a, b):
            return over_tracks(point[0][a] * point[0][b] + point[1][a] * point[1][b])

        s00, s01, s02 = 1.0 + pair(0, 0), pair(0, 1), pair(0, 2)
        s11, s12, s22 = 1.0 + pair(1, 1), pair(1, 2), 1.0 + pair(2, 2)
        c00 = s11 * s22 - s12 * s12
        c01 = s12 * s02 - s01 * s22
        c02 = s01 * s12 - s11 * s02
        c11 = s22 * s00 - s02 * s02
        c12 = s02 * s01 - s12 * s00
        c22 = s00 * s11 - s01 * s01
        determinant = s00 * c00 + s01 * c01 + s02 * c02
        inverse = [c / determinant for c in (c00, c01, c02, c11, c12, c22)]
        gradient = [
            -over_tracks(point[0][a] * error[0] + point[1][a] * error[1]) for a in range(3)
        ]
        for at, value in enumerate(inverse + gradient):
            state_ref[at : at + 1, lanes] = value
        solved = times_inverse(inverse, gradient)
        u0 = times_inverse(inverse, point[0])
        u1 = times_inverse(inverse, point[1])

        def along(left, right):
            return left[0] * right[0] + left[1] * right[1] + left[2] * right[2]

        camera = index_ref[:, lanes]
        owner = owner_of(camera)
        local = camera - owner * CAM_DEV
        b01 = -along(u0, point[1])
        root0 = jnp.sqrt(1.0 - along(u0, point[0]))
        root1 = b01 / root0
        root2 = jnp.sqrt(1.0 - along(u1, point[1]) - root1 * root1)
        inverse0, inverse2 = 1.0 / root0, 1.0 / root2
        side0 = (error[0] + along(solved, point[0])) * inverse0
        side1 = (error[1] + along(solved, point[1]) - root1 * side0) * inverse2
        values = [root0 * camera_ref[j, :, lanes] + root1 * camera_ref[9 + j, :, lanes] for j in range(9)]
        values += [root2 * camera_ref[9 + j, :, lanes] for j in range(9)]
        values += [side0, side1, (local + 1).astype(F32)]
        for at, value in enumerate((inverse0, root1, inverse2)):
            root_ref[at * TRACK : (at + 1) * TRACK, lanes] = value
        for f in range(WIDTH):
            at = (chunk * WIDTH + f) * TRACK
            pay_ref[at : at + TRACK, :] = values[f]


def dispatch_kernel(code_ref, pay_ref, flag_ref, out_ref, slot_ref, block_ref):
    rows = OWNERS * ROWS
    zeros = jnp.zeros((8, LANES), F32)
    slots_ref = slot_ref.reshape(BLOCKS * LANES, LANES)
    blocks_ref = block_ref.reshape(GROUPS * rows + 8, LANES)

    def clear(at, carry):
        for j in range(16):
            blocks_ref[pl.ds(pl.multiple_of(at * 128 + j * 8, 8), 8), :] = zeros
        return carry

    lax.fori_loop(0, GROUPS * rows // 128, clear, 0)
    within = iota((LANES, LANES), 1) % WIDTH
    for first in range(0, BLOCKS, GROUPS):
        blocks = []
        for block in range(first, first + GROUPS):
            chunk, s = divmod(block, TRACK)
            if block < BLOCKS:
                blocks.append(pay_ref[pl.ds(chunk * WIDTH * TRACK + s, WIDTH, stride=TRACK), :])
            else:
                blocks.append(jnp.zeros((WIDTH, LANES), F32))
        turned = jnp.transpose(jnp.concatenate(blocks + [zeros[0 : LANES - COUNT_AT]], axis=0))
        for block in range(first, min(first + GROUPS, BLOCKS)):
            slots_ref[block * LANES : (block + 1) * LANES, :] = jnp.take_along_axis(
                turned, within + (block - first) * WIDTH, axis=1, mode="promise_in_bounds"
            )

    def place(block, carry):
        for start in range(0, LANES, 32):
            columns = range(start, start + 32)
            codes = [code_ref[block, j] for j in columns]
            slots = [slot_ref[block, j] for j in columns]
            for code, slot in zip(codes, slots):
                block_ref[code] = slot
        return carry

    lax.fori_loop(0, BLOCKS, place, 0)
    group = iota((8, LANES), 1) // WIDTH

    def merge(at, carry):
        for j in range(8):
            start = pl.multiple_of(at * 64 + j * 8, 8)
            value = zeros
            for k in range(GROUPS):
                value = jnp.where(group == k, blocks_ref[pl.ds(k * rows + start, 8), :], value)
            out_ref[pl.ds(start, 8), :] = value
        return carry

    lax.fori_loop(0, rows // 64, merge, 0)
    lane = iota((OWNERS, LANES), 1)
    leading = pl.ds(0, OWNERS, stride=ROWS)
    out_ref[leading, :] = jnp.where(lane >= COUNT_AT, flag_ref[...], out_ref[leading, :])


def solve(factor, roots, vector):
    forward = []
    for i in range(9):
        value = vector[i]
        for j in range(i):
            value = value - factor[i, j] * forward[j]
        forward.append(value / roots[i])
    result = [None] * 9
    for i in reversed(range(9)):
        value = forward[i]
        for j in range(i + 1, 9):
            value = value - factor[j, i] * result[j]
        result[i] = value / roots[i]
    return result


def hot_cameras(feature_ref, hot_ref, block):
    names = iota((LANES, LANES), 0)
    for r in range(8):
        camera = feature_ref[pl.ds(CAMERA_AT * SPAN + block * 8 + r, 1), :].astype(jnp.int32) - 1
        hot = jnp.where(names == (camera & (LANES - 1)), 1.0, 0.0).astype(BF16)
        hot_ref[:, pl.ds(pl.multiple_of(block * PT_DEV + r * LANES, LANES), LANES)] = hot


def features_of(feature_ref, f, block):
    return feature_ref[pl.ds(pl.multiple_of(f * SPAN + block * 8, 8), 8), :]


def image_slots(vector, feature_ref, table_ref, image_ref, blocks):
    for j in range(9):
        for c in range(3):
            at = (3 * j + c) * 8
            table_ref[at : at + 8, :] = jnp.broadcast_to(vector[j][c : c + 1, :], (8, LANES))

    def one(block, carry):
        camera = features_of(feature_ref, CAMERA_AT, block).astype(jnp.int32) - 1
        third = camera >> 7
        lane = camera & (LANES - 1)
        images = [jnp.zeros((8, LANES), F32)] * 2
        for j in range(9):
            found = [
                jnp.take_along_axis(
                    table_ref[(3 * j + c) * 8 : (3 * j + c + 1) * 8, :],
                    lane,
                    axis=1,
                    mode="promise_in_bounds",
                )
                for c in range(3)
            ]
            value = jnp.where(third == 1, found[1], jnp.where(third == 2, found[2], found[0]))
            for i in range(2):
                images[i] = images[i] + features_of(feature_ref, 9 * i + j, block) * value
        for i in range(2):
            image_ref[pl.ds(pl.multiple_of(i * LANES + block * 8, 8), 8), :] = images[i]
        return carry

    lax.fori_loop(0, blocks, one, 0)


def keep_parts(part_ref, feature_ref, parts_ref, block, count):
    for r in range(8):
        lanes = pl.ds(pl.multiple_of(block * PT_DEV + r * LANES, LANES), LANES)
        camera = feature_ref[pl.ds(CAMERA_AT * SPAN + block * 8 + r, 1), :].astype(jnp.int32) - 1
        value = part_ref[pl.ds(r, count, stride=8), :]
        high = value.astype(BF16).astype(F32)
        both = jnp.concatenate([high, value - high], axis=0).astype(BF16)
        third = jnp.broadcast_to(camera >> 7, (16, LANES))
        for c in range(3):
            inside = jnp.where(third == c, 1.0, 0.0).astype(BF16)
            inside = jnp.concatenate([inside] * (count // 8), axis=0)
            parts_ref[2 * c * count : 2 * (c + 1) * count, lanes] = both * inside


def camera_sums(parts_ref, hot_ref, part_ref, sum_ref, count, many):
    few = FEW * LANES
    sum_ref[...] = dot_lanes(parts_ref[:, 0:few], hot_ref[:, 0:few])

    @pl.when(many)
    def _():
        sum_ref[...] += dot_lanes(parts_ref[:, few:], hot_ref[:, few:])

    part_ref[...] = jnp.zeros(part_ref.shape, F32)
    for c in range(3):
        at = 2 * c * count
        part_ref[pl.ds(c, count, stride=8), :] = (
            sum_ref[at : at + count, :] + sum_ref[at + count : at + 2 * count, :]
        )


def turn_in(got_ref, i):
    return jnp.transpose(got_ref[pl.ds(i, OWNERS, stride=2), :])


def turn_out(image_ref, out_ref):
    for i in range(2):
        out_ref[pl.ds(i, OWNERS, stride=2), :] = jnp.transpose(
            image_ref[i * LANES : (i + 1) * LANES, :]
        )


def first_camera_kernel(got_ref, feature_ref, factor_ref, first_ref, out_ref, flag_ref, hot_ref, parts_ref, table_ref, image_ref, sum_ref, part_ref):
    image_ref[...] = jnp.zeros((2 * LANES, LANES), F32)
    feature_ref[...] = jnp.zeros(feature_ref.shape, F32)

    def take_row(q):
        turned = jnp.transpose(got_ref[pl.ds(q, OWNERS, stride=ROWS), :])
        for k in range(GROUPS):
            feature_ref[pl.ds(q * GROUPS + k, WIDTH, stride=SPAN), :] = turned[
                k * WIDTH : (k + 1) * WIDTH, :
            ]
        return turned

    turned = take_row(0)
    flag_ref[...] = jnp.broadcast_to(
        jnp.max(turned[COUNT_AT + 1 : COUNT_AT + 2, :], axis=1, keepdims=True), (8, LANES)
    )
    most = jnp.max(turned[COUNT_AT : COUNT_AT + 1, :])
    many = most > FEW
    blocks = jnp.where(many, SPAN // 8, FEW // 8)
    few_rows = -(-FEW // GROUPS)
    for q in range(1, few_rows):
        take_row(q)

    @pl.when(many)
    def _():
        for q in range(few_rows, ROWS):
            take_row(q)

    part_ref[...] = jnp.zeros((ENTRIES * 8, LANES), F32)

    def gather_terms(block, carry):
        hot_cameras(feature_ref, hot_ref, block)
        f = [features_of(feature_ref, at, block) for at in range(20)]
        for at, (j, k) in enumerate(block_pairs):
            part_ref[at * 8 : (at + 1) * 8, :] = f[j] * f[k] + f[9 + j] * f[9 + k]
        for j in range(9):
            part_ref[(45 + j) * 8 : (46 + j) * 8, :] = -(f[j] * f[18] + f[9 + j] * f[19])
        keep_parts(part_ref, feature_ref, parts_ref, block, ENTRIES)
        return carry

    lax.fori_loop(0, blocks, gather_terms, 0)
    camera_sums(parts_ref, hot_ref, part_ref, sum_ref, ENTRIES, many)
    matrix = {}
    for at, (j, k) in enumerate(block_pairs):
        entry = part_ref[at * 8 : (at + 1) * 8, :]
        matrix[k, j] = entry + 1.0 if j == k else entry
    side = [part_ref[(45 + j) * 8 : (46 + j) * 8, :] for j in range(9)]
    factor, roots = {}, []
    for j in range(9):
        pivot = matrix[j, j]
        for m in range(j):
            pivot = pivot - factor[j, m] * factor[j, m]
        roots.append(jnp.sqrt(pivot))
        for i in range(j + 1, 9):
            running = matrix[i, j]
            for m in range(j):
                running = running - factor[i, m] * factor[j, m]
            factor[i, j] = running / roots[j]
    for at, (j, k) in enumerate(block_pairs):
        factor_ref[at * 8 : (at + 1) * 8, :] = roots[j] if j == k else factor[k, j]
    first = solve(factor, roots, side)
    energy = side[0] * first[0]
    for j in range(1, 9):
        energy = energy + side[j] * first[j]
    for j in range(9):
        first_ref[j * 8 : (j + 1) * 8, :] = first[j]
    first_ref[72:80, :] = energy
    first_ref[80:88, :] = jnp.broadcast_to(jnp.max(turned[COUNT_AT : COUNT_AT + 1, :], axis=1, keepdims=True), (8, LANES))
    image_slots(first, feature_ref, table_ref, image_ref, blocks)
    turn_out(image_ref, out_ref)


def either_span(flag_ref, work):
    many = jnp.max(flag_ref[0:8, :]) > FEW
    pl.when(many)(lambda: work(SPAN))
    pl.when(jnp.logical_not(many))(lambda: work(FEW))


def pull_slots(got_ref, route_ref, point_ref, length_ref, state_ref, root_ref, value_ref, pulled_ref, curve_ref, span, back):
    images = []
    for i in range(2):
        images.append(turn_in(got_ref, i)[0:span, :])
    high, low = two_parts(jnp.concatenate(images, axis=0))
    parts = jnp.concatenate([high, low], axis=1)
    owners = iota((OWNERS, PT_DEV), 0)
    ranks = iota((span, PT_DEV), 0)
    for s in range(TRACK):
        hot = jnp.where(owners == route_ref[s : s + 1, :], 1.0, 0.0).astype(BF16)
        got = dot(parts, jnp.concatenate([hot, hot], axis=0))
        here = ranks == route_ref[TRACK + s : TRACK + s + 1, :]
        for i in range(2):
            value_ref[i * TRACK + s : i * TRACK + s + 1, :] = jnp.sum(
                jnp.where(here, got[i * span : (i + 1) * span, :], 0.0), axis=0, keepdims=True
            )
    curve = jnp.zeros((TRACK, LANES), F32)
    for chunk in range(PT_DEV // LANES):
        lanes = slice(chunk * LANES, (chunk + 1) * LANES)
        used = used_slots(length_ref, lanes)
        point = masked_points(point_ref, used, lanes)
        root = [root_ref[at * TRACK : (at + 1) * TRACK, lanes] for at in range(3)]
        image1 = value_ref[TRACK : 2 * TRACK, lanes] * root[2]
        image = [(value_ref[0:TRACK, lanes] - root[1] * image1) * root[0], image1]
        pulled = [over_tracks(point[0][a] * image[0] + point[1][a] * image[1]) for a in range(3)]
        inverse = [state_ref[at : at + 1, lanes] for at in range(6)]
        solved = times_inverse(inverse, pulled)
        for a in range(3):
            pulled_ref[a : a + 1, lanes] = pulled[a]
        result = [
            image[i] - (point[i][0] * solved[0] + point[i][1] * solved[1] + point[i][2] * solved[2])
            for i in range(2)
        ]
        if back:
            result0 = result[0] * root[0]
            value_ref[0:TRACK, lanes] = result0
            value_ref[TRACK : 2 * TRACK, lanes] = (result[1] - root[1] * result0) * root[2]
        else:
            curve = curve + image[0] * result[0] + image[1] * result[1]
    if not back:
        curve_ref[...] = curve


def first_point_kernel(got_ref, route_ref, point_ref, length_ref, state_ref, root_ref, flag_ref, pulled_ref, out_ref, value_ref, image_ref):
    image_ref[...] = jnp.zeros((2 * LANES, LANES), F32)
    owners = iota((OWNERS, PT_DEV), 0)

    def work(span):
        pull_slots(got_ref, route_ref, point_ref, length_ref, state_ref, root_ref, value_ref, pulled_ref, None, span, True)
        ranks = iota((span, PT_DEV), 0)
        sums = jnp.zeros((4 * span, OWNERS), F32)
        for s in range(TRACK):
            hot = jnp.where(owners == route_ref[s : s + 1, :], 1.0, 0.0).astype(BF16)
            here = ranks == route_ref[TRACK + s : TRACK + s + 1, :]
            spread = []
            for i in range(2):
                value = value_ref[i * TRACK + s : i * TRACK + s + 1, :]
                spread.append(jnp.where(here, value, 0.0))
            high, low = two_parts(jnp.concatenate(spread, axis=0))
            sums = sums + dot_lanes(jnp.concatenate([high, low], axis=0), hot)
        sums = sums[0 : 2 * span] + sums[2 * span :]
        for i in range(2):
            image_ref[i * LANES : i * LANES + span, :] = sums[i * span : (i + 1) * span, :]

    either_span(flag_ref, work)
    turn_out(image_ref, out_ref)


def second_point_kernel(got_ref, route_ref, point_ref, length_ref, state_ref, root_ref, flag_ref, pulled_ref, out_ref, scalar_ref, value_ref, curve_ref):
    def work(span):
        pull_slots(got_ref, route_ref, point_ref, length_ref, state_ref, root_ref, value_ref, pulled_ref, curve_ref, span, False)

    either_span(flag_ref, work)
    out_ref[...] = jnp.broadcast_to(total(curve_ref[...]), (OWNERS, LANES))
    scalar_ref[...] = jnp.broadcast_to(
        jnp.sum(got_ref[pl.ds(0, OWNERS, stride=2), :], axis=0, keepdims=True), (8, LANES)
    )


def second_camera_kernel(got_ref, feature_ref, factor_ref, first_ref, second_ref, out_ref, hot_ref, parts_ref, table_ref, image_ref, sum_ref, wide_ref):
    for i in range(2):
        image_ref[i * LANES : (i + 1) * LANES, :] = turn_in(got_ref, i)
    many = jnp.max(first_ref[80:88, :]) > FEW
    blocks = jnp.where(many, SPAN // 8, FEW // 8)
    wide_ref[...] = jnp.zeros((LANES, LANES), F32)

    def gather_terms(block, carry):
        hot_cameras(feature_ref, hot_ref, block)
        back = [
            image_ref[pl.ds(pl.multiple_of(i * LANES + block * 8, 8), 8), :] for i in range(2)
        ]
        for j in range(9):
            wide_ref[j * 8 : (j + 1) * 8, :] = (
                features_of(feature_ref, j, block) * back[0]
                + features_of(feature_ref, 9 + j, block) * back[1]
            )
        keep_parts(wide_ref, feature_ref, parts_ref, block, 16)
        return carry

    lax.fori_loop(0, blocks, gather_terms, 0)
    camera_sums(parts_ref, hot_ref, wide_ref, sum_ref, 16, many)
    first = [first_ref[j * 8 : (j + 1) * 8, :] for j in range(9)]
    image = [first[j] + wide_ref[j * 8 : (j + 1) * 8, :] for j in range(9)]
    factor, roots = {}, []
    for at, (j, k) in enumerate(block_pairs):
        entry = factor_ref[at * 8 : (at + 1) * 8, :]
        if j == k:
            roots.append(entry)
        else:
            factor[k, j] = entry
    second = solve(factor, roots, image)
    for j in range(9):
        second_ref[j * 8 : (j + 1) * 8, :] = second[j]

    def inner(left, right):
        value = left[0] * right[0]
        for j in range(1, 9):
            value = value + left[j] * right[j]
        return value

    image_slots(second, feature_ref, table_ref, image_ref, blocks)
    scalars = [first_ref[72:80, :], inner(first, image), inner(image, second), inner(second, second)]
    for at, value in enumerate(scalars):
        image_ref[SPAN + at : SPAN + at + 1, :] = jnp.broadcast_to(total(value), (1, LANES))
    turn_out(image_ref, out_ref)


def finish_kernel(curve_ref, scalar_ref, first_ref, second_ref, state_ref, first_pulled_ref, second_pulled_ref, flag_ref, dense_camera_ref, dense_point_ref, camera_out, point_out, camera_ref, point_ref, camera_sem, point_sem):
    over = flag_ref[0:1, 0:1] > CAP
    own = jnp.sum(curve_ref[...], axis=0, keepdims=True)[:, 0:1]
    energy, curvature, crossed, square = [
        scalar_ref[0:1, SPAN + at : SPAN + at + 1] for at in range(4)
    ]
    step_size = energy / curvature
    renewed = step_size * step_size * crossed - energy
    ratio = 1.0 + renewed / energy
    second_step = renewed / (
        ratio * ratio * curvature
        - 2.0 * step_size * ratio * crossed
        + step_size * step_size * (square + own)
    )
    first_weight = step_size + second_step * ratio
    second_weight = -second_step * step_size
    for c in range(3):
        moved = (
            first_weight * first_ref[pl.ds(c, 9, stride=8), :]
            + second_weight * second_ref[pl.ds(c, 9, stride=8), :]
        )
        lanes = slice(c * LANES, (c + 1) * LANES)
        camera_ref[:, lanes] = jnp.where(over, dense_camera_ref[:, lanes], moved)
    camera_copy = pltpu.make_async_copy(camera_ref, camera_out, camera_sem)
    camera_copy.start()
    left = [
        state_ref[6 + a : 7 + a, :]
        - first_weight * first_pulled_ref[a : a + 1, :]
        - second_weight * second_pulled_ref[a : a + 1, :]
        for a in range(3)
    ]
    moved = times_inverse([state_ref[at : at + 1, :] for at in range(6)], left)
    for a in range(3):
        point_ref[a : a + 1, :] = jnp.where(over, dense_point_ref[a : a + 1, :], moved[a])
    point_copy = pltpu.make_async_copy(point_ref, point_out, point_sem)
    point_copy.start()
    camera_copy.wait()
    point_copy.wait()


def call(kernel, outs, scratch, operands, in_scalar=0):
    specs = [
        pl.BlockSpec(memory_space=pltpu.SMEM if at < in_scalar else pltpu.VMEM)
        for at in range(len(operands))
    ]
    return pl.pallas_call(
        kernel,
        out_shape=[jax.ShapeDtypeStruct(shape, dtype) for shape, dtype in outs],
        in_specs=specs,
        out_specs=[pl.BlockSpec(memory_space=pltpu.VMEM)] * len(outs),
        scratch_shapes=[pltpu.VMEM(shape, dtype) for shape, dtype in scratch],
        compiler_params=PARAMS,
    )(*operands)


def exchange(rows):
    blocks = rows.reshape(OWNERS, 1, -1)
    blocks = lax.all_to_all(blocks, ("row", "col"), split_axis=0, concat_axis=0, tiled=True)
    return blocks.reshape(rows.shape)


def by_slots(camera_jacobian, point_jacobian, residuals, observed_camera, track_length):
    lengths = track_length.reshape(1, PT_DEV)
    in_vmem = [pl.BlockSpec(memory_space=pltpu.VMEM)]
    held = [(18, TRACK, PT_DEV), (6, TRACK, PT_DEV), (2, TRACK, PT_DEV)]
    outs = [
        ((WIDTH * PT_DEV * TRACK // LANES, LANES), F32),
        ((BLOCKS, LANES), jnp.int32),
        ((2 * TRACK, PT_DEV), jnp.int32),
        ((16, PT_DEV), F32),
        ((3 * TRACK, PT_DEV), F32),
        ((OWNERS, LANES), F32),
    ]
    pay, code, route, state, root, flag = pl.pallas_call(
        prepare_kernel,
        out_shape=[jax.ShapeDtypeStruct(shape, dtype) for shape, dtype in outs],
        in_specs=[pl.BlockSpec(memory_space=pl.ANY)] * 3 + in_vmem * 2,
        out_specs=in_vmem * len(outs),
        scratch_shapes=[pltpu.VMEM(shape, F32) for shape in held]
        + [pltpu.SemaphoreType.DMA] * 3,
        compiler_params=PARAMS,
    )(camera_jacobian, point_jacobian, residuals, observed_camera, lengths)
    (sent,) = call(
        dispatch_kernel,
        [((OWNERS * ROWS, LANES), F32)],
        [((BLOCKS, LANES, 1, LANES), F32), ((GROUPS * OWNERS * ROWS + 8, 1, LANES), F32)],
        (code, pay, flag),
        in_scalar=1,
    )
    hot = ((LANES, SPAN * LANES), BF16)
    table = ((27 * 8, LANES), F32)
    image = ((2 * LANES, LANES), F32)
    pair = ((2 * OWNERS, LANES), F32)
    features, factor, first, out, overflow = call(
        first_camera_kernel,
        [((WIDTH * SPAN, LANES), F32), ((45 * 8, LANES), F32), ((88, LANES), F32), pair, ((8, LANES), F32)],
        [hot, ((6 * ENTRIES, SPAN * LANES), BF16), table, image, ((6 * ENTRIES, LANES), F32), ((ENTRIES * 8, LANES), F32)],
        (exchange(sent),),
    )
    first_pulled, out = call(
        first_point_kernel,
        [((8, PT_DEV), F32), pair],
        [((2 * TRACK, PT_DEV), F32), image],
        (exchange(out), route, point_jacobian, lengths, state, root, flag),
    )
    second, out = call(
        second_camera_kernel,
        [((72, LANES), F32), pair],
        [hot, ((96, SPAN * LANES), BF16), table, image, ((96, LANES), F32), ((LANES, LANES), F32)],
        (exchange(out), features, factor, first),
    )
    second_pulled, curve, scalars = call(
        second_point_kernel,
        [((8, PT_DEV), F32), ((OWNERS, LANES), F32), ((8, LANES), F32)],
        [((2 * TRACK, PT_DEV), F32), ((TRACK, LANES), F32)],
        (exchange(out), route, point_jacobian, lengths, state, root, flag),
    )
    return overflow, (exchange(curve), scalars, first, second, state, first_pulled, second_pulled)


def finish(*operands):
    shapes = [(9, CAM_DEV), (3, PT_DEV)]
    return tuple(
        pl.pallas_call(
            finish_kernel,
            out_shape=[jax.ShapeDtypeStruct(shape, F32) for shape in shapes],
            in_specs=[pl.BlockSpec(memory_space=pltpu.VMEM)] * len(operands),
            out_specs=[pl.BlockSpec(memory_space=pltpu.HBM)] * 2,
            scratch_shapes=[pltpu.VMEM(shape, F32) for shape in shapes]
            + [pltpu.SemaphoreType.DMA] * 2,
            compiler_params=PARAMS,
        )(*operands)
    )


damping = 1.0


def inverse_small(matrix):
    entries = [[matrix[row_at, col_at] for col_at in range(3)] for row_at in range(3)]
    cofactor = [
        [
            entries[(row_at + 1) % 3][(col_at + 1) % 3]
            * entries[(row_at + 2) % 3][(col_at + 2) % 3]
            - entries[(row_at + 1) % 3][(col_at + 2) % 3]
            * entries[(row_at + 2) % 3][(col_at + 1) % 3]
            for col_at in range(3)
        ]
        for row_at in range(3)
    ]
    determinant = (
        entries[0][0] * cofactor[0][0]
        + entries[0][1] * cofactor[0][1]
        + entries[0][2] * cofactor[0][2]
    )
    return jnp.stack(
        [
            jnp.stack([cofactor[col_at][row_at] / determinant for col_at in range(3)])
            for row_at in range(3)
        ]
    )


def block_inverse(matrix):
    factor = {}
    for col_at in range(9):
        pivot_value = matrix[col_at, col_at]
        for middle in range(col_at):
            pivot_value = pivot_value - factor[col_at, middle] * factor[col_at, middle]
        diagonal_root = jnp.sqrt(pivot_value)
        factor[col_at, col_at] = diagonal_root
        for row_at in range(col_at + 1, 9):
            running = matrix[row_at, col_at]
            for middle in range(col_at):
                running = running - factor[row_at, middle] * factor[col_at, middle]
            factor[row_at, col_at] = running / diagonal_root
    factor_inverse = {}
    for row_at in range(9):
        factor_inverse[row_at, row_at] = 1.0 / factor[row_at, row_at]
        for col_at in range(row_at):
            running = factor[row_at, col_at] * factor_inverse[col_at, col_at]
            for middle in range(col_at + 1, row_at):
                running = running + factor[row_at, middle] * factor_inverse[middle, col_at]
            factor_inverse[row_at, col_at] = -running / factor[row_at, row_at]
    result_rows = []
    for row_at in range(9):
        entries = []
        for col_at in range(9):
            running = (
                factor_inverse[max(row_at, col_at), row_at]
                * factor_inverse[max(row_at, col_at), col_at]
            )
            for middle in range(max(row_at, col_at) + 1, 9):
                running = running + factor_inverse[middle, row_at] * factor_inverse[middle, col_at]
            entries.append(running)
        result_rows.append(jnp.stack(entries))
    return jnp.stack(result_rows)


def assemble(packed):
    positions = {}
    for index_at, pair in enumerate(block_pairs):
        positions[pair[0], pair[1]] = index_at
        positions[pair[1], pair[0]] = index_at
    return jnp.stack(
        [
            jnp.stack(
                [
                    packed[positions[row_at, col_at]] + (damping if row_at == col_at else 0.0)
                    for col_at in range(9)
                ]
            )
            for row_at in range(9)
        ]
    )


def apply_blocks(inverse_blocks, vector):
    return jnp.sum(inverse_blocks * vector[None], axis=1)


def slot_basics(camera_jacobian, point_jacobian, residuals, track_length):
    tracks = camera_jacobian.shape[1]
    in_track = (jnp.arange(tracks, dtype=jnp.int32)[:, None] < track_length[None, :]).astype(
        jnp.float32
    )
    camera_blocks = camera_jacobian.reshape(2, 9, tracks, -1) * in_track
    point_blocks = point_jacobian.reshape(2, 3, tracks, -1) * in_track
    errors = residuals * in_track
    coupling = jnp.sum(camera_blocks[:, :, None] * point_blocks[:, None], axis=0)
    point_system = jnp.sum(point_blocks[:, :, None] * point_blocks[:, None], axis=(0, 3))
    point_system = point_system + damping * jnp.eye(3, dtype=jnp.float32)[:, :, None]
    point_inverse = inverse_small(point_system)
    point_gradient = -jnp.sum(point_blocks * errors[:, None], axis=(0, 2))
    return (camera_blocks, errors, coupling, point_inverse, point_gradient)


def camera_terms(camera_blocks, errors, coupling, point_inverse, point_gradient):
    solved = jnp.sum(point_inverse * point_gradient[None], axis=1)
    scaled = coupling[:, 0][:, None] * point_inverse[0][None, :, None, :]
    for middle in range(1, 3):
        scaled = scaled + coupling[:, middle][:, None] * point_inverse[middle][None, :, None, :]
    packed = []
    for leading, trailing in block_pairs:
        packed.append(
            jnp.sum(camera_blocks[:, leading] * camera_blocks[:, trailing], axis=0)
            - jnp.sum(scaled[leading] * coupling[trailing], axis=0)
        )
    right_side = -jnp.sum(camera_blocks * errors[:, None], axis=0) - jnp.sum(
        coupling * solved[None, :, None], axis=1
    )
    return jnp.concatenate([jnp.stack(packed), right_side], axis=0)


def slot_product(camera_blocks, coupling, point_inverse, gathered):
    projected = jnp.sum(camera_blocks * gathered[None], axis=1)
    pulled = jnp.sum(coupling * gathered[:, None], axis=(0, 2))
    solved = jnp.sum(point_inverse * pulled[None], axis=1)
    return jnp.sum(camera_blocks * projected[:, None], axis=0) - jnp.sum(
        coupling * solved[None, :, None], axis=1
    )


def by_dense(camera_jacobian, point_jacobian, residuals, observed_camera, track_length):
    camera_blocks, errors, coupling, point_inverse, point_gradient = slot_basics(
        camera_jacobian, point_jacobian, residuals, track_length
    )
    tracks, points = observed_camera.shape
    rows, cols = lax.axis_size("row"), lax.axis_size("col")
    cameras = CAM_DEV * rows * cols
    flat_cameras = observed_camera.reshape(-1)

    def into_cameras(values):
        width = values.shape[0]
        by_camera = (
            jnp.zeros((cameras, width), jnp.float32).at[flat_cameras].add(jnp.transpose(values))
        )
        return jnp.transpose(by_camera)

    def pick_slots(whole):
        slot_rows = jnp.transpose(whole)[flat_cameras]
        return jnp.transpose(slot_rows).reshape(9, tracks, points)

    def spread_out(value):
        copies = jnp.broadcast_to(value[:, None], (9, OWNERS, CAM_DEV)).reshape(9, cameras)
        return lax.all_to_all(copies, ("row", "col"), split_axis=1, concat_axis=1, tiled=True)

    term_values = camera_terms(
        camera_blocks, errors, coupling, point_inverse, point_gradient
    ).reshape(54, -1)
    local_terms = into_cameras(term_values).reshape(54, rows * cols, CAM_DEV)
    own_terms = jnp.sum(
        lax.all_to_all(local_terms, ("row", "col"), split_axis=1, concat_axis=1, tiled=True), axis=1
    )
    inverse_blocks = block_inverse(assemble(own_terms[:45]))
    right_side = own_terms[45:]

    first = apply_blocks(inverse_blocks, right_side)
    first_slots = pick_slots(spread_out(first))
    first_pulled = jnp.sum(coupling * first_slots[:, None], axis=(0, 2))
    contrib = slot_product(camera_blocks, coupling, point_inverse, first_slots)
    local_image = into_cameras(contrib.reshape(9, -1)).reshape(9, OWNERS, CAM_DEV)
    gathered_image = lax.all_to_all(
        local_image, ("row", "col"), split_axis=1, concat_axis=1, tiled=True
    )
    first_image = damping * first + jnp.sum(gathered_image, axis=1)

    second = apply_blocks(inverse_blocks, first_image)
    second_slots = pick_slots(spread_out(second))
    second_pulled = jnp.sum(coupling * second_slots[:, None], axis=(0, 2))
    projected = jnp.sum(camera_blocks * second_slots[None], axis=1)
    solved = jnp.sum(point_inverse * second_pulled[None], axis=1)
    own_sums = jnp.stack(
        [
            jnp.sum(right_side * first),
            jnp.sum(first * first_image),
            jnp.sum(first_image * second),
            jnp.sum(second * second)
            + jnp.sum(projected * projected)
            - jnp.sum(second_pulled * solved),
        ]
    )
    spread = jnp.broadcast_to(own_sums[None], (OWNERS, 4))
    energy, curvature, crossed, second_curvature = jnp.sum(exchange(spread), axis=0)
    step_size = energy / curvature
    renewed = step_size * step_size * crossed - energy
    ratio = 1.0 + renewed / energy
    second_step = renewed / (
        ratio * ratio * curvature
        - 2.0 * step_size * ratio * crossed
        + step_size * step_size * second_curvature
    )
    first_weight = step_size + second_step * ratio
    second_weight = -second_step * step_size
    camera_move = first_weight * first + second_weight * second
    pulled = first_weight * first_pulled + second_weight * second_pulled
    point_move = jnp.sum(point_inverse * (point_gradient - pulled)[None], axis=1)
    return (camera_move, point_move)


def on_device(camera_jacobian, point_jacobian, residuals, observed_camera, track_length):
    operands = (camera_jacobian, point_jacobian, residuals, observed_camera, track_length)
    overflow, kept = by_slots(*operands)
    dense = lax.cond(
        overflow[0, 0] > CAP,
        lambda *given: by_dense(*given),
        lambda *given: (jnp.zeros((9, CAM_DEV), F32), jnp.zeros((3, PT_DEV), F32)),
        *operands,
    )
    return finish(*kept, overflow, *dense)


def solution(mesh):
    in_specs = (
        P(None, None, ("row", "col")),
        P(None, None, ("row", "col")),
        P(None, None, ("row", "col")),
        P(None, ("row", "col")),
        P(("row", "col")),
    )
    out_specs = (P(None, ("row", "col")), P(None, ("row", "col")))
    return jax.shard_map(
        on_device, mesh=mesh, in_specs=in_specs, out_specs=out_specs, check_vma=False
    )
```

```python
import jax
import jax.numpy as jnp
from jax import lax
from jax.experimental import pallas as pl
from jax.experimental.pallas import tpu as pltpu
from jax.sharding import PartitionSpec as P

CAM_DEV = 384
TRACK = 8
PT_DEV = 1024
OWNERS = 128
LANES = 128
WIDTH = 21
GROUPS = 6
ROWS = 13
CAP = GROUPS * ROWS
SPAN = 80
FEW = 64
CAMERA_AT = 20
ENTRIES = 56
COUNT_AT = GROUPS * WIDTH
BLOCKS = TRACK * PT_DEV // LANES

F32 = jnp.float32
BF16 = jnp.bfloat16
PARAMS = pltpu.CompilerParams(vmem_limit_bytes=48 * 2**20)
block_pairs = [(leading, trailing) for leading in range(9) for trailing in range(leading, 9)]


def iota(shape, axis):
    return lax.broadcasted_iota(jnp.int32, shape, axis)


def two_parts(value):
    high = value.astype(BF16)
    low = (value - high.astype(F32)).astype(BF16)
    return high, low


def dot(left, right):
    return jnp.dot(left, right, preferred_element_type=F32)


def dot_lanes(left, right):
    return lax.dot_general(left, right, (((1,), (1,)), ((), ())), preferred_element_type=F32)


def total(value):
    return jnp.sum(jnp.sum(value, axis=0, keepdims=True), axis=1, keepdims=True)


def over_tracks(value):
    return jnp.sum(value, axis=0, keepdims=True)


def used_slots(length_ref, lanes):
    return iota((TRACK, LANES), 0) < length_ref[:, lanes]


def masked_points(point_ref, used, lanes):
    return [
        [jnp.where(used, point_ref[3 * i + a, :, lanes], 0.0) for a in range(3)] for i in range(2)
    ]


def times_inverse(inverse, vector):
    v00, v01, v02, v11, v12, v22 = inverse
    x, y, z = vector
    return [v00 * x + v01 * y + v02 * z, v01 * x + v11 * y + v12 * z, v02 * x + v12 * y + v22 * z]


def owner_of(camera):
    return ((camera >> 7) * 171) >> 9


def prepare_kernel(camera_in, point_in, error_in, index_ref, length_ref, pay_ref, code_ref, route_ref, state_ref, root_ref, flag_ref, camera_ref, point_ref, error_ref, camera_sem, point_sem, error_sem):
    copies = [
        pltpu.make_async_copy(camera_in, camera_ref, camera_sem),
        pltpu.make_async_copy(point_in, point_ref, point_sem),
        pltpu.make_async_copy(error_in, error_ref, error_sem),
    ]
    for copy in copies:
        copy.start()
    used = iota((TRACK, PT_DEV), 0) < length_ref[...]
    route_ref[0:TRACK, :] = jnp.where(used, owner_of(index_ref[...]), OWNERS)

    step = 256
    upto = jnp.where(iota((step, step), 0) <= iota((step, step), 1), 1.0, 0.0).astype(BF16)
    before = jnp.zeros((OWNERS, step), F32)
    names = iota((OWNERS, step), 0)
    for s in range(TRACK):
        for chunk in range(PT_DEV // step):
            lanes = slice(chunk * step, (chunk + 1) * step)
            chosen = names == route_ref[s : s + 1, lanes]
            hot = jnp.where(chosen, 1.0, 0.0).astype(BF16)
            counts = dot(hot, upto)
            rank = jnp.sum(jnp.where(chosen, counts + before, 0.0), axis=0, keepdims=True) - 1.0
            before = before + jnp.broadcast_to(counts[:, step - 1 : step], (OWNERS, step))
            route_ref[TRACK + s : TRACK + s + 1, lanes] = rank.astype(jnp.int32)

    owner = route_ref[0:TRACK, :]
    rank = route_ref[TRACK : 2 * TRACK, :]
    fits = (owner < OWNERS) & (rank < CAP)
    row_at = (rank * 171) >> 10
    place = (rank - row_at * GROUPS) * (OWNERS * ROWS) + owner * ROWS + row_at
    code = jnp.where(fits, place, GROUPS * OWNERS * ROWS)
    for chunk in range(PT_DEV // LANES):
        code_ref[chunk * TRACK : (chunk + 1) * TRACK, :] = code[:, chunk * LANES : (chunk + 1) * LANES]
    most = jnp.max(jnp.max(before, axis=0, keepdims=True), axis=1, keepdims=True)
    lane = iota((OWNERS, LANES), 1)
    flag_ref[...] = jnp.where(lane > COUNT_AT, most, before[:, 0:LANES])
    for copy in copies:
        copy.wait()
    for chunk in range(PT_DEV // LANES):
        lanes = slice(chunk * LANES, (chunk + 1) * LANES)
        used = used_slots(length_ref, lanes)
        point = masked_points(point_ref, used, lanes)
        error = [jnp.where(used, error_ref[i, :, lanes], 0.0) for i in range(2)]

        def pair(a, b):
            return over_tracks(point[0][a] * point[0][b] + point[1][a] * point[1][b])

        s00, s01, s02 = 1.0 + pair(0, 0), pair(0, 1), pair(0, 2)
        s11, s12, s22 = 1.0 + pair(1, 1), pair(1, 2), 1.0 + pair(2, 2)
        c00 = s11 * s22 - s12 * s12
        c01 = s12 * s02 - s01 * s22
        c02 = s01 * s12 - s11 * s02
        c11 = s22 * s00 - s02 * s02
        c12 = s02 * s01 - s12 * s00
        c22 = s00 * s11 - s01 * s01
        determinant = s00 * c00 + s01 * c01 + s02 * c02
        inverse = [c / determinant for c in (c00, c01, c02, c11, c12, c22)]
        gradient = [
            -over_tracks(point[0][a] * error[0] + point[1][a] * error[1]) for a in range(3)
        ]
        for at, value in enumerate(inverse + gradient):
            state_ref[at : at + 1, lanes] = value
        solved = times_inverse(inverse, gradient)
        u0 = times_inverse(inverse, point[0])
        u1 = times_inverse(inverse, point[1])

        def along(left, right):
            return left[0] * right[0] + left[1] * right[1] + left[2] * right[2]

        camera = index_ref[:, lanes]
        owner = owner_of(camera)
        local = camera - owner * CAM_DEV
        b01 = -along(u0, point[1])
        root0 = jnp.sqrt(1.0 - along(u0, point[0]))
        root1 = b01 / root0
        root2 = jnp.sqrt(1.0 - along(u1, point[1]) - root1 * root1)
        inverse0, inverse2 = 1.0 / root0, 1.0 / root2
        side0 = (error[0] + along(solved, point[0])) * inverse0
        side1 = (error[1] + along(solved, point[1]) - root1 * side0) * inverse2
        values = [root0 * camera_ref[j, :, lanes] + root1 * camera_ref[9 + j, :, lanes] for j in range(9)]
        values += [root2 * camera_ref[9 + j, :, lanes] for j in range(9)]
        values += [side0, side1, (local + 1).astype(F32)]
        for at, value in enumerate((inverse0, root1, inverse2)):
            root_ref[at * TRACK : (at + 1) * TRACK, lanes] = value
        for f in range(WIDTH):
            at = (chunk * WIDTH + f) * TRACK
            pay_ref[at : at + TRACK, :] = values[f]


def dispatch_kernel(code_ref, pay_ref, flag_ref, out_ref, slot_ref, block_ref):
    rows = OWNERS * ROWS
    zeros = jnp.zeros((8, LANES), F32)
    slots_ref = slot_ref.reshape(BLOCKS * LANES, LANES)
    blocks_ref = block_ref.reshape(GROUPS * rows + 8, LANES)

    share = -(-GROUPS * rows // (BLOCKS * 8)) * 8
    within = iota((LANES, LANES), 1) % WIDTH
    for first in range(0, BLOCKS, GROUPS):
        blocks = []
        for block in range(first, first + GROUPS):
            chunk, s = divmod(block, TRACK)
            if block < BLOCKS:
                blocks.append(pay_ref[pl.ds(chunk * WIDTH * TRACK + s, WIDTH, stride=TRACK), :])
            else:
                blocks.append(jnp.zeros((WIDTH, LANES), F32))
        turned = jnp.transpose(jnp.concatenate(blocks + [zeros[0 : LANES - COUNT_AT]], axis=0))
        for block in range(first, min(first + GROUPS, BLOCKS)):
            slots_ref[block * LANES : (block + 1) * LANES, :] = jnp.take_along_axis(
                turned, within + (block - first) * WIDTH, axis=1, mode="promise_in_bounds"
            )
            start = min(block * share, GROUPS * rows)
            count = min(share, GROUPS * rows - start)
            if count:
                blocks_ref[start : start + count, :] = jnp.zeros((count, LANES), F32)

    def place(block, carry):
        def load(start):
            columns = range(start, min(start + 16, LANES))
            return [(code_ref[block, j], slot_ref[block, j]) for j in columns]

        ready = load(0)
        for start in range(16, LANES + 16, 16):
            coming = load(start)
            for code, slot in ready:
                block_ref[code] = slot
            ready = coming
        return carry

    lax.fori_loop(0, BLOCKS, place, 0)
    group = iota((8, LANES), 1) // WIDTH

    def merge(at, carry):
        for j in range(8):
            start = pl.multiple_of(at * 64 + j * 8, 8)
            value = zeros
            for k in range(GROUPS):
                value = jnp.where(group == k, blocks_ref[pl.ds(k * rows + start, 8), :], value)
            out_ref[pl.ds(start, 8), :] = value
        return carry

    lax.fori_loop(0, rows // 64, merge, 0)
    lane = iota((OWNERS, LANES), 1)
    leading = pl.ds(0, OWNERS, stride=ROWS)
    out_ref[leading, :] = jnp.where(lane >= COUNT_AT, flag_ref[...], out_ref[leading, :])


def solve(factor, roots, vector):
    forward = []
    for i in range(9):
        value = vector[i]
        for j in range(i):
            value = value - factor[i, j] * forward[j]
        forward.append(value / roots[i])
    result = [None] * 9
    for i in reversed(range(9)):
        value = forward[i]
        for j in range(i + 1, 9):
            value = value - factor[j, i] * result[j]
        result[i] = value / roots[i]
    return result


def hot_cameras(feature_ref, hot_ref, block):
    names = iota((LANES, LANES), 0)
    for r in range(8):
        camera = feature_ref[pl.ds(CAMERA_AT * SPAN + block * 8 + r, 1), :].astype(jnp.int32) - 1
        hot = jnp.where(names == (camera & (LANES - 1)), 1.0, 0.0).astype(BF16)
        hot_ref[:, pl.ds(pl.multiple_of(block * PT_DEV + r * LANES, LANES), LANES)] = hot


def features_of(feature_ref, f, block):
    return feature_ref[pl.ds(pl.multiple_of(f * SPAN + block * 8, 8), 8), :]


def image_slots(vector, feature_ref, table_ref, image_ref, blocks):
    for j in range(9):
        for c in range(3):
            at = (3 * j + c) * 8
            table_ref[at : at + 8, :] = jnp.broadcast_to(vector[j][c : c + 1, :], (8, LANES))

    def one(block, carry):
        camera = features_of(feature_ref, CAMERA_AT, block).astype(jnp.int32) - 1
        third = camera >> 7
        lane = camera & (LANES - 1)
        images = [jnp.zeros((8, LANES), F32)] * 2
        for j in range(9):
            found = [
                jnp.take_along_axis(
                    table_ref[(3 * j + c) * 8 : (3 * j + c + 1) * 8, :],
                    lane,
                    axis=1,
                    mode="promise_in_bounds",
                )
                for c in range(3)
            ]
            value = jnp.where(third == 1, found[1], jnp.where(third == 2, found[2], found[0]))
            for i in range(2):
                images[i] = images[i] + features_of(feature_ref, 9 * i + j, block) * value
        for i in range(2):
            image_ref[pl.ds(pl.multiple_of(i * LANES + block * 8, 8), 8), :] = images[i]
        return carry

    lax.fori_loop(0, blocks, one, 0)


def keep_parts(part_ref, feature_ref, parts_ref, block, count):
    for r in range(8):
        lanes = pl.ds(pl.multiple_of(block * PT_DEV + r * LANES, LANES), LANES)
        camera = feature_ref[pl.ds(CAMERA_AT * SPAN + block * 8 + r, 1), :].astype(jnp.int32) - 1
        value = part_ref[pl.ds(r, count, stride=8), :]
        high = value.astype(BF16).astype(F32)
        both = jnp.concatenate([high, value - high], axis=0).astype(BF16)
        third = jnp.broadcast_to(camera >> 7, (16, LANES))
        for c in range(3):
            inside = jnp.where(third == c, 1.0, 0.0).astype(BF16)
            inside = jnp.concatenate([inside] * (count // 8), axis=0)
            parts_ref[2 * c * count : 2 * (c + 1) * count, lanes] = both * inside


def camera_sums(parts_ref, hot_ref, part_ref, sum_ref, count, many):
    few = FEW * LANES
    sum_ref[...] = dot_lanes(parts_ref[:, 0:few], hot_ref[:, 0:few])

    @pl.when(many)
    def _():
        sum_ref[...] += dot_lanes(parts_ref[:, few:], hot_ref[:, few:])

    part_ref[...] = jnp.zeros(part_ref.shape, F32)
    for c in range(3):
        at = 2 * c * count
        part_ref[pl.ds(c, count, stride=8), :] = (
            sum_ref[at : at + count, :] + sum_ref[at + count : at + 2 * count, :]
        )


def turn_in(got_ref, i):
    return jnp.transpose(got_ref[pl.ds(i, OWNERS, stride=2), :])


def turn_out(image_ref, out_ref):
    for i in range(2):
        out_ref[pl.ds(i, OWNERS, stride=2), :] = jnp.transpose(
            image_ref[i * LANES : (i + 1) * LANES, :]
        )


def first_camera_kernel(got_ref, feature_ref, factor_ref, first_ref, out_ref, flag_ref, hot_ref, parts_ref, table_ref, image_ref, sum_ref, part_ref):
    image_ref[...] = jnp.zeros((2 * LANES, LANES), F32)
    feature_ref[...] = jnp.zeros(feature_ref.shape, F32)

    def take_row(q):
        turned = jnp.transpose(got_ref[pl.ds(q, OWNERS, stride=ROWS), :])
        for k in range(GROUPS):
            feature_ref[pl.ds(q * GROUPS + k, WIDTH, stride=SPAN), :] = turned[
                k * WIDTH : (k + 1) * WIDTH, :
            ]
        return turned

    turned = take_row(0)
    flag_ref[...] = jnp.broadcast_to(
        jnp.max(turned[COUNT_AT + 1 : COUNT_AT + 2, :], axis=1, keepdims=True), (8, LANES)
    )
    most = jnp.max(turned[COUNT_AT : COUNT_AT + 1, :])
    many = most > FEW
    blocks = jnp.where(many, SPAN // 8, FEW // 8)
    few_rows = -(-FEW // GROUPS)
    for q in range(1, few_rows):
        take_row(q)

    @pl.when(many)
    def _():
        for q in range(few_rows, ROWS):
            take_row(q)

    part_ref[...] = jnp.zeros((ENTRIES * 8, LANES), F32)

    def gather_terms(block, carry):
        hot_cameras(feature_ref, hot_ref, block)
        f = [features_of(feature_ref, at, block) for at in range(20)]
        for at, (j, k) in enumerate(block_pairs):
            part_ref[at * 8 : (at + 1) * 8, :] = f[j] * f[k] + f[9 + j] * f[9 + k]
        for j in range(9):
            part_ref[(45 + j) * 8 : (46 + j) * 8, :] = -(f[j] * f[18] + f[9 + j] * f[19])
        keep_parts(part_ref, feature_ref, parts_ref, block, ENTRIES)
        return carry

    lax.fori_loop(0, blocks, gather_terms, 0)
    camera_sums(parts_ref, hot_ref, part_ref, sum_ref, ENTRIES, many)
    matrix = {}
    for at, (j, k) in enumerate(block_pairs):
        entry = part_ref[at * 8 : (at + 1) * 8, :]
        matrix[k, j] = entry + 1.0 if j == k else entry
    side = [part_ref[(45 + j) * 8 : (46 + j) * 8, :] for j in range(9)]
    factor, roots = {}, []
    for j in range(9):
        pivot = matrix[j, j]
        for m in range(j):
            pivot = pivot - factor[j, m] * factor[j, m]
        roots.append(jnp.sqrt(pivot))
        for i in range(j + 1, 9):
            running = matrix[i, j]
            for m in range(j):
                running = running - factor[i, m] * factor[j, m]
            factor[i, j] = running / roots[j]
    for at, (j, k) in enumerate(block_pairs):
        factor_ref[at * 8 : (at + 1) * 8, :] = roots[j] if j == k else factor[k, j]
    first = solve(factor, roots, side)
    energy = side[0] * first[0]
    for j in range(1, 9):
        energy = energy + side[j] * first[j]
    for j in range(9):
        first_ref[j * 8 : (j + 1) * 8, :] = first[j]
    first_ref[72:80, :] = energy
    first_ref[80:88, :] = jnp.broadcast_to(jnp.max(turned[COUNT_AT : COUNT_AT + 1, :], axis=1, keepdims=True), (8, LANES))
    image_slots(first, feature_ref, table_ref, image_ref, blocks)
    turn_out(image_ref, out_ref)


def either_span(flag_ref, work):
    many = jnp.max(flag_ref[0:8, :]) > FEW
    pl.when(many)(lambda: work(SPAN))
    pl.when(jnp.logical_not(many))(lambda: work(FEW))


def pull_slots(got_ref, route_ref, point_ref, length_ref, state_ref, root_ref, value_ref, pulled_ref, curve_ref, span, back):
    images = []
    for i in range(2):
        images.append(turn_in(got_ref, i)[0:span, :])
    high, low = two_parts(jnp.concatenate(images, axis=0))
    parts = jnp.concatenate([high, low], axis=1)
    owners = iota((OWNERS, PT_DEV), 0)
    ranks = iota((span, PT_DEV), 0)
    for s in range(TRACK):
        hot = jnp.where(owners == route_ref[s : s + 1, :], 1.0, 0.0).astype(BF16)
        got = dot(parts, jnp.concatenate([hot, hot], axis=0))
        here = ranks == route_ref[TRACK + s : TRACK + s + 1, :]
        for i in range(2):
            value_ref[i * TRACK + s : i * TRACK + s + 1, :] = jnp.sum(
                jnp.where(here, got[i * span : (i + 1) * span, :], 0.0), axis=0, keepdims=True
            )
    curve = jnp.zeros((TRACK, LANES), F32)
    for chunk in range(PT_DEV // LANES):
        lanes = slice(chunk * LANES, (chunk + 1) * LANES)
        used = used_slots(length_ref, lanes)
        point = masked_points(point_ref, used, lanes)
        root = [root_ref[at * TRACK : (at + 1) * TRACK, lanes] for at in range(3)]
        image1 = value_ref[TRACK : 2 * TRACK, lanes] * root[2]
        image = [(value_ref[0:TRACK, lanes] - root[1] * image1) * root[0], image1]
        pulled = [over_tracks(point[0][a] * image[0] + point[1][a] * image[1]) for a in range(3)]
        inverse = [state_ref[at : at + 1, lanes] for at in range(6)]
        solved = times_inverse(inverse, pulled)
        for a in range(3):
            pulled_ref[a : a + 1, lanes] = pulled[a]
        result = [
            image[i] - (point[i][0] * solved[0] + point[i][1] * solved[1] + point[i][2] * solved[2])
            for i in range(2)
        ]
        if back:
            result0 = result[0] * root[0]
            value_ref[0:TRACK, lanes] = result0
            value_ref[TRACK : 2 * TRACK, lanes] = (result[1] - root[1] * result0) * root[2]
        else:
            curve = curve + image[0] * result[0] + image[1] * result[1]
    if not back:
        curve_ref[...] = curve


def first_point_kernel(got_ref, route_ref, point_ref, length_ref, state_ref, root_ref, flag_ref, pulled_ref, out_ref, value_ref, image_ref):
    image_ref[...] = jnp.zeros((2 * LANES, LANES), F32)
    owners = iota((OWNERS, PT_DEV), 0)

    def work(span):
        pull_slots(got_ref, route_ref, point_ref, length_ref, state_ref, root_ref, value_ref, pulled_ref, None, span, True)
        ranks = iota((span, PT_DEV), 0)
        sums = jnp.zeros((4 * span, OWNERS), F32)
        for s in range(TRACK):
            hot = jnp.where(owners == route_ref[s : s + 1, :], 1.0, 0.0).astype(BF16)
            here = ranks == route_ref[TRACK + s : TRACK + s + 1, :]
            spread = []
            for i in range(2):
                value = value_ref[i * TRACK + s : i * TRACK + s + 1, :]
                spread.append(jnp.where(here, value, 0.0))
            high, low = two_parts(jnp.concatenate(spread, axis=0))
            sums = sums + dot_lanes(jnp.concatenate([high, low], axis=0), hot)
        sums = sums[0 : 2 * span] + sums[2 * span :]
        for i in range(2):
            image_ref[i * LANES : i * LANES + span, :] = sums[i * span : (i + 1) * span, :]

    either_span(flag_ref, work)
    turn_out(image_ref, out_ref)


def second_point_kernel(got_ref, route_ref, point_ref, length_ref, state_ref, root_ref, flag_ref, pulled_ref, out_ref, scalar_ref, value_ref, curve_ref):
    def work(span):
        pull_slots(got_ref, route_ref, point_ref, length_ref, state_ref, root_ref, value_ref, pulled_ref, curve_ref, span, False)

    either_span(flag_ref, work)
    out_ref[...] = jnp.broadcast_to(total(curve_ref[...]), (OWNERS, LANES))
    scalar_ref[...] = jnp.broadcast_to(
        jnp.sum(got_ref[pl.ds(0, OWNERS, stride=2), :], axis=0, keepdims=True), (8, LANES)
    )


def second_camera_kernel(got_ref, feature_ref, factor_ref, first_ref, second_ref, out_ref, hot_ref, parts_ref, table_ref, image_ref, sum_ref, wide_ref):
    for i in range(2):
        image_ref[i * LANES : (i + 1) * LANES, :] = turn_in(got_ref, i)
    many = jnp.max(first_ref[80:88, :]) > FEW
    blocks = jnp.where(many, SPAN // 8, FEW // 8)
    wide_ref[...] = jnp.zeros((LANES, LANES), F32)

    def gather_terms(block, carry):
        hot_cameras(feature_ref, hot_ref, block)
        back = [
            image_ref[pl.ds(pl.multiple_of(i * LANES + block * 8, 8), 8), :] for i in range(2)
        ]
        for j in range(9):
            wide_ref[j * 8 : (j + 1) * 8, :] = (
                features_of(feature_ref, j, block) * back[0]
                + features_of(feature_ref, 9 + j, block) * back[1]
            )
        keep_parts(wide_ref, feature_ref, parts_ref, block, 16)
        return carry

    lax.fori_loop(0, blocks, gather_terms, 0)
    camera_sums(parts_ref, hot_ref, wide_ref, sum_ref, 16, many)
    first = [first_ref[j * 8 : (j + 1) * 8, :] for j in range(9)]
    image = [first[j] + wide_ref[j * 8 : (j + 1) * 8, :] for j in range(9)]
    factor, roots = {}, []
    for at, (j, k) in enumerate(block_pairs):
        entry = factor_ref[at * 8 : (at + 1) * 8, :]
        if j == k:
            roots.append(entry)
        else:
            factor[k, j] = entry
    second = solve(factor, roots, image)
    for j in range(9):
        second_ref[j * 8 : (j + 1) * 8, :] = second[j]

    def inner(left, right):
        value = left[0] * right[0]
        for j in range(1, 9):
            value = value + left[j] * right[j]
        return value

    image_slots(second, feature_ref, table_ref, image_ref, blocks)
    scalars = [first_ref[72:80, :], inner(first, image), inner(image, second), inner(second, second)]
    for at, value in enumerate(scalars):
        image_ref[SPAN + at : SPAN + at + 1, :] = jnp.broadcast_to(total(value), (1, LANES))
    turn_out(image_ref, out_ref)


def finish_kernel(curve_ref, scalar_ref, first_ref, second_ref, state_ref, first_pulled_ref, second_pulled_ref, camera_out, point_out, camera_ref, point_ref, camera_sem, point_sem):
    own = jnp.sum(curve_ref[...], axis=0, keepdims=True)[:, 0:1]
    energy, curvature, crossed, square = [
        scalar_ref[0:1, SPAN + at : SPAN + at + 1] for at in range(4)
    ]
    step_size = energy / curvature
    renewed = step_size * step_size * crossed - energy
    ratio = 1.0 + renewed / energy
    second_step = renewed / (
        ratio * ratio * curvature
        - 2.0 * step_size * ratio * crossed
        + step_size * step_size * (square + own)
    )
    first_weight = step_size + second_step * ratio
    second_weight = -second_step * step_size
    for c in range(3):
        camera_ref[:, c * LANES : (c + 1) * LANES] = (
            first_weight * first_ref[pl.ds(c, 9, stride=8), :]
            + second_weight * second_ref[pl.ds(c, 9, stride=8), :]
        )
    camera_copy = pltpu.make_async_copy(camera_ref, camera_out, camera_sem)
    camera_copy.start()
    left = [
        state_ref[6 + a : 7 + a, :]
        - first_weight * first_pulled_ref[a : a + 1, :]
        - second_weight * second_pulled_ref[a : a + 1, :]
        for a in range(3)
    ]
    moved = times_inverse([state_ref[at : at + 1, :] for at in range(6)], left)
    for a in range(3):
        point_ref[a : a + 1, :] = moved[a]
    point_copy = pltpu.make_async_copy(point_ref, point_out, point_sem)
    point_copy.start()
    camera_copy.wait()
    point_copy.wait()


def call(kernel, outs, scratch, operands, in_scalar=0):
    specs = [
        pl.BlockSpec(memory_space=pltpu.SMEM if at < in_scalar else pltpu.VMEM)
        for at in range(len(operands))
    ]
    return pl.pallas_call(
        kernel,
        out_shape=[jax.ShapeDtypeStruct(shape, dtype) for shape, dtype in outs],
        in_specs=specs,
        out_specs=[pl.BlockSpec(memory_space=pltpu.VMEM)] * len(outs),
        scratch_shapes=[pltpu.VMEM(shape, dtype) for shape, dtype in scratch],
        compiler_params=PARAMS,
    )(*operands)


def exchange(rows):
    blocks = rows.reshape(OWNERS, 1, -1)
    blocks = lax.all_to_all(blocks, ("row", "col"), split_axis=0, concat_axis=0, tiled=True)
    return blocks.reshape(rows.shape)


def by_slots(camera_jacobian, point_jacobian, residuals, observed_camera, track_length):
    lengths = track_length.reshape(1, PT_DEV)
    in_vmem = [pl.BlockSpec(memory_space=pltpu.VMEM)]
    held = [(18, TRACK, PT_DEV), (6, TRACK, PT_DEV), (2, TRACK, PT_DEV)]
    outs = [
        ((WIDTH * PT_DEV * TRACK // LANES, LANES), F32),
        ((BLOCKS, LANES), jnp.int32),
        ((2 * TRACK, PT_DEV), jnp.int32),
        ((16, PT_DEV), F32),
        ((3 * TRACK, PT_DEV), F32),
        ((OWNERS, LANES), F32),
    ]
    pay, code, route, state, root, flag = pl.pallas_call(
        prepare_kernel,
        out_shape=[jax.ShapeDtypeStruct(shape, dtype) for shape, dtype in outs],
        in_specs=[pl.BlockSpec(memory_space=pl.ANY)] * 3 + in_vmem * 2,
        out_specs=in_vmem * len(outs),
        scratch_shapes=[pltpu.VMEM(shape, F32) for shape in held]
        + [pltpu.SemaphoreType.DMA] * 3,
        compiler_params=PARAMS,
    )(camera_jacobian, point_jacobian, residuals, observed_camera, lengths)
    (sent,) = call(
        dispatch_kernel,
        [((OWNERS * ROWS, LANES), F32)],
        [((BLOCKS, LANES, 1, LANES), F32), ((GROUPS * OWNERS * ROWS + 8, 1, LANES), F32)],
        (code, pay, flag),
        in_scalar=1,
    )
    hot = ((LANES, SPAN * LANES), BF16)
    table = ((27 * 8, LANES), F32)
    image = ((2 * LANES, LANES), F32)
    pair = ((2 * OWNERS, LANES), F32)
    features, factor, first, out, overflow = call(
        first_camera_kernel,
        [((WIDTH * SPAN, LANES), F32), ((45 * 8, LANES), F32), ((88, LANES), F32), pair, ((8, LANES), F32)],
        [hot, ((6 * ENTRIES, SPAN * LANES), BF16), table, image, ((6 * ENTRIES, LANES), F32), ((ENTRIES * 8, LANES), F32)],
        (exchange(sent),),
    )
    first_pulled, out = call(
        first_point_kernel,
        [((8, PT_DEV), F32), pair],
        [((2 * TRACK, PT_DEV), F32), image],
        (exchange(out), route, point_jacobian, lengths, state, root, flag),
    )
    second, out = call(
        second_camera_kernel,
        [((72, LANES), F32), pair],
        [hot, ((96, SPAN * LANES), BF16), table, image, ((96, LANES), F32), ((LANES, LANES), F32)],
        (exchange(out), features, factor, first),
    )
    second_pulled, curve, scalars = call(
        second_point_kernel,
        [((8, PT_DEV), F32), ((OWNERS, LANES), F32), ((8, LANES), F32)],
        [((2 * TRACK, PT_DEV), F32), ((TRACK, LANES), F32)],
        (exchange(out), route, point_jacobian, lengths, state, root, flag),
    )
    return overflow[0, 0], (exchange(curve), scalars, first, second, state, first_pulled, second_pulled)


def finish(*operands):
    shapes = [(9, CAM_DEV), (3, PT_DEV)]
    return tuple(
        pl.pallas_call(
            finish_kernel,
            out_shape=[jax.ShapeDtypeStruct(shape, F32) for shape in shapes],
            in_specs=[pl.BlockSpec(memory_space=pltpu.VMEM)] * len(operands),
            out_specs=[pl.BlockSpec(memory_space=pltpu.HBM)] * 2,
            scratch_shapes=[pltpu.VMEM(shape, F32) for shape in shapes]
            + [pltpu.SemaphoreType.DMA] * 2,
            compiler_params=PARAMS,
        )(*operands)
    )


damping = 1.0


def inverse_small(matrix):
    entries = [[matrix[row_at, col_at] for col_at in range(3)] for row_at in range(3)]
    cofactor = [
        [
            entries[(row_at + 1) % 3][(col_at + 1) % 3]
            * entries[(row_at + 2) % 3][(col_at + 2) % 3]
            - entries[(row_at + 1) % 3][(col_at + 2) % 3]
            * entries[(row_at + 2) % 3][(col_at + 1) % 3]
            for col_at in range(3)
        ]
        for row_at in range(3)
    ]
    determinant = (
        entries[0][0] * cofactor[0][0]
        + entries[0][1] * cofactor[0][1]
        + entries[0][2] * cofactor[0][2]
    )
    return jnp.stack(
        [
            jnp.stack([cofactor[col_at][row_at] / determinant for col_at in range(3)])
            for row_at in range(3)
        ]
    )


def block_inverse(matrix):
    factor = {}
    for col_at in range(9):
        pivot_value = matrix[col_at, col_at]
        for middle in range(col_at):
            pivot_value = pivot_value - factor[col_at, middle] * factor[col_at, middle]
        diagonal_root = jnp.sqrt(pivot_value)
        factor[col_at, col_at] = diagonal_root
        for row_at in range(col_at + 1, 9):
            running = matrix[row_at, col_at]
            for middle in range(col_at):
                running = running - factor[row_at, middle] * factor[col_at, middle]
            factor[row_at, col_at] = running / diagonal_root
    factor_inverse = {}
    for row_at in range(9):
        factor_inverse[row_at, row_at] = 1.0 / factor[row_at, row_at]
        for col_at in range(row_at):
            running = factor[row_at, col_at] * factor_inverse[col_at, col_at]
            for middle in range(col_at + 1, row_at):
                running = running + factor[row_at, middle] * factor_inverse[middle, col_at]
            factor_inverse[row_at, col_at] = -running / factor[row_at, row_at]
    result_rows = []
    for row_at in range(9):
        entries = []
        for col_at in range(9):
            running = (
                factor_inverse[max(row_at, col_at), row_at]
                * factor_inverse[max(row_at, col_at), col_at]
            )
            for middle in range(max(row_at, col_at) + 1, 9):
                running = running + factor_inverse[middle, row_at] * factor_inverse[middle, col_at]
            entries.append(running)
        result_rows.append(jnp.stack(entries))
    return jnp.stack(result_rows)


def assemble(packed):
    positions = {}
    for index_at, pair in enumerate(block_pairs):
        positions[pair[0], pair[1]] = index_at
        positions[pair[1], pair[0]] = index_at
    return jnp.stack(
        [
            jnp.stack(
                [
                    packed[positions[row_at, col_at]] + (damping if row_at == col_at else 0.0)
                    for col_at in range(9)
                ]
            )
            for row_at in range(9)
        ]
    )


def apply_blocks(inverse_blocks, vector):
    return jnp.sum(inverse_blocks * vector[None], axis=1)


def slot_basics(camera_jacobian, point_jacobian, residuals, track_length):
    tracks = camera_jacobian.shape[1]
    in_track = (jnp.arange(tracks, dtype=jnp.int32)[:, None] < track_length[None, :]).astype(
        jnp.float32
    )
    camera_blocks = camera_jacobian.reshape(2, 9, tracks, -1) * in_track
    point_blocks = point_jacobian.reshape(2, 3, tracks, -1) * in_track
    errors = residuals * in_track
    coupling = jnp.sum(camera_blocks[:, :, None] * point_blocks[:, None], axis=0)
    point_system = jnp.sum(point_blocks[:, :, None] * point_blocks[:, None], axis=(0, 3))
    point_system = point_system + damping * jnp.eye(3, dtype=jnp.float32)[:, :, None]
    point_inverse = inverse_small(point_system)
    point_gradient = -jnp.sum(point_blocks * errors[:, None], axis=(0, 2))
    return (camera_blocks, errors, coupling, point_inverse, point_gradient)


def camera_terms(camera_blocks, errors, coupling, point_inverse, point_gradient):
    solved = jnp.sum(point_inverse * point_gradient[None], axis=1)
    scaled = coupling[:, 0][:, None] * point_inverse[0][None, :, None, :]
    for middle in range(1, 3):
        scaled = scaled + coupling[:, middle][:, None] * point_inverse[middle][None, :, None, :]
    packed = []
    for leading, trailing in block_pairs:
        packed.append(
            jnp.sum(camera_blocks[:, leading] * camera_blocks[:, trailing], axis=0)
            - jnp.sum(scaled[leading] * coupling[trailing], axis=0)
        )
    right_side = -jnp.sum(camera_blocks * errors[:, None], axis=0) - jnp.sum(
        coupling * solved[None, :, None], axis=1
    )
    return jnp.concatenate([jnp.stack(packed), right_side], axis=0)


def slot_product(camera_blocks, coupling, point_inverse, gathered):
    projected = jnp.sum(camera_blocks * gathered[None], axis=1)
    pulled = jnp.sum(coupling * gathered[:, None], axis=(0, 2))
    solved = jnp.sum(point_inverse * pulled[None], axis=1)
    return jnp.sum(camera_blocks * projected[:, None], axis=0) - jnp.sum(
        coupling * solved[None, :, None], axis=1
    )


def by_dense(camera_jacobian, point_jacobian, residuals, observed_camera, track_length):
    camera_blocks, errors, coupling, point_inverse, point_gradient = slot_basics(
        camera_jacobian, point_jacobian, residuals, track_length
    )
    tracks, points = observed_camera.shape
    rows, cols = lax.axis_size("row"), lax.axis_size("col")
    cameras = CAM_DEV * rows * cols
    flat_cameras = observed_camera.reshape(-1)

    def into_cameras(values):
        width = values.shape[0]
        by_camera = (
            jnp.zeros((cameras, width), jnp.float32).at[flat_cameras].add(jnp.transpose(values))
        )
        return jnp.transpose(by_camera)

    def pick_slots(whole):
        slot_rows = jnp.transpose(whole)[flat_cameras]
        return jnp.transpose(slot_rows).reshape(9, tracks, points)

    def spread_out(value):
        copies = jnp.broadcast_to(value[:, None], (9, OWNERS, CAM_DEV)).reshape(9, cameras)
        return lax.all_to_all(copies, ("row", "col"), split_axis=1, concat_axis=1, tiled=True)

    term_values = camera_terms(
        camera_blocks, errors, coupling, point_inverse, point_gradient
    ).reshape(54, -1)
    local_terms = into_cameras(term_values).reshape(54, rows * cols, CAM_DEV)
    own_terms = jnp.sum(
        lax.all_to_all(local_terms, ("row", "col"), split_axis=1, concat_axis=1, tiled=True), axis=1
    )
    inverse_blocks = block_inverse(assemble(own_terms[:45]))
    right_side = own_terms[45:]

    first = apply_blocks(inverse_blocks, right_side)
    first_slots = pick_slots(spread_out(first))
    first_pulled = jnp.sum(coupling * first_slots[:, None], axis=(0, 2))
    contrib = slot_product(camera_blocks, coupling, point_inverse, first_slots)
    local_image = into_cameras(contrib.reshape(9, -1)).reshape(9, OWNERS, CAM_DEV)
    gathered_image = lax.all_to_all(
        local_image, ("row", "col"), split_axis=1, concat_axis=1, tiled=True
    )
    first_image = damping * first + jnp.sum(gathered_image, axis=1)

    second = apply_blocks(inverse_blocks, first_image)
    second_slots = pick_slots(spread_out(second))
    second_pulled = jnp.sum(coupling * second_slots[:, None], axis=(0, 2))
    projected = jnp.sum(camera_blocks * second_slots[None], axis=1)
    solved = jnp.sum(point_inverse * second_pulled[None], axis=1)
    own_sums = jnp.stack(
        [
            jnp.sum(right_side * first),
            jnp.sum(first * first_image),
            jnp.sum(first_image * second),
            jnp.sum(second * second)
            + jnp.sum(projected * projected)
            - jnp.sum(second_pulled * solved),
        ]
    )
    spread = jnp.broadcast_to(own_sums[None], (OWNERS, 4))
    energy, curvature, crossed, second_curvature = jnp.sum(exchange(spread), axis=0)
    step_size = energy / curvature
    renewed = step_size * step_size * crossed - energy
    ratio = 1.0 + renewed / energy
    second_step = renewed / (
        ratio * ratio * curvature
        - 2.0 * step_size * ratio * crossed
        + step_size * step_size * second_curvature
    )
    first_weight = step_size + second_step * ratio
    second_weight = -second_step * step_size
    camera_move = first_weight * first + second_weight * second
    pulled = first_weight * first_pulled + second_weight * second_pulled
    point_move = jnp.sum(point_inverse * (point_gradient - pulled)[None], axis=1)
    return (camera_move, point_move)


def on_device(camera_jacobian, point_jacobian, residuals, observed_camera, track_length):
    operands = (camera_jacobian, point_jacobian, residuals, observed_camera, track_length)
    overflow, kept = by_slots(*operands)
    return lax.cond(
        overflow > CAP,
        lambda given, unused: by_dense(*given),
        lambda unused, found: finish(*found),
        operands,
        kept,
    )


def solution(mesh):
    in_specs = (
        P(None, None, ("row", "col")),
        P(None, None, ("row", "col")),
        P(None, None, ("row", "col")),
        P(None, ("row", "col")),
        P(("row", "col")),
    )
    out_specs = (P(None, ("row", "col")), P(None, ("row", "col")))
    return jax.shard_map(
        on_device, mesh=mesh, in_specs=in_specs, out_specs=out_specs, check_vma=False
    )
```

```python
import jax
import jax.numpy as jnp
from jax import lax
from jax.experimental import pallas as pl
from jax.experimental.pallas import tpu as pltpu
from jax.sharding import PartitionSpec as P

CAM_DEV = 384
TRACK = 8
PT_DEV = 1024
OWNERS = 128
LANES = 128
WIDTH = 21
GROUPS = 6
ROWS = 13
CAP = GROUPS * ROWS
SPAN = 80
FEW = 64
CAMERA_AT = 20
ENTRIES = 56
COUNT_AT = GROUPS * WIDTH
BLOCKS = TRACK * PT_DEV // LANES

F32 = jnp.float32
BF16 = jnp.bfloat16
PARAMS = pltpu.CompilerParams(vmem_limit_bytes=48 * 2**20)
block_pairs = [(leading, trailing) for leading in range(9) for trailing in range(leading, 9)]


def iota(shape, axis):
    return lax.broadcasted_iota(jnp.int32, shape, axis)


def two_parts(value):
    high = value.astype(BF16)
    low = (value - high.astype(F32)).astype(BF16)
    return high, low


def dot(left, right):
    return jnp.dot(left, right, preferred_element_type=F32)


def dot_lanes(left, right):
    return lax.dot_general(left, right, (((1,), (1,)), ((), ())), preferred_element_type=F32)


def total(value):
    return jnp.sum(jnp.sum(value, axis=0, keepdims=True), axis=1, keepdims=True)


def over_tracks(value):
    return jnp.sum(value, axis=0, keepdims=True)


def used_slots(length_ref, lanes):
    return iota((TRACK, LANES), 0) < length_ref[:, lanes]


def masked_points(point_ref, used, lanes):
    return [
        [jnp.where(used, point_ref[3 * i + a, :, lanes], 0.0) for a in range(3)] for i in range(2)
    ]


def times_inverse(inverse, vector):
    v00, v01, v02, v11, v12, v22 = inverse
    x, y, z = vector
    return [v00 * x + v01 * y + v02 * z, v01 * x + v11 * y + v12 * z, v02 * x + v12 * y + v22 * z]


def owner_of(camera):
    return ((camera >> 7) * 171) >> 9


def prepare_kernel(camera_in, point_in, error_in, index_ref, length_ref, pay_ref, code_ref, route_ref, state_ref, root_ref, flag_ref, owned_ref, camera_ref, point_ref, error_ref, camera_sem, point_sem, error_sem):
    copies = [
        pltpu.make_async_copy(camera_in, camera_ref, camera_sem),
        pltpu.make_async_copy(point_in, point_ref, point_sem),
        pltpu.make_async_copy(error_in, error_ref, error_sem),
    ]
    for copy in copies:
        copy.start()
    used = iota((TRACK, PT_DEV), 0) < length_ref[...]
    route_ref[0:TRACK, :] = jnp.where(used, owner_of(index_ref[...]), OWNERS)

    step = 256
    upto = jnp.where(iota((step, step), 0) <= iota((step, step), 1), 1.0, 0.0).astype(BF16)
    before = jnp.zeros((OWNERS, step), F32)
    names = iota((OWNERS, step), 0)
    for s in range(TRACK):
        for chunk in range(PT_DEV // step):
            lanes = slice(chunk * step, (chunk + 1) * step)
            chosen = names == route_ref[s : s + 1, lanes]
            hot = jnp.where(chosen, 1.0, 0.0).astype(BF16)
            owned_ref[s, :, lanes] = hot
            counts = dot(hot, upto)
            rank = jnp.sum(jnp.where(chosen, counts + before, 0.0), axis=0, keepdims=True) - 1.0
            before = before + jnp.broadcast_to(counts[:, step - 1 : step], (OWNERS, step))
            route_ref[TRACK + s : TRACK + s + 1, lanes] = rank.astype(jnp.int32)

    owner = route_ref[0:TRACK, :]
    rank = route_ref[TRACK : 2 * TRACK, :]
    fits = (owner < OWNERS) & (rank < CAP)
    row_at = (rank * 171) >> 10
    place = (rank - row_at * GROUPS) * (OWNERS * ROWS) + owner * ROWS + row_at
    code = jnp.where(fits, place, GROUPS * OWNERS * ROWS)
    for chunk in range(PT_DEV // LANES):
        code_ref[chunk * TRACK : (chunk + 1) * TRACK, :] = code[:, chunk * LANES : (chunk + 1) * LANES]
    most = jnp.max(jnp.max(before, axis=0, keepdims=True), axis=1, keepdims=True)
    lane = iota((OWNERS, LANES), 1)
    flag_ref[...] = jnp.where(lane > COUNT_AT, most, before[:, 0:LANES])
    for copy in copies:
        copy.wait()
    for chunk in range(PT_DEV // LANES):
        lanes = slice(chunk * LANES, (chunk + 1) * LANES)
        used = used_slots(length_ref, lanes)
        point = masked_points(point_ref, used, lanes)
        error = [jnp.where(used, error_ref[i, :, lanes], 0.0) for i in range(2)]

        def pair(a, b):
            return over_tracks(point[0][a] * point[0][b] + point[1][a] * point[1][b])

        s00, s01, s02 = 1.0 + pair(0, 0), pair(0, 1), pair(0, 2)
        s11, s12, s22 = 1.0 + pair(1, 1), pair(1, 2), 1.0 + pair(2, 2)
        c00 = s11 * s22 - s12 * s12
        c01 = s12 * s02 - s01 * s22
        c02 = s01 * s12 - s11 * s02
        c11 = s22 * s00 - s02 * s02
        c12 = s02 * s01 - s12 * s00
        c22 = s00 * s11 - s01 * s01
        determinant = s00 * c00 + s01 * c01 + s02 * c02
        inverse = [c / determinant for c in (c00, c01, c02, c11, c12, c22)]
        gradient = [
            -over_tracks(point[0][a] * error[0] + point[1][a] * error[1]) for a in range(3)
        ]
        for at, value in enumerate(inverse + gradient):
            state_ref[at : at + 1, lanes] = value
        solved = times_inverse(inverse, gradient)
        u0 = times_inverse(inverse, point[0])
        u1 = times_inverse(inverse, point[1])

        def along(left, right):
            return left[0] * right[0] + left[1] * right[1] + left[2] * right[2]

        camera = index_ref[:, lanes]
        owner = owner_of(camera)
        local = camera - owner * CAM_DEV
        b01 = -along(u0, point[1])
        root0 = jnp.sqrt(1.0 - along(u0, point[0]))
        root1 = b01 / root0
        root2 = jnp.sqrt(1.0 - along(u1, point[1]) - root1 * root1)
        inverse0, inverse2 = 1.0 / root0, 1.0 / root2
        side0 = (error[0] + along(solved, point[0])) * inverse0
        side1 = (error[1] + along(solved, point[1]) - root1 * side0) * inverse2
        values = [root0 * camera_ref[j, :, lanes] + root1 * camera_ref[9 + j, :, lanes] for j in range(9)]
        values += [root2 * camera_ref[9 + j, :, lanes] for j in range(9)]
        values += [side0, side1, (local + 1).astype(F32)]
        for at, value in enumerate((inverse0, root1, inverse2)):
            root_ref[at * TRACK : (at + 1) * TRACK, lanes] = value
        for f in range(WIDTH):
            at = (chunk * WIDTH + f) * TRACK
            pay_ref[at : at + TRACK, :] = values[f]


def dispatch_kernel(code_in, pay_ref, flag_ref, out_ref, code_ref, slot_ref, block_ref, code_sem):
    copy = pltpu.make_async_copy(code_in, code_ref, code_sem)
    copy.start()
    rows = OWNERS * ROWS
    zeros = jnp.zeros((8, LANES), F32)
    slots_ref = slot_ref.reshape(BLOCKS * LANES, LANES)
    blocks_ref = block_ref.reshape(GROUPS * rows + 8, LANES)

    share = -(-GROUPS * rows // (BLOCKS * 8)) * 8
    within = iota((LANES, LANES), 1) % WIDTH
    for first in range(0, BLOCKS, GROUPS):
        blocks = []
        for block in range(first, first + GROUPS):
            chunk, s = divmod(block, TRACK)
            if block < BLOCKS:
                blocks.append(pay_ref[pl.ds(chunk * WIDTH * TRACK + s, WIDTH, stride=TRACK), :])
            else:
                blocks.append(jnp.zeros((WIDTH, LANES), F32))
        turned = jnp.transpose(jnp.concatenate(blocks + [zeros[0 : LANES - COUNT_AT]], axis=0))
        for block in range(first, min(first + GROUPS, BLOCKS)):
            slots_ref[block * LANES : (block + 1) * LANES, :] = jnp.take_along_axis(
                turned, within + (block - first) * WIDTH, axis=1, mode="promise_in_bounds"
            )
            start = min(block * share, GROUPS * rows)
            count = min(share, GROUPS * rows - start)
            if count:
                blocks_ref[start : start + count, :] = jnp.zeros((count, LANES), F32)

    copy.wait()

    def place(block, carry):
        def load(start):
            columns = range(start, min(start + 16, LANES))
            return [(code_ref[block, j], slot_ref[block, j]) for j in columns]

        ready = load(0)
        for start in range(16, LANES + 16, 16):
            coming = load(start)
            for code, slot in ready:
                block_ref[code] = slot
            ready = coming
        return carry

    lax.fori_loop(0, BLOCKS, place, 0)
    group = iota((8, LANES), 1) // WIDTH

    def merge(at, carry):
        for j in range(8):
            start = pl.multiple_of(at * 64 + j * 8, 8)
            value = zeros
            for k in range(GROUPS):
                value = jnp.where(group == k, blocks_ref[pl.ds(k * rows + start, 8), :], value)
            out_ref[pl.ds(start, 8), :] = value
        return carry

    lax.fori_loop(0, rows // 64, merge, 0)
    lane = iota((OWNERS, LANES), 1)
    leading = pl.ds(0, OWNERS, stride=ROWS)
    out_ref[leading, :] = jnp.where(lane >= COUNT_AT, flag_ref[...], out_ref[leading, :])


def solve(factor, roots, vector):
    forward = []
    for i in range(9):
        value = vector[i]
        for j in range(i):
            value = value - factor[i, j] * forward[j]
        forward.append(value / roots[i])
    result = [None] * 9
    for i in reversed(range(9)):
        value = forward[i]
        for j in range(i + 1, 9):
            value = value - factor[j, i] * result[j]
        result[i] = value / roots[i]
    return result


def hot_cameras(feature_ref, hot_ref, block):
    names = iota((LANES, LANES), 0)
    for r in range(8):
        camera = feature_ref[pl.ds(CAMERA_AT * SPAN + block * 8 + r, 1), :].astype(jnp.int32) - 1
        hot = jnp.where(names == (camera & (LANES - 1)), 1.0, 0.0).astype(BF16)
        hot_ref[:, block * PT_DEV + r * LANES : block * PT_DEV + (r + 1) * LANES] = hot


def features_of(feature_ref, f, block):
    start = f * SPAN + block * 8
    return feature_ref[pl.ds(start if isinstance(block, int) else pl.multiple_of(start, 8), 8), :]


def image_slots(vector, feature_ref, table_ref, image_ref, blocks):
    for j in range(9):
        for c in range(3):
            at = (3 * j + c) * 8
            table_ref[at : at + 8, :] = jnp.broadcast_to(vector[j][c : c + 1, :], (8, LANES))

    def one(block, carry):
        camera = features_of(feature_ref, CAMERA_AT, block).astype(jnp.int32) - 1
        third = camera >> 7
        lane = camera & (LANES - 1)
        images = [jnp.zeros((8, LANES), F32)] * 2
        for j in range(9):
            found = [
                jnp.take_along_axis(
                    table_ref[(3 * j + c) * 8 : (3 * j + c + 1) * 8, :],
                    lane,
                    axis=1,
                    mode="promise_in_bounds",
                )
                for c in range(3)
            ]
            value = jnp.where(third == 1, found[1], jnp.where(third == 2, found[2], found[0]))
            for i in range(2):
                images[i] = images[i] + features_of(feature_ref, 9 * i + j, block) * value
        for i in range(2):
            image_ref[pl.ds(pl.multiple_of(i * LANES + block * 8, 8), 8), :] = images[i]
        return carry

    lax.fori_loop(0, blocks, one, 0)


def keep_parts(part_ref, feature_ref, parts_ref, block, count):
    for r in range(8):
        lanes = slice(block * PT_DEV + r * LANES, block * PT_DEV + (r + 1) * LANES)
        camera = feature_ref[pl.ds(CAMERA_AT * SPAN + block * 8 + r, 1), :].astype(jnp.int32) - 1
        value = part_ref[pl.ds(r, count, stride=8), :]
        high = value.astype(BF16).astype(F32)
        both = jnp.concatenate([high, value - high], axis=0).astype(BF16)
        third = jnp.broadcast_to(camera >> 7, (16, LANES))
        for c in range(3):
            inside = jnp.where(third == c, 1.0, 0.0).astype(BF16)
            inside = jnp.concatenate([inside] * (count // 8), axis=0)
            parts_ref[2 * c * count : 2 * (c + 1) * count, lanes] = both * inside


def camera_sums(terms, parts_ref, hot_ref, part_ref, sum_ref, count, many):
    def block_sums(block):
        terms(block)
        lanes = slice(block * PT_DEV, (block + 1) * PT_DEV)
        return dot_lanes(parts_ref[:, lanes], hot_ref[:, lanes])

    sums = block_sums(0)
    for block in range(1, FEW // 8):
        sums = sums + block_sums(block)
    sum_ref[...] = sums

    @pl.when(many)
    def _():
        for block in range(FEW // 8, SPAN // 8):
            sum_ref[...] += block_sums(block)

    part_ref[...] = jnp.zeros(part_ref.shape, F32)
    for c in range(3):
        at = 2 * c * count
        part_ref[pl.ds(c, count, stride=8), :] = (
            sum_ref[at : at + count, :] + sum_ref[at + count : at + 2 * count, :]
        )


def turn_in(got_ref, i):
    return jnp.transpose(got_ref[pl.ds(i, OWNERS, stride=2), :])


def turn_out(image_ref, out_ref):
    for i in range(2):
        out_ref[pl.ds(i, OWNERS, stride=2), :] = jnp.transpose(
            image_ref[i * LANES : (i + 1) * LANES, :]
        )


def first_camera_kernel(got_ref, feature_ref, factor_ref, first_ref, out_ref, flag_ref, hot_ref, parts_ref, table_ref, image_ref, sum_ref, part_ref):
    image_ref[...] = jnp.zeros((2 * LANES, LANES), F32)
    feature_ref[...] = jnp.zeros(feature_ref.shape, F32)

    def take_row(q):
        turned = jnp.transpose(got_ref[pl.ds(q, OWNERS, stride=ROWS), :])
        for k in range(GROUPS):
            feature_ref[pl.ds(q * GROUPS + k, WIDTH, stride=SPAN), :] = turned[
                k * WIDTH : (k + 1) * WIDTH, :
            ]
        return turned

    turned = take_row(0)
    worst = jnp.max(turned[COUNT_AT + 1 : COUNT_AT + 2, :])
    flag_ref[0, 0] = jnp.where(worst > CAP, 1, 0)
    most = jnp.max(turned[COUNT_AT : COUNT_AT + 1, :])
    many = most > FEW
    blocks = jnp.where(many, SPAN // 8, FEW // 8)
    few_rows = -(-FEW // GROUPS)
    for q in range(1, few_rows):
        take_row(q)

    @pl.when(many)
    def _():
        for q in range(few_rows, ROWS):
            take_row(q)

    part_ref[...] = jnp.zeros((ENTRIES * 8, LANES), F32)

    def gather_terms(block):
        hot_cameras(feature_ref, hot_ref, block)
        f = [features_of(feature_ref, at, block) for at in range(20)]
        for at, (j, k) in enumerate(block_pairs):
            part_ref[at * 8 : (at + 1) * 8, :] = f[j] * f[k] + f[9 + j] * f[9 + k]
        for j in range(9):
            part_ref[(45 + j) * 8 : (46 + j) * 8, :] = -(f[j] * f[18] + f[9 + j] * f[19])
        keep_parts(part_ref, feature_ref, parts_ref, block, ENTRIES)

    camera_sums(gather_terms, parts_ref, hot_ref, part_ref, sum_ref, ENTRIES, many)
    matrix = {}
    for at, (j, k) in enumerate(block_pairs):
        entry = part_ref[at * 8 : (at + 1) * 8, :]
        matrix[k, j] = entry + 1.0 if j == k else entry
    side = [part_ref[(45 + j) * 8 : (46 + j) * 8, :] for j in range(9)]
    factor, roots = {}, []
    for j in range(9):
        pivot = matrix[j, j]
        for m in range(j):
            pivot = pivot - factor[j, m] * factor[j, m]
        roots.append(jnp.sqrt(pivot))
        for i in range(j + 1, 9):
            running = matrix[i, j]
            for m in range(j):
                running = running - factor[i, m] * factor[j, m]
            factor[i, j] = running / roots[j]
    for at, (j, k) in enumerate(block_pairs):
        factor_ref[at * 8 : (at + 1) * 8, :] = roots[j] if j == k else factor[k, j]
    first = solve(factor, roots, side)
    energy = side[0] * first[0]
    for j in range(1, 9):
        energy = energy + side[j] * first[j]
    for j in range(9):
        first_ref[j * 8 : (j + 1) * 8, :] = first[j]
    first_ref[72:80, :] = energy
    first_ref[80:88, :] = jnp.broadcast_to(jnp.max(turned[COUNT_AT : COUNT_AT + 1, :], axis=1, keepdims=True), (8, LANES))
    image_slots(first, feature_ref, table_ref, image_ref, blocks)
    turn_out(image_ref, out_ref)


def either_span(flag_ref, work):
    many = jnp.max(flag_ref[0:8, :]) > FEW
    pl.when(many)(lambda: work(SPAN))
    pl.when(jnp.logical_not(many))(lambda: work(FEW))


def pull_slots(got_ref, route_ref, point_ref, length_ref, state_ref, root_ref, owned_ref, value_ref, pulled_ref, curve_ref, span, back):
    images = []
    for i in range(2):
        images.append(turn_in(got_ref, i)[0:span, :])
    high, low = two_parts(jnp.concatenate(images, axis=0))
    parts = jnp.concatenate([high, low], axis=1)
    ranks = iota((span, PT_DEV), 0)
    for s in range(TRACK):
        hot = owned_ref[s]
        got = dot(parts, jnp.concatenate([hot, hot], axis=0))
        here = ranks == route_ref[TRACK + s : TRACK + s + 1, :]
        for i in range(2):
            value_ref[i * TRACK + s : i * TRACK + s + 1, :] = jnp.sum(
                jnp.where(here, got[i * span : (i + 1) * span, :], 0.0), axis=0, keepdims=True
            )
    curve = jnp.zeros((TRACK, LANES), F32)
    for chunk in range(PT_DEV // LANES):
        lanes = slice(chunk * LANES, (chunk + 1) * LANES)
        used = used_slots(length_ref, lanes)
        point = masked_points(point_ref, used, lanes)
        root = [root_ref[at * TRACK : (at + 1) * TRACK, lanes] for at in range(3)]
        image1 = value_ref[TRACK : 2 * TRACK, lanes] * root[2]
        image = [(value_ref[0:TRACK, lanes] - root[1] * image1) * root[0], image1]
        pulled = [over_tracks(point[0][a] * image[0] + point[1][a] * image[1]) for a in range(3)]
        inverse = [state_ref[at : at + 1, lanes] for at in range(6)]
        solved = times_inverse(inverse, pulled)
        for a in range(3):
            pulled_ref[a : a + 1, lanes] = pulled[a]
        result = [
            image[i] - (point[i][0] * solved[0] + point[i][1] * solved[1] + point[i][2] * solved[2])
            for i in range(2)
        ]
        if back:
            result0 = result[0] * root[0]
            value_ref[0:TRACK, lanes] = result0
            value_ref[TRACK : 2 * TRACK, lanes] = (result[1] - root[1] * result0) * root[2]
        else:
            curve = curve + image[0] * result[0] + image[1] * result[1]
    if not back:
        curve_ref[...] = curve


def first_point_kernel(got_ref, route_ref, point_ref, length_ref, state_ref, root_ref, flag_ref, owned_ref, pulled_ref, out_ref, value_ref, image_ref):
    image_ref[...] = jnp.zeros((2 * LANES, LANES), F32)

    def work(span):
        pull_slots(got_ref, route_ref, point_ref, length_ref, state_ref, root_ref, owned_ref, value_ref, pulled_ref, None, span, True)
        ranks = iota((span, PT_DEV), 0)
        sums = jnp.zeros((4 * span, OWNERS), F32)
        for s in range(TRACK):
            here = ranks == route_ref[TRACK + s : TRACK + s + 1, :]
            spread = []
            for i in range(2):
                value = value_ref[i * TRACK + s : i * TRACK + s + 1, :]
                spread.append(jnp.where(here, value, 0.0))
            high, low = two_parts(jnp.concatenate(spread, axis=0))
            sums = sums + dot_lanes(jnp.concatenate([high, low], axis=0), owned_ref[s])
        sums = sums[0 : 2 * span] + sums[2 * span :]
        for i in range(2):
            image_ref[i * LANES : i * LANES + span, :] = sums[i * span : (i + 1) * span, :]

    either_span(flag_ref, work)
    turn_out(image_ref, out_ref)


def second_point_kernel(got_ref, route_ref, point_ref, length_ref, state_ref, root_ref, flag_ref, owned_ref, pulled_ref, out_ref, scalar_ref, value_ref, curve_ref):
    def work(span):
        pull_slots(got_ref, route_ref, point_ref, length_ref, state_ref, root_ref, owned_ref, value_ref, pulled_ref, curve_ref, span, False)

    either_span(flag_ref, work)
    out_ref[...] = jnp.broadcast_to(total(curve_ref[...]), (OWNERS, LANES))
    scalar_ref[...] = jnp.broadcast_to(
        jnp.sum(got_ref[pl.ds(0, OWNERS, stride=2), :], axis=0, keepdims=True), (8, LANES)
    )


def second_camera_kernel(got_ref, feature_ref, factor_ref, first_ref, second_ref, out_ref, hot_ref, parts_ref, table_ref, image_ref, sum_ref, wide_ref):
    for i in range(2):
        image_ref[i * LANES : (i + 1) * LANES, :] = turn_in(got_ref, i)
    many = jnp.max(first_ref[80:88, :]) > FEW
    blocks = jnp.where(many, SPAN // 8, FEW // 8)
    wide_ref[...] = jnp.zeros((LANES, LANES), F32)

    def gather_terms(block):
        hot_cameras(feature_ref, hot_ref, block)
        back = [
            image_ref[i * LANES + block * 8 : i * LANES + (block + 1) * 8, :] for i in range(2)
        ]
        for j in range(9):
            wide_ref[j * 8 : (j + 1) * 8, :] = (
                features_of(feature_ref, j, block) * back[0]
                + features_of(feature_ref, 9 + j, block) * back[1]
            )
        keep_parts(wide_ref, feature_ref, parts_ref, block, 16)

    camera_sums(gather_terms, parts_ref, hot_ref, wide_ref, sum_ref, 16, many)
    first = [first_ref[j * 8 : (j + 1) * 8, :] for j in range(9)]
    image = [first[j] + wide_ref[j * 8 : (j + 1) * 8, :] for j in range(9)]
    factor, roots = {}, []
    for at, (j, k) in enumerate(block_pairs):
        entry = factor_ref[at * 8 : (at + 1) * 8, :]
        if j == k:
            roots.append(entry)
        else:
            factor[k, j] = entry
    second = solve(factor, roots, image)
    for j in range(9):
        second_ref[j * 8 : (j + 1) * 8, :] = second[j]

    def inner(left, right):
        value = left[0] * right[0]
        for j in range(1, 9):
            value = value + left[j] * right[j]
        return value

    image_slots(second, feature_ref, table_ref, image_ref, blocks)
    scalars = [first_ref[72:80, :], inner(first, image), inner(image, second), inner(second, second)]
    for at, value in enumerate(scalars):
        image_ref[SPAN + at : SPAN + at + 1, :] = jnp.broadcast_to(total(value), (1, LANES))
    turn_out(image_ref, out_ref)


def finish_kernel(curve_ref, scalar_ref, first_ref, second_ref, state_ref, first_pulled_ref, second_pulled_ref, camera_out, point_out, camera_ref, point_ref, camera_sem, point_sem):
    own = jnp.sum(curve_ref[...], axis=0, keepdims=True)[:, 0:1]
    energy, curvature, crossed, square = [
        scalar_ref[0:1, SPAN + at : SPAN + at + 1] for at in range(4)
    ]
    step_size = energy / curvature
    renewed = step_size * step_size * crossed - energy
    ratio = 1.0 + renewed / energy
    second_step = renewed / (
        ratio * ratio * curvature
        - 2.0 * step_size * ratio * crossed
        + step_size * step_size * (square + own)
    )
    first_weight = step_size + second_step * ratio
    second_weight = -second_step * step_size
    for c in range(3):
        camera_ref[:, c * LANES : (c + 1) * LANES] = (
            first_weight * first_ref[pl.ds(c, 9, stride=8), :]
            + second_weight * second_ref[pl.ds(c, 9, stride=8), :]
        )
    camera_copy = pltpu.make_async_copy(camera_ref, camera_out, camera_sem)
    camera_copy.start()
    left = [
        state_ref[6 + a : 7 + a, :]
        - first_weight * first_pulled_ref[a : a + 1, :]
        - second_weight * second_pulled_ref[a : a + 1, :]
        for a in range(3)
    ]
    moved = times_inverse([state_ref[at : at + 1, :] for at in range(6)], left)
    for a in range(3):
        point_ref[a : a + 1, :] = moved[a]
    point_copy = pltpu.make_async_copy(point_ref, point_out, point_sem)
    point_copy.start()
    camera_copy.wait()
    point_copy.wait()


def call(kernel, outs, scratch, operands, in_scalar=0):
    specs = [
        pl.BlockSpec(memory_space=pltpu.SMEM if at < in_scalar else pltpu.VMEM)
        for at in range(len(operands))
    ]
    return pl.pallas_call(
        kernel,
        out_shape=[jax.ShapeDtypeStruct(shape, dtype) for shape, dtype in outs],
        in_specs=specs,
        out_specs=[
            pl.BlockSpec(memory_space=pltpu.SMEM if shape == (1, 1) else pltpu.VMEM)
            for shape, unused in outs
        ],
        scratch_shapes=[pltpu.VMEM(shape, dtype) for shape, dtype in scratch],
        compiler_params=PARAMS,
    )(*operands)


def exchange(rows):
    blocks = rows.reshape(OWNERS, 1, -1)
    blocks = lax.all_to_all(blocks, ("row", "col"), split_axis=0, concat_axis=0, tiled=True)
    return blocks.reshape(rows.shape)


def by_slots(camera_jacobian, point_jacobian, residuals, observed_camera, track_length):
    lengths = track_length.reshape(1, PT_DEV)
    in_vmem = [pl.BlockSpec(memory_space=pltpu.VMEM)]
    held = [(18, TRACK, PT_DEV), (6, TRACK, PT_DEV), (2, TRACK, PT_DEV)]
    outs = [
        ((WIDTH * PT_DEV * TRACK // LANES, LANES), F32),
        ((BLOCKS, LANES), jnp.int32),
        ((2 * TRACK, PT_DEV), jnp.int32),
        ((16, PT_DEV), F32),
        ((3 * TRACK, PT_DEV), F32),
        ((OWNERS, LANES), F32),
        ((TRACK, OWNERS, PT_DEV), BF16),
    ]
    pay, code, route, state, root, flag, owned = pl.pallas_call(
        prepare_kernel,
        out_shape=[jax.ShapeDtypeStruct(shape, dtype) for shape, dtype in outs],
        in_specs=[pl.BlockSpec(memory_space=pl.ANY)] * 3 + in_vmem * 2,
        out_specs=in_vmem * len(outs),
        scratch_shapes=[pltpu.VMEM(shape, F32) for shape in held]
        + [pltpu.SemaphoreType.DMA] * 3,
        compiler_params=PARAMS,
    )(camera_jacobian, point_jacobian, residuals, observed_camera, lengths)
    sent = pl.pallas_call(
        dispatch_kernel,
        out_shape=jax.ShapeDtypeStruct((OWNERS * ROWS, LANES), F32),
        in_specs=in_vmem * 3,
        out_specs=in_vmem[0],
        scratch_shapes=[
            pltpu.SMEM((BLOCKS, LANES), jnp.int32),
            pltpu.VMEM((BLOCKS, LANES, 1, LANES), F32),
            pltpu.VMEM((GROUPS * OWNERS * ROWS + 8, 1, LANES), F32),
            pltpu.SemaphoreType.DMA,
        ],
        compiler_params=PARAMS,
    )(code, pay, flag)
    hot = ((LANES, SPAN * LANES), BF16)
    table = ((27 * 8, LANES), F32)
    image = ((2 * LANES, LANES), F32)
    pair = ((2 * OWNERS, LANES), F32)
    features, factor, first, out, overflow = call(
        first_camera_kernel,
        [((WIDTH * SPAN, LANES), F32), ((45 * 8, LANES), F32), ((88, LANES), F32), pair, ((1, 1), jnp.int32)],
        [hot, ((6 * ENTRIES, SPAN * LANES), BF16), table, image, ((6 * ENTRIES, LANES), F32), ((ENTRIES * 8, LANES), F32)],
        (exchange(sent),),
    )
    first_pulled, out = call(
        first_point_kernel,
        [((8, PT_DEV), F32), pair],
        [((2 * TRACK, PT_DEV), F32), image],
        (exchange(out), route, point_jacobian, lengths, state, root, flag, owned),
    )
    second, out = call(
        second_camera_kernel,
        [((72, LANES), F32), pair],
        [hot, ((96, SPAN * LANES), BF16), table, image, ((96, LANES), F32), ((LANES, LANES), F32)],
        (exchange(out), features, factor, first),
    )
    second_pulled, curve, scalars = call(
        second_point_kernel,
        [((8, PT_DEV), F32), ((OWNERS, LANES), F32), ((8, LANES), F32)],
        [((2 * TRACK, PT_DEV), F32), ((TRACK, LANES), F32)],
        (exchange(out), route, point_jacobian, lengths, state, root, flag, owned),
    )
    return overflow[0, 0], (exchange(curve), scalars, first, second, state, first_pulled, second_pulled)


def finish(*operands):
    shapes = [(9, CAM_DEV), (3, PT_DEV)]
    return tuple(
        pl.pallas_call(
            finish_kernel,
            out_shape=[jax.ShapeDtypeStruct(shape, F32) for shape in shapes],
            in_specs=[pl.BlockSpec(memory_space=pltpu.VMEM)] * len(operands),
            out_specs=[pl.BlockSpec(memory_space=pltpu.HBM)] * 2,
            scratch_shapes=[pltpu.VMEM(shape, F32) for shape in shapes]
            + [pltpu.SemaphoreType.DMA] * 2,
            compiler_params=PARAMS,
        )(*operands)
    )


damping = 1.0


def inverse_small(matrix):
    entries = [[matrix[row_at, col_at] for col_at in range(3)] for row_at in range(3)]
    cofactor = [
        [
            entries[(row_at + 1) % 3][(col_at + 1) % 3]
            * entries[(row_at + 2) % 3][(col_at + 2) % 3]
            - entries[(row_at + 1) % 3][(col_at + 2) % 3]
            * entries[(row_at + 2) % 3][(col_at + 1) % 3]
            for col_at in range(3)
        ]
        for row_at in range(3)
    ]
    determinant = (
        entries[0][0] * cofactor[0][0]
        + entries[0][1] * cofactor[0][1]
        + entries[0][2] * cofactor[0][2]
    )
    return jnp.stack(
        [
            jnp.stack([cofactor[col_at][row_at] / determinant for col_at in range(3)])
            for row_at in range(3)
        ]
    )


def block_inverse(matrix):
    factor = {}
    for col_at in range(9):
        pivot_value = matrix[col_at, col_at]
        for middle in range(col_at):
            pivot_value = pivot_value - factor[col_at, middle] * factor[col_at, middle]
        diagonal_root = jnp.sqrt(pivot_value)
        factor[col_at, col_at] = diagonal_root
        for row_at in range(col_at + 1, 9):
            running = matrix[row_at, col_at]
            for middle in range(col_at):
                running = running - factor[row_at, middle] * factor[col_at, middle]
            factor[row_at, col_at] = running / diagonal_root
    factor_inverse = {}
    for row_at in range(9):
        factor_inverse[row_at, row_at] = 1.0 / factor[row_at, row_at]
        for col_at in range(row_at):
            running = factor[row_at, col_at] * factor_inverse[col_at, col_at]
            for middle in range(col_at + 1, row_at):
                running = running + factor[row_at, middle] * factor_inverse[middle, col_at]
            factor_inverse[row_at, col_at] = -running / factor[row_at, row_at]
    result_rows = []
    for row_at in range(9):
        entries = []
        for col_at in range(9):
            running = (
                factor_inverse[max(row_at, col_at), row_at]
                * factor_inverse[max(row_at, col_at), col_at]
            )
            for middle in range(max(row_at, col_at) + 1, 9):
                running = running + factor_inverse[middle, row_at] * factor_inverse[middle, col_at]
            entries.append(running)
        result_rows.append(jnp.stack(entries))
    return jnp.stack(result_rows)


def assemble(packed):
    positions = {}
    for index_at, pair in enumerate(block_pairs):
        positions[pair[0], pair[1]] = index_at
        positions[pair[1], pair[0]] = index_at
    return jnp.stack(
        [
            jnp.stack(
                [
                    packed[positions[row_at, col_at]] + (damping if row_at == col_at else 0.0)
                    for col_at in range(9)
                ]
            )
            for row_at in range(9)
        ]
    )


def apply_blocks(inverse_blocks, vector):
    return jnp.sum(inverse_blocks * vector[None], axis=1)


def slot_basics(camera_jacobian, point_jacobian, residuals, track_length):
    tracks = camera_jacobian.shape[1]
    in_track = (jnp.arange(tracks, dtype=jnp.int32)[:, None] < track_length[None, :]).astype(
        jnp.float32
    )
    camera_blocks = camera_jacobian.reshape(2, 9, tracks, -1) * in_track
    point_blocks = point_jacobian.reshape(2, 3, tracks, -1) * in_track
    errors = residuals * in_track
    coupling = jnp.sum(camera_blocks[:, :, None] * point_blocks[:, None], axis=0)
    point_system = jnp.sum(point_blocks[:, :, None] * point_blocks[:, None], axis=(0, 3))
    point_system = point_system + damping * jnp.eye(3, dtype=jnp.float32)[:, :, None]
    point_inverse = inverse_small(point_system)
    point_gradient = -jnp.sum(point_blocks * errors[:, None], axis=(0, 2))
    return (camera_blocks, errors, coupling, point_inverse, point_gradient)


def camera_terms(camera_blocks, errors, coupling, point_inverse, point_gradient):
    solved = jnp.sum(point_inverse * point_gradient[None], axis=1)
    scaled = coupling[:, 0][:, None] * point_inverse[0][None, :, None, :]
    for middle in range(1, 3):
        scaled = scaled + coupling[:, middle][:, None] * point_inverse[middle][None, :, None, :]
    packed = []
    for leading, trailing in block_pairs:
        packed.append(
            jnp.sum(camera_blocks[:, leading] * camera_blocks[:, trailing], axis=0)
            - jnp.sum(scaled[leading] * coupling[trailing], axis=0)
        )
    right_side = -jnp.sum(camera_blocks * errors[:, None], axis=0) - jnp.sum(
        coupling * solved[None, :, None], axis=1
    )
    return jnp.concatenate([jnp.stack(packed), right_side], axis=0)


def slot_product(camera_blocks, coupling, point_inverse, gathered):
    projected = jnp.sum(camera_blocks * gathered[None], axis=1)
    pulled = jnp.sum(coupling * gathered[:, None], axis=(0, 2))
    solved = jnp.sum(point_inverse * pulled[None], axis=1)
    return jnp.sum(camera_blocks * projected[:, None], axis=0) - jnp.sum(
        coupling * solved[None, :, None], axis=1
    )


def by_dense(camera_jacobian, point_jacobian, residuals, observed_camera, track_length):
    camera_blocks, errors, coupling, point_inverse, point_gradient = slot_basics(
        camera_jacobian, point_jacobian, residuals, track_length
    )
    tracks, points = observed_camera.shape
    rows, cols = lax.axis_size("row"), lax.axis_size("col")
    cameras = CAM_DEV * rows * cols
    flat_cameras = observed_camera.reshape(-1)

    def into_cameras(values):
        width = values.shape[0]
        by_camera = (
            jnp.zeros((cameras, width), jnp.float32).at[flat_cameras].add(jnp.transpose(values))
        )
        return jnp.transpose(by_camera)

    def pick_slots(whole):
        slot_rows = jnp.transpose(whole)[flat_cameras]
        return jnp.transpose(slot_rows).reshape(9, tracks, points)

    def spread_out(value):
        copies = jnp.broadcast_to(value[:, None], (9, OWNERS, CAM_DEV)).reshape(9, cameras)
        return lax.all_to_all(copies, ("row", "col"), split_axis=1, concat_axis=1, tiled=True)

    term_values = camera_terms(
        camera_blocks, errors, coupling, point_inverse, point_gradient
    ).reshape(54, -1)
    local_terms = into_cameras(term_values).reshape(54, rows * cols, CAM_DEV)
    own_terms = jnp.sum(
        lax.all_to_all(local_terms, ("row", "col"), split_axis=1, concat_axis=1, tiled=True), axis=1
    )
    inverse_blocks = block_inverse(assemble(own_terms[:45]))
    right_side = own_terms[45:]

    first = apply_blocks(inverse_blocks, right_side)
    first_slots = pick_slots(spread_out(first))
    first_pulled = jnp.sum(coupling * first_slots[:, None], axis=(0, 2))
    contrib = slot_product(camera_blocks, coupling, point_inverse, first_slots)
    local_image = into_cameras(contrib.reshape(9, -1)).reshape(9, OWNERS, CAM_DEV)
    gathered_image = lax.all_to_all(
        local_image, ("row", "col"), split_axis=1, concat_axis=1, tiled=True
    )
    first_image = damping * first + jnp.sum(gathered_image, axis=1)

    second = apply_blocks(inverse_blocks, first_image)
    second_slots = pick_slots(spread_out(second))
    second_pulled = jnp.sum(coupling * second_slots[:, None], axis=(0, 2))
    projected = jnp.sum(camera_blocks * second_slots[None], axis=1)
    solved = jnp.sum(point_inverse * second_pulled[None], axis=1)
    own_sums = jnp.stack(
        [
            jnp.sum(right_side * first),
            jnp.sum(first * first_image),
            jnp.sum(first_image * second),
            jnp.sum(second * second)
            + jnp.sum(projected * projected)
            - jnp.sum(second_pulled * solved),
        ]
    )
    spread = jnp.broadcast_to(own_sums[None], (OWNERS, 4))
    energy, curvature, crossed, second_curvature = jnp.sum(exchange(spread), axis=0)
    step_size = energy / curvature
    renewed = step_size * step_size * crossed - energy
    ratio = 1.0 + renewed / energy
    second_step = renewed / (
        ratio * ratio * curvature
        - 2.0 * step_size * ratio * crossed
        + step_size * step_size * second_curvature
    )
    first_weight = step_size + second_step * ratio
    second_weight = -second_step * step_size
    camera_move = first_weight * first + second_weight * second
    pulled = first_weight * first_pulled + second_weight * second_pulled
    point_move = jnp.sum(point_inverse * (point_gradient - pulled)[None], axis=1)
    return (camera_move, point_move)


def on_device(camera_jacobian, point_jacobian, residuals, observed_camera, track_length):
    operands = (camera_jacobian, point_jacobian, residuals, observed_camera, track_length)
    overflow, kept = by_slots(*operands)
    return lax.cond(
        overflow > 0,
        lambda given, unused: by_dense(*given),
        lambda unused, found: finish(*found),
        operands,
        kept,
    )


def solution(mesh):
    in_specs = (
        P(None, None, ("row", "col")),
        P(None, None, ("row", "col")),
        P(None, None, ("row", "col")),
        P(None, ("row", "col")),
        P(("row", "col")),
    )
    out_specs = (P(None, ("row", "col")), P(None, ("row", "col")))
    return jax.shard_map(
        on_device, mesh=mesh, in_specs=in_specs, out_specs=out_specs, check_vma=False
    )
```

```python
import jax
import jax.numpy as jnp
from jax import lax
from jax.experimental import pallas as pl
from jax.experimental.pallas import tpu as pltpu
from jax.sharding import PartitionSpec as P

CAM_DEV = 384
TRACK = 8
PT_DEV = 1024
OWNERS = 128
LANES = 128
WIDTH = 21
GROUPS = 6
ROWS = 13
CAP = GROUPS * ROWS
SPAN = 80
FEW = 64
CAMERA_AT = 20
ENTRIES = 56
COUNT_AT = GROUPS * WIDTH
BLOCKS = TRACK * PT_DEV // LANES

F32 = jnp.float32
BF16 = jnp.bfloat16
PARAMS = pltpu.CompilerParams(vmem_limit_bytes=48 * 2**20)
block_pairs = [(leading, trailing) for leading in range(9) for trailing in range(leading, 9)]


def iota(shape, axis):
    return lax.broadcasted_iota(jnp.int32, shape, axis)


def two_parts(value):
    high = value.astype(BF16)
    low = (value - high.astype(F32)).astype(BF16)
    return high, low


def dot(left, right):
    return jnp.dot(left, right, preferred_element_type=F32)


def dot_lanes(left, right):
    return lax.dot_general(left, right, (((1,), (1,)), ((), ())), preferred_element_type=F32)


def total(value):
    return jnp.sum(jnp.sum(value, axis=0, keepdims=True), axis=1, keepdims=True)


def over_tracks(value):
    return jnp.sum(value, axis=0, keepdims=True)


def used_slots(length_ref, lanes):
    return iota((TRACK, LANES), 0) < length_ref[:, lanes]


def masked_points(point_ref, used, lanes):
    return [
        [jnp.where(used, point_ref[3 * i + a, :, lanes], 0.0) for a in range(3)] for i in range(2)
    ]


def times_inverse(inverse, vector):
    v00, v01, v02, v11, v12, v22 = inverse
    x, y, z = vector
    return [v00 * x + v01 * y + v02 * z, v01 * x + v11 * y + v12 * z, v02 * x + v12 * y + v22 * z]


def owner_of(camera):
    return ((camera >> 7) * 171) >> 9


def prepare_kernel(camera_in, point_in, error_in, index_ref, length_ref, out_ref, route_ref, state_ref, root_ref, flag_ref, owned_ref, camera_ref, point_ref, error_ref, pay_ref, code_ref, near_ref, slot_ref, block_ref, camera_sem, point_sem, error_sem, code_sem):
    copies = [
        pltpu.make_async_copy(camera_in, camera_ref, camera_sem),
        pltpu.make_async_copy(point_in, point_ref, point_sem),
        pltpu.make_async_copy(error_in, error_ref, error_sem),
    ]
    for copy in copies:
        copy.start()
    used = iota((TRACK, PT_DEV), 0) < length_ref[...]
    route_ref[0:TRACK, :] = jnp.where(used, owner_of(index_ref[...]), OWNERS)

    step = 256
    upto = jnp.where(iota((step, step), 0) <= iota((step, step), 1), 1.0, 0.0).astype(BF16)
    before = jnp.zeros((OWNERS, step), F32)
    names = iota((OWNERS, step), 0)
    for s in range(TRACK):
        for chunk in range(PT_DEV // step):
            lanes = slice(chunk * step, (chunk + 1) * step)
            chosen = names == route_ref[s : s + 1, lanes]
            hot = jnp.where(chosen, 1.0, 0.0).astype(BF16)
            owned_ref[s, :, lanes] = hot
            counts = dot(hot, upto)
            rank = jnp.sum(jnp.where(chosen, counts + before, 0.0), axis=0, keepdims=True) - 1.0
            before = before + jnp.broadcast_to(counts[:, step - 1 : step], (OWNERS, step))
            route_ref[TRACK + s : TRACK + s + 1, lanes] = rank.astype(jnp.int32)

    owner = route_ref[0:TRACK, :]
    rank = route_ref[TRACK : 2 * TRACK, :]
    fits = (owner < OWNERS) & (rank < CAP)
    row_at = (rank * 171) >> 10
    place = (rank - row_at * GROUPS) * (OWNERS * ROWS) + owner * ROWS + row_at
    code = jnp.where(fits, place, GROUPS * OWNERS * ROWS)
    for chunk in range(PT_DEV // LANES):
        code_ref[chunk * TRACK : (chunk + 1) * TRACK, :] = code[:, chunk * LANES : (chunk + 1) * LANES]
    code_copy = pltpu.make_async_copy(code_ref, near_ref, code_sem)
    code_copy.start()
    most = jnp.max(jnp.max(before, axis=0, keepdims=True), axis=1, keepdims=True)
    lane = iota((OWNERS, LANES), 1)
    flag_ref[...] = jnp.where(lane > COUNT_AT, most, before[:, 0:LANES])
    for copy in copies:
        copy.wait()
    for chunk in range(PT_DEV // LANES):
        lanes = slice(chunk * LANES, (chunk + 1) * LANES)
        used = used_slots(length_ref, lanes)
        point = masked_points(point_ref, used, lanes)
        error = [jnp.where(used, error_ref[i, :, lanes], 0.0) for i in range(2)]

        def pair(a, b):
            return over_tracks(point[0][a] * point[0][b] + point[1][a] * point[1][b])

        s00, s01, s02 = 1.0 + pair(0, 0), pair(0, 1), pair(0, 2)
        s11, s12, s22 = 1.0 + pair(1, 1), pair(1, 2), 1.0 + pair(2, 2)
        c00 = s11 * s22 - s12 * s12
        c01 = s12 * s02 - s01 * s22
        c02 = s01 * s12 - s11 * s02
        c11 = s22 * s00 - s02 * s02
        c12 = s02 * s01 - s12 * s00
        c22 = s00 * s11 - s01 * s01
        determinant = s00 * c00 + s01 * c01 + s02 * c02
        scale = 1.0 / determinant
        inverse = [c * scale for c in (c00, c01, c02, c11, c12, c22)]
        gradient = [
            -over_tracks(point[0][a] * error[0] + point[1][a] * error[1]) for a in range(3)
        ]
        for at, value in enumerate(inverse + gradient):
            state_ref[at : at + 1, lanes] = value
        solved = times_inverse(inverse, gradient)
        u0 = times_inverse(inverse, point[0])
        u1 = times_inverse(inverse, point[1])

        def along(left, right):
            return left[0] * right[0] + left[1] * right[1] + left[2] * right[2]

        camera = index_ref[:, lanes]
        owner = owner_of(camera)
        local = camera - owner * CAM_DEV
        b01 = -along(u0, point[1])
        root0 = jnp.sqrt(1.0 - along(u0, point[0]))
        root1 = b01 / root0
        root2 = jnp.sqrt(1.0 - along(u1, point[1]) - root1 * root1)
        inverse0, inverse2 = 1.0 / root0, 1.0 / root2
        side0 = (error[0] + along(solved, point[0])) * inverse0
        side1 = (error[1] + along(solved, point[1]) - root1 * side0) * inverse2
        values = [root0 * camera_ref[j, :, lanes] + root1 * camera_ref[9 + j, :, lanes] for j in range(9)]
        values += [root2 * camera_ref[9 + j, :, lanes] for j in range(9)]
        values += [side0, side1, (local + 1).astype(F32)]
        for at, value in enumerate((inverse0, root1, inverse2)):
            root_ref[at * TRACK : (at + 1) * TRACK, lanes] = value
        for f in range(WIDTH):
            at = (chunk * WIDTH + f) * TRACK
            pay_ref[at : at + TRACK, :] = values[f]
    dispatch(near_ref, pay_ref, flag_ref, out_ref, slot_ref, block_ref, code_copy)


def dispatch(code_ref, pay_ref, flag_ref, out_ref, slot_ref, block_ref, code_copy):
    rows = OWNERS * ROWS
    zeros = jnp.zeros((8, LANES), F32)
    slots_ref = slot_ref.reshape(BLOCKS * LANES, LANES)
    blocks_ref = block_ref.reshape(GROUPS * rows + 8, LANES)

    share = -(-GROUPS * rows // (BLOCKS * 8)) * 8
    within = iota((LANES, LANES), 1) % WIDTH
    for first in range(0, BLOCKS, GROUPS):
        blocks = []
        for block in range(first, first + GROUPS):
            chunk, s = divmod(block, TRACK)
            if block < BLOCKS:
                blocks.append(pay_ref[pl.ds(chunk * WIDTH * TRACK + s, WIDTH, stride=TRACK), :])
            else:
                blocks.append(jnp.zeros((WIDTH, LANES), F32))
        turned = jnp.transpose(jnp.concatenate(blocks + [zeros[0 : LANES - COUNT_AT]], axis=0))
        for block in range(first, min(first + GROUPS, BLOCKS)):
            slots_ref[block * LANES : (block + 1) * LANES, :] = jnp.take_along_axis(
                turned, within + (block - first) * WIDTH, axis=1, mode="promise_in_bounds"
            )
            start = min(block * share, GROUPS * rows)
            count = min(share, GROUPS * rows - start)
            if count:
                blocks_ref[start : start + count, :] = jnp.zeros((count, LANES), F32)

    code_copy.wait()

    def place(block, carry):
        def load(start):
            columns = range(start, min(start + 16, LANES))
            return [(code_ref[block, j], slot_ref[block, j]) for j in columns]

        ready = load(0)
        for start in range(16, LANES + 16, 16):
            coming = load(start)
            for code, slot in ready:
                block_ref[code] = slot
            ready = coming
        return carry

    lax.fori_loop(0, BLOCKS, place, 0)
    group = iota((8, LANES), 1) // WIDTH

    def merge(at, carry):
        for j in range(8):
            start = pl.multiple_of(at * 64 + j * 8, 8)
            value = zeros
            for k in range(GROUPS):
                value = jnp.where(group == k, blocks_ref[pl.ds(k * rows + start, 8), :], value)
            out_ref[pl.ds(start, 8), :] = value
        return carry

    lax.fori_loop(0, rows // 64, merge, 0)
    lane = iota((OWNERS, LANES), 1)
    leading = pl.ds(0, OWNERS, stride=ROWS)
    out_ref[leading, :] = jnp.where(lane >= COUNT_AT, flag_ref[...], out_ref[leading, :])


def solve(factor, scales, vector):
    forward = []
    for i in range(9):
        value = vector[i]
        for j in range(i):
            value = value - factor[i, j] * forward[j]
        forward.append(value * scales[i])
    result = [None] * 9
    for i in reversed(range(9)):
        value = forward[i]
        for j in range(i + 1, 9):
            value = value - factor[j, i] * result[j]
        result[i] = value * scales[i]
    return result


def hot_cameras(feature_ref, hot_ref, block):
    names = iota((LANES, LANES), 0)
    for r in range(8):
        camera = feature_ref[pl.ds(CAMERA_AT * SPAN + block * 8 + r, 1), :].astype(jnp.int32) - 1
        hot = jnp.where(names == (camera & (LANES - 1)), 1.0, 0.0).astype(BF16)
        hot_ref[:, block * PT_DEV + r * LANES : block * PT_DEV + (r + 1) * LANES] = hot


def features_of(feature_ref, f, block):
    start = f * SPAN + block * 8
    return feature_ref[start : start + 8, :]


def image_slots(vector, feature_ref, table_ref, image_ref, many):
    for j in range(9):
        for c in range(3):
            at = (3 * j + c) * 8
            table_ref[at : at + 8, :] = jnp.broadcast_to(vector[j][c : c + 1, :], (8, LANES))

    def one(block):
        camera = features_of(feature_ref, CAMERA_AT, block).astype(jnp.int32) - 1
        third = camera >> 7
        lane = camera & (LANES - 1)
        images = [jnp.zeros((8, LANES), F32)] * 2
        for j in range(9):
            found = [
                jnp.take_along_axis(
                    table_ref[(3 * j + c) * 8 : (3 * j + c + 1) * 8, :],
                    lane,
                    axis=1,
                    mode="promise_in_bounds",
                )
                for c in range(3)
            ]
            value = jnp.where(third == 1, found[1], jnp.where(third == 2, found[2], found[0]))
            for i in range(2):
                images[i] = images[i] + features_of(feature_ref, 9 * i + j, block) * value
        for i in range(2):
            start = i * LANES + block * 8
            image_ref[start : start + 8, :] = images[i]

    for block in range(FEW // 8):
        one(block)

    @pl.when(many)
    def _():
        for block in range(FEW // 8, SPAN // 8):
            one(block)


def keep_parts(part_ref, feature_ref, parts_ref, block, count):
    for r in range(8):
        lanes = slice(block * PT_DEV + r * LANES, block * PT_DEV + (r + 1) * LANES)
        camera = feature_ref[pl.ds(CAMERA_AT * SPAN + block * 8 + r, 1), :].astype(jnp.int32) - 1
        value = part_ref[pl.ds(r, count, stride=8), :]
        high = value.astype(BF16).astype(F32)
        both = jnp.concatenate([high, value - high], axis=0).astype(BF16)
        third = jnp.broadcast_to(camera >> 7, (16, LANES))
        for c in range(3):
            inside = jnp.where(third == c, 1.0, 0.0).astype(BF16)
            inside = jnp.concatenate([inside] * (count // 8), axis=0)
            parts_ref[2 * c * count : 2 * (c + 1) * count, lanes] = both * inside


def camera_sums(terms, parts_ref, hot_ref, part_ref, sum_ref, count, many):
    def block_sums(block):
        terms(block)
        lanes = slice(block * PT_DEV, (block + 1) * PT_DEV)
        return dot_lanes(parts_ref[:, lanes], hot_ref[:, lanes])

    sums = block_sums(0)
    for block in range(1, FEW // 8):
        sums = sums + block_sums(block)
    sum_ref[...] = sums

    @pl.when(many)
    def _():
        for block in range(FEW // 8, SPAN // 8):
            sum_ref[...] += block_sums(block)

    part_ref[...] = jnp.zeros(part_ref.shape, F32)
    for c in range(3):
        at = 2 * c * count
        part_ref[pl.ds(c, count, stride=8), :] = (
            sum_ref[at : at + count, :] + sum_ref[at + count : at + 2 * count, :]
        )


def turn_in(got_ref, i):
    return jnp.transpose(got_ref[pl.ds(i, OWNERS, stride=2), :])


def turn_out(image_ref, out_ref):
    for i in range(2):
        out_ref[pl.ds(i, OWNERS, stride=2), :] = jnp.transpose(
            image_ref[i * LANES : (i + 1) * LANES, :]
        )


def first_camera_kernel(got_ref, feature_ref, factor_ref, first_ref, out_ref, flag_ref, hot_ref, parts_ref, table_ref, image_ref, sum_ref, part_ref):
    image_ref[...] = jnp.zeros((2 * LANES, LANES), F32)
    feature_ref[...] = jnp.zeros(feature_ref.shape, F32)

    def take_row(q):
        turned = jnp.transpose(got_ref[pl.ds(q, OWNERS, stride=ROWS), :])
        for k in range(GROUPS):
            feature_ref[pl.ds(q * GROUPS + k, WIDTH, stride=SPAN), :] = turned[
                k * WIDTH : (k + 1) * WIDTH, :
            ]
        return turned

    turned = take_row(0)
    worst = jnp.max(turned[COUNT_AT + 1 : COUNT_AT + 2, :])
    flag_ref[0, 0] = jnp.where(worst > CAP, 1, 0)
    most = jnp.max(turned[COUNT_AT : COUNT_AT + 1, :])
    many = most > FEW
    few_rows = -(-FEW // GROUPS)
    for q in range(1, few_rows):
        take_row(q)

    @pl.when(many)
    def _():
        for q in range(few_rows, ROWS):
            take_row(q)

    part_ref[...] = jnp.zeros((ENTRIES * 8, LANES), F32)

    def gather_terms(block):
        hot_cameras(feature_ref, hot_ref, block)
        f = [features_of(feature_ref, at, block) for at in range(20)]
        for at, (j, k) in enumerate(block_pairs):
            part_ref[at * 8 : (at + 1) * 8, :] = f[j] * f[k] + f[9 + j] * f[9 + k]
        for j in range(9):
            part_ref[(45 + j) * 8 : (46 + j) * 8, :] = -(f[j] * f[18] + f[9 + j] * f[19])
        keep_parts(part_ref, feature_ref, parts_ref, block, ENTRIES)

    camera_sums(gather_terms, parts_ref, hot_ref, part_ref, sum_ref, ENTRIES, many)
    matrix = {}
    for at, (j, k) in enumerate(block_pairs):
        entry = part_ref[at * 8 : (at + 1) * 8, :]
        matrix[k, j] = entry + 1.0 if j == k else entry
    side = [part_ref[(45 + j) * 8 : (46 + j) * 8, :] for j in range(9)]
    factor, scales = {}, []
    for j in range(9):
        pivot = matrix[j, j]
        for m in range(j):
            pivot = pivot - factor[j, m] * factor[j, m]
        scales.append(1.0 / jnp.sqrt(pivot))
        for i in range(j + 1, 9):
            running = matrix[i, j]
            for m in range(j):
                running = running - factor[i, m] * factor[j, m]
            factor[i, j] = running * scales[j]
    for at, (j, k) in enumerate(block_pairs):
        factor_ref[at * 8 : (at + 1) * 8, :] = scales[j] if j == k else factor[k, j]
    first = solve(factor, scales, side)
    energy = side[0] * first[0]
    for j in range(1, 9):
        energy = energy + side[j] * first[j]
    for j in range(9):
        first_ref[j * 8 : (j + 1) * 8, :] = first[j]
    first_ref[72:80, :] = energy
    first_ref[80:88, :] = jnp.broadcast_to(jnp.max(turned[COUNT_AT : COUNT_AT + 1, :], axis=1, keepdims=True), (8, LANES))
    image_slots(first, feature_ref, table_ref, image_ref, many)
    turn_out(image_ref, out_ref)


def either_span(flag_ref, work):
    many = jnp.max(flag_ref[0:8, :]) > FEW
    pl.when(many)(lambda: work(SPAN))
    pl.when(jnp.logical_not(many))(lambda: work(FEW))


def pull_slots(got_ref, route_ref, point_ref, length_ref, state_ref, root_ref, owned_ref, value_ref, pulled_ref, curve_ref, span, back):
    images = []
    for i in range(2):
        images.append(turn_in(got_ref, i)[0:span, :])
    high, low = two_parts(jnp.concatenate(images, axis=0))
    parts = jnp.concatenate([high, low], axis=1)
    ranks = iota((span, PT_DEV), 0)
    for s in range(TRACK):
        hot = owned_ref[s]
        got = dot(parts, jnp.concatenate([hot, hot], axis=0))
        here = ranks == route_ref[TRACK + s : TRACK + s + 1, :]
        for i in range(2):
            value_ref[i * TRACK + s : i * TRACK + s + 1, :] = jnp.sum(
                jnp.where(here, got[i * span : (i + 1) * span, :], 0.0), axis=0, keepdims=True
            )
    curve = jnp.zeros((TRACK, LANES), F32)
    for chunk in range(PT_DEV // LANES):
        lanes = slice(chunk * LANES, (chunk + 1) * LANES)
        used = used_slots(length_ref, lanes)
        point = masked_points(point_ref, used, lanes)
        root = [root_ref[at * TRACK : (at + 1) * TRACK, lanes] for at in range(3)]
        image1 = value_ref[TRACK : 2 * TRACK, lanes] * root[2]
        image = [(value_ref[0:TRACK, lanes] - root[1] * image1) * root[0], image1]
        pulled = [over_tracks(point[0][a] * image[0] + point[1][a] * image[1]) for a in range(3)]
        inverse = [state_ref[at : at + 1, lanes] for at in range(6)]
        solved = times_inverse(inverse, pulled)
        for a in range(3):
            pulled_ref[a : a + 1, lanes] = pulled[a]
        result = [
            image[i] - (point[i][0] * solved[0] + point[i][1] * solved[1] + point[i][2] * solved[2])
            for i in range(2)
        ]
        if back:
            result0 = result[0] * root[0]
            value_ref[0:TRACK, lanes] = result0
            value_ref[TRACK : 2 * TRACK, lanes] = (result[1] - root[1] * result0) * root[2]
        else:
            curve = curve + image[0] * result[0] + image[1] * result[1]
    if not back:
        curve_ref[...] = curve


def first_point_kernel(got_ref, route_ref, point_ref, length_ref, state_ref, root_ref, flag_ref, owned_ref, pulled_ref, out_ref, value_ref, image_ref):
    image_ref[...] = jnp.zeros((2 * LANES, LANES), F32)

    def work(span):
        pull_slots(got_ref, route_ref, point_ref, length_ref, state_ref, root_ref, owned_ref, value_ref, pulled_ref, None, span, True)
        ranks = iota((span, PT_DEV), 0)
        sums = jnp.zeros((4 * span, OWNERS), F32)
        for s in range(TRACK):
            here = ranks == route_ref[TRACK + s : TRACK + s + 1, :]
            spread = []
            for i in range(2):
                value = value_ref[i * TRACK + s : i * TRACK + s + 1, :]
                spread.append(jnp.where(here, value, 0.0))
            high, low = two_parts(jnp.concatenate(spread, axis=0))
            sums = sums + dot_lanes(jnp.concatenate([high, low], axis=0), owned_ref[s])
        sums = sums[0 : 2 * span] + sums[2 * span :]
        for i in range(2):
            image_ref[i * LANES : i * LANES + span, :] = sums[i * span : (i + 1) * span, :]

    either_span(flag_ref, work)
    turn_out(image_ref, out_ref)


def second_point_kernel(got_ref, route_ref, point_ref, length_ref, state_ref, root_ref, flag_ref, owned_ref, pulled_ref, out_ref, scalar_ref, value_ref, curve_ref):
    def work(span):
        pull_slots(got_ref, route_ref, point_ref, length_ref, state_ref, root_ref, owned_ref, value_ref, pulled_ref, curve_ref, span, False)

    either_span(flag_ref, work)
    out_ref[...] = jnp.broadcast_to(total(curve_ref[...]), (OWNERS, LANES))
    scalar_ref[...] = jnp.broadcast_to(
        jnp.sum(got_ref[pl.ds(0, OWNERS, stride=2), :], axis=0, keepdims=True), (8, LANES)
    )


def second_camera_kernel(got_ref, feature_ref, factor_ref, first_ref, second_ref, out_ref, hot_ref, parts_ref, table_ref, image_ref, sum_ref, wide_ref):
    for i in range(2):
        image_ref[i * LANES : (i + 1) * LANES, :] = turn_in(got_ref, i)
    many = jnp.max(first_ref[80:88, :]) > FEW
    wide_ref[...] = jnp.zeros((LANES, LANES), F32)

    def gather_terms(block):
        hot_cameras(feature_ref, hot_ref, block)
        back = [
            image_ref[i * LANES + block * 8 : i * LANES + (block + 1) * 8, :] for i in range(2)
        ]
        for j in range(9):
            wide_ref[j * 8 : (j + 1) * 8, :] = (
                features_of(feature_ref, j, block) * back[0]
                + features_of(feature_ref, 9 + j, block) * back[1]
            )
        keep_parts(wide_ref, feature_ref, parts_ref, block, 16)

    camera_sums(gather_terms, parts_ref, hot_ref, wide_ref, sum_ref, 16, many)
    first = [first_ref[j * 8 : (j + 1) * 8, :] for j in range(9)]
    image = [first[j] + wide_ref[j * 8 : (j + 1) * 8, :] for j in range(9)]
    factor, scales = {}, []
    for at, (j, k) in enumerate(block_pairs):
        entry = factor_ref[at * 8 : (at + 1) * 8, :]
        if j == k:
            scales.append(entry)
        else:
            factor[k, j] = entry
    second = solve(factor, scales, image)
    for j in range(9):
        second_ref[j * 8 : (j + 1) * 8, :] = second[j]

    def inner(left, right):
        value = left[0] * right[0]
        for j in range(1, 9):
            value = value + left[j] * right[j]
        return value

    image_slots(second, feature_ref, table_ref, image_ref, many)
    scalars = [first_ref[72:80, :], inner(first, image), inner(image, second), inner(second, second)]
    for at, value in enumerate(scalars):
        image_ref[SPAN + at : SPAN + at + 1, :] = jnp.broadcast_to(total(value), (1, LANES))
    turn_out(image_ref, out_ref)


def finish_kernel(curve_ref, scalar_ref, first_ref, second_ref, state_ref, first_pulled_ref, second_pulled_ref, camera_out, point_out, camera_ref, point_ref, camera_sem, point_sem):
    own = jnp.sum(curve_ref[...], axis=0, keepdims=True)[:, 0:1]
    energy, curvature, crossed, square = [
        scalar_ref[0:1, SPAN + at : SPAN + at + 1] for at in range(4)
    ]
    step_size = energy / curvature
    renewed = step_size * step_size * crossed - energy
    ratio = 1.0 + renewed / energy
    second_step = renewed / (
        ratio * ratio * curvature
        - 2.0 * step_size * ratio * crossed
        + step_size * step_size * (square + own)
    )
    first_weight = step_size + second_step * ratio
    second_weight = -second_step * step_size
    for c in range(3):
        camera_ref[:, c * LANES : (c + 1) * LANES] = (
            first_weight * first_ref[pl.ds(c, 9, stride=8), :]
            + second_weight * second_ref[pl.ds(c, 9, stride=8), :]
        )
    camera_copy = pltpu.make_async_copy(camera_ref, camera_out, camera_sem)
    camera_copy.start()
    left = [
        state_ref[6 + a : 7 + a, :]
        - first_weight * first_pulled_ref[a : a + 1, :]
        - second_weight * second_pulled_ref[a : a + 1, :]
        for a in range(3)
    ]
    moved = times_inverse([state_ref[at : at + 1, :] for at in range(6)], left)
    for a in range(3):
        point_ref[a : a + 1, :] = moved[a]
    point_copy = pltpu.make_async_copy(point_ref, point_out, point_sem)
    point_copy.start()
    camera_copy.wait()
    point_copy.wait()


def call(kernel, outs, scratch, operands, in_scalar=0):
    specs = [
        pl.BlockSpec(memory_space=pltpu.SMEM if at < in_scalar else pltpu.VMEM)
        for at in range(len(operands))
    ]
    return pl.pallas_call(
        kernel,
        out_shape=[jax.ShapeDtypeStruct(shape, dtype) for shape, dtype in outs],
        in_specs=specs,
        out_specs=[
            pl.BlockSpec(memory_space=pltpu.SMEM if shape == (1, 1) else pltpu.VMEM)
            for shape, unused in outs
        ],
        scratch_shapes=[pltpu.VMEM(shape, dtype) for shape, dtype in scratch],
        compiler_params=PARAMS,
    )(*operands)


def exchange(rows):
    blocks = rows.reshape(OWNERS, 1, -1)
    blocks = lax.all_to_all(blocks, ("row", "col"), split_axis=0, concat_axis=0, tiled=True)
    return blocks.reshape(rows.shape)


def by_slots(camera_jacobian, point_jacobian, residuals, observed_camera, track_length):
    lengths = track_length.reshape(1, PT_DEV)
    in_vmem = [pl.BlockSpec(memory_space=pltpu.VMEM)]
    held = [(18, TRACK, PT_DEV), (6, TRACK, PT_DEV), (2, TRACK, PT_DEV)]
    outs = [
        ((OWNERS * ROWS, LANES), F32),
        ((2 * TRACK, PT_DEV), jnp.int32),
        ((16, PT_DEV), F32),
        ((3 * TRACK, PT_DEV), F32),
        ((OWNERS, LANES), F32),
        ((TRACK, OWNERS, PT_DEV), BF16),
    ]
    sent, route, state, root, flag, owned = pl.pallas_call(
        prepare_kernel,
        out_shape=[jax.ShapeDtypeStruct(shape, dtype) for shape, dtype in outs],
        in_specs=[pl.BlockSpec(memory_space=pl.ANY)] * 3 + in_vmem * 2,
        out_specs=in_vmem * len(outs),
        scratch_shapes=[pltpu.VMEM(shape, F32) for shape in held]
        + [
            pltpu.VMEM((WIDTH * BLOCKS, LANES), F32),
            pltpu.VMEM((BLOCKS, LANES), jnp.int32),
            pltpu.SMEM((BLOCKS, LANES), jnp.int32),
            pltpu.VMEM((BLOCKS, LANES, 1, LANES), F32),
            pltpu.VMEM((GROUPS * OWNERS * ROWS + 8, 1, LANES), F32),
        ]
        + [pltpu.SemaphoreType.DMA] * 4,
        compiler_params=PARAMS,
    )(camera_jacobian, point_jacobian, residuals, observed_camera, lengths)
    hot = ((LANES, SPAN * LANES), BF16)
    table = ((27 * 8, LANES), F32)
    image = ((2 * LANES, LANES), F32)
    pair = ((2 * OWNERS, LANES), F32)
    features, factor, first, out, overflow = call(
        first_camera_kernel,
        [((WIDTH * SPAN, LANES), F32), ((45 * 8, LANES), F32), ((88, LANES), F32), pair, ((1, 1), jnp.int32)],
        [hot, ((6 * ENTRIES, SPAN * LANES), BF16), table, image, ((6 * ENTRIES, LANES), F32), ((ENTRIES * 8, LANES), F32)],
        (exchange(sent),),
    )
    first_pulled, out = call(
        first_point_kernel,
        [((8, PT_DEV), F32), pair],
        [((2 * TRACK, PT_DEV), F32), image],
        (exchange(out), route, point_jacobian, lengths, state, root, flag, owned),
    )
    second, out = call(
        second_camera_kernel,
        [((72, LANES), F32), pair],
        [hot, ((96, SPAN * LANES), BF16), table, image, ((96, LANES), F32), ((LANES, LANES), F32)],
        (exchange(out), features, factor, first),
    )
    second_pulled, curve, scalars = call(
        second_point_kernel,
        [((8, PT_DEV), F32), ((OWNERS, LANES), F32), ((8, LANES), F32)],
        [((2 * TRACK, PT_DEV), F32), ((TRACK, LANES), F32)],
        (exchange(out), route, point_jacobian, lengths, state, root, flag, owned),
    )
    return overflow[0, 0], (exchange(curve), scalars, first, second, state, first_pulled, second_pulled)


def finish(*operands):
    shapes = [(9, CAM_DEV), (3, PT_DEV)]
    return tuple(
        pl.pallas_call(
            finish_kernel,
            out_shape=[jax.ShapeDtypeStruct(shape, F32) for shape in shapes],
            in_specs=[pl.BlockSpec(memory_space=pltpu.VMEM)] * len(operands),
            out_specs=[pl.BlockSpec(memory_space=pltpu.HBM)] * 2,
            scratch_shapes=[pltpu.VMEM(shape, F32) for shape in shapes]
            + [pltpu.SemaphoreType.DMA] * 2,
            compiler_params=PARAMS,
        )(*operands)
    )


damping = 1.0


def inverse_small(matrix):
    entries = [[matrix[row_at, col_at] for col_at in range(3)] for row_at in range(3)]
    cofactor = [
        [
            entries[(row_at + 1) % 3][(col_at + 1) % 3]
            * entries[(row_at + 2) % 3][(col_at + 2) % 3]
            - entries[(row_at + 1) % 3][(col_at + 2) % 3]
            * entries[(row_at + 2) % 3][(col_at + 1) % 3]
            for col_at in range(3)
        ]
        for row_at in range(3)
    ]
    determinant = (
        entries[0][0] * cofactor[0][0]
        + entries[0][1] * cofactor[0][1]
        + entries[0][2] * cofactor[0][2]
    )
    return jnp.stack(
        [
            jnp.stack([cofactor[col_at][row_at] / determinant for col_at in range(3)])
            for row_at in range(3)
        ]
    )


def block_inverse(matrix):
    factor = {}
    for col_at in range(9):
        pivot_value = matrix[col_at, col_at]
        for middle in range(col_at):
            pivot_value = pivot_value - factor[col_at, middle] * factor[col_at, middle]
        diagonal_root = jnp.sqrt(pivot_value)
        factor[col_at, col_at] = diagonal_root
        for row_at in range(col_at + 1, 9):
            running = matrix[row_at, col_at]
            for middle in range(col_at):
                running = running - factor[row_at, middle] * factor[col_at, middle]
            factor[row_at, col_at] = running / diagonal_root
    factor_inverse = {}
    for row_at in range(9):
        factor_inverse[row_at, row_at] = 1.0 / factor[row_at, row_at]
        for col_at in range(row_at):
            running = factor[row_at, col_at] * factor_inverse[col_at, col_at]
            for middle in range(col_at + 1, row_at):
                running = running + factor[row_at, middle] * factor_inverse[middle, col_at]
            factor_inverse[row_at, col_at] = -running / factor[row_at, row_at]
    result_rows = []
    for row_at in range(9):
        entries = []
        for col_at in range(9):
            running = (
                factor_inverse[max(row_at, col_at), row_at]
                * factor_inverse[max(row_at, col_at), col_at]
            )
            for middle in range(max(row_at, col_at) + 1, 9):
                running = running + factor_inverse[middle, row_at] * factor_inverse[middle, col_at]
            entries.append(running)
        result_rows.append(jnp.stack(entries))
    return jnp.stack(result_rows)


def assemble(packed):
    positions = {}
    for index_at, pair in enumerate(block_pairs):
        positions[pair[0], pair[1]] = index_at
        positions[pair[1], pair[0]] = index_at
    return jnp.stack(
        [
            jnp.stack(
                [
                    packed[positions[row_at, col_at]] + (damping if row_at == col_at else 0.0)
                    for col_at in range(9)
                ]
            )
            for row_at in range(9)
        ]
    )


def apply_blocks(inverse_blocks, vector):
    return jnp.sum(inverse_blocks * vector[None], axis=1)


def slot_basics(camera_jacobian, point_jacobian, residuals, track_length):
    tracks = camera_jacobian.shape[1]
    in_track = (jnp.arange(tracks, dtype=jnp.int32)[:, None] < track_length[None, :]).astype(
        jnp.float32
    )
    camera_blocks = camera_jacobian.reshape(2, 9, tracks, -1) * in_track
    point_blocks = point_jacobian.reshape(2, 3, tracks, -1) * in_track
    errors = residuals * in_track
    coupling = jnp.sum(camera_blocks[:, :, None] * point_blocks[:, None], axis=0)
    point_system = jnp.sum(point_blocks[:, :, None] * point_blocks[:, None], axis=(0, 3))
    point_system = point_system + damping * jnp.eye(3, dtype=jnp.float32)[:, :, None]
    point_inverse = inverse_small(point_system)
    point_gradient = -jnp.sum(point_blocks * errors[:, None], axis=(0, 2))
    return (camera_blocks, errors, coupling, point_inverse, point_gradient)


def camera_terms(camera_blocks, errors, coupling, point_inverse, point_gradient):
    solved = jnp.sum(point_inverse * point_gradient[None], axis=1)
    scaled = coupling[:, 0][:, None] * point_inverse[0][None, :, None, :]
    for middle in range(1, 3):
        scaled = scaled + coupling[:, middle][:, None] * point_inverse[middle][None, :, None, :]
    packed = []
    for leading, trailing in block_pairs:
        packed.append(
            jnp.sum(camera_blocks[:, leading] * camera_blocks[:, trailing], axis=0)
            - jnp.sum(scaled[leading] * coupling[trailing], axis=0)
        )
    right_side = -jnp.sum(camera_blocks * errors[:, None], axis=0) - jnp.sum(
        coupling * solved[None, :, None], axis=1
    )
    return jnp.concatenate([jnp.stack(packed), right_side], axis=0)


def slot_product(camera_blocks, coupling, point_inverse, gathered):
    projected = jnp.sum(camera_blocks * gathered[None], axis=1)
    pulled = jnp.sum(coupling * gathered[:, None], axis=(0, 2))
    solved = jnp.sum(point_inverse * pulled[None], axis=1)
    return jnp.sum(camera_blocks * projected[:, None], axis=0) - jnp.sum(
        coupling * solved[None, :, None], axis=1
    )


def by_dense(camera_jacobian, point_jacobian, residuals, observed_camera, track_length):
    camera_blocks, errors, coupling, point_inverse, point_gradient = slot_basics(
        camera_jacobian, point_jacobian, residuals, track_length
    )
    tracks, points = observed_camera.shape
    rows, cols = lax.axis_size("row"), lax.axis_size("col")
    cameras = CAM_DEV * rows * cols
    flat_cameras = observed_camera.reshape(-1)

    def into_cameras(values):
        width = values.shape[0]
        by_camera = (
            jnp.zeros((cameras, width), jnp.float32).at[flat_cameras].add(jnp.transpose(values))
        )
        return jnp.transpose(by_camera)

    def pick_slots(whole):
        slot_rows = jnp.transpose(whole)[flat_cameras]
        return jnp.transpose(slot_rows).reshape(9, tracks, points)

    def spread_out(value):
        copies = jnp.broadcast_to(value[:, None], (9, OWNERS, CAM_DEV)).reshape(9, cameras)
        return lax.all_to_all(copies, ("row", "col"), split_axis=1, concat_axis=1, tiled=True)

    term_values = camera_terms(
        camera_blocks, errors, coupling, point_inverse, point_gradient
    ).reshape(54, -1)
    local_terms = into_cameras(term_values).reshape(54, rows * cols, CAM_DEV)
    own_terms = jnp.sum(
        lax.all_to_all(local_terms, ("row", "col"), split_axis=1, concat_axis=1, tiled=True), axis=1
    )
    inverse_blocks = block_inverse(assemble(own_terms[:45]))
    right_side = own_terms[45:]

    first = apply_blocks(inverse_blocks, right_side)
    first_slots = pick_slots(spread_out(first))
    first_pulled = jnp.sum(coupling * first_slots[:, None], axis=(0, 2))
    contrib = slot_product(camera_blocks, coupling, point_inverse, first_slots)
    local_image = into_cameras(contrib.reshape(9, -1)).reshape(9, OWNERS, CAM_DEV)
    gathered_image = lax.all_to_all(
        local_image, ("row", "col"), split_axis=1, concat_axis=1, tiled=True
    )
    first_image = damping * first + jnp.sum(gathered_image, axis=1)

    second = apply_blocks(inverse_blocks, first_image)
    second_slots = pick_slots(spread_out(second))
    second_pulled = jnp.sum(coupling * second_slots[:, None], axis=(0, 2))
    projected = jnp.sum(camera_blocks * second_slots[None], axis=1)
    solved = jnp.sum(point_inverse * second_pulled[None], axis=1)
    own_sums = jnp.stack(
        [
            jnp.sum(right_side * first),
            jnp.sum(first * first_image),
            jnp.sum(first_image * second),
            jnp.sum(second * second)
            + jnp.sum(projected * projected)
            - jnp.sum(second_pulled * solved),
        ]
    )
    spread = jnp.broadcast_to(own_sums[None], (OWNERS, 4))
    energy, curvature, crossed, second_curvature = jnp.sum(exchange(spread), axis=0)
    step_size = energy / curvature
    renewed = step_size * step_size * crossed - energy
    ratio = 1.0 + renewed / energy
    second_step = renewed / (
        ratio * ratio * curvature
        - 2.0 * step_size * ratio * crossed
        + step_size * step_size * second_curvature
    )
    first_weight = step_size + second_step * ratio
    second_weight = -second_step * step_size
    camera_move = first_weight * first + second_weight * second
    pulled = first_weight * first_pulled + second_weight * second_pulled
    point_move = jnp.sum(point_inverse * (point_gradient - pulled)[None], axis=1)
    return (camera_move, point_move)


def on_device(camera_jacobian, point_jacobian, residuals, observed_camera, track_length):
    operands = (camera_jacobian, point_jacobian, residuals, observed_camera, track_length)
    overflow, kept = by_slots(*operands)
    return lax.cond(
        overflow > 0,
        lambda given, unused: by_dense(*given),
        lambda unused, found: finish(*found),
        operands,
        kept,
    )


def solution(mesh):
    in_specs = (
        P(None, None, ("row", "col")),
        P(None, None, ("row", "col")),
        P(None, None, ("row", "col")),
        P(None, ("row", "col")),
        P(("row", "col")),
    )
    out_specs = (P(None, ("row", "col")), P(None, ("row", "col")))
    return jax.shard_map(
        on_device, mesh=mesh, in_specs=in_specs, out_specs=out_specs, check_vma=False
    )
```

```python
import jax
import jax.numpy as jnp
from jax import lax
from jax.experimental import pallas as pl
from jax.experimental.pallas import tpu as pltpu
from jax.sharding import PartitionSpec as P

CAM_DEV = 384
TRACK = 8
PT_DEV = 1024
OWNERS = 128
LANES = 128
WIDTH = 21
GROUPS = 6
ROWS = 13
CAP = GROUPS * ROWS
SPAN = 80
FEW = 64
CAMERA_AT = 20
ENTRIES = 56
COUNT_AT = GROUPS * WIDTH
BLOCKS = TRACK * PT_DEV // LANES

F32 = jnp.float32
BF16 = jnp.bfloat16
PARAMS = pltpu.CompilerParams(vmem_limit_bytes=48 * 2**20)
block_pairs = [(leading, trailing) for leading in range(9) for trailing in range(leading, 9)]


def iota(shape, axis):
    return lax.broadcasted_iota(jnp.int32, shape, axis)


def two_parts(value):
    high = value.astype(BF16)
    low = (value - high.astype(F32)).astype(BF16)
    return high, low


def dot(left, right):
    return jnp.dot(left, right, preferred_element_type=F32)


def dot_lanes(left, right):
    return lax.dot_general(left, right, (((1,), (1,)), ((), ())), preferred_element_type=F32)


def total(value):
    return jnp.sum(jnp.sum(value, axis=0, keepdims=True), axis=1, keepdims=True)


def over_tracks(value):
    return jnp.sum(value, axis=0, keepdims=True)


def used_slots(length_ref, lanes):
    return iota((TRACK, LANES), 0) < length_ref[:, lanes]


def times_inverse(inverse, vector):
    v00, v01, v02, v11, v12, v22 = inverse
    x, y, z = vector
    return [v00 * x + v01 * y + v02 * z, v01 * x + v11 * y + v12 * z, v02 * x + v12 * y + v22 * z]


def owner_of(camera):
    return ((camera >> 7) * 171) >> 9


def prepare_kernel(camera_in, point_in, error_in, index_ref, length_ref, out_ref, route_ref, state_ref, root_ref, flag_ref, owned_ref, masked_ref, camera_ref, point_ref, error_ref, pay_ref, code_ref, near_ref, slot_ref, block_ref, camera_sem, point_sem, error_sem, code_sem):
    copies = [
        pltpu.make_async_copy(camera_in, camera_ref, camera_sem),
        pltpu.make_async_copy(point_in, point_ref, point_sem),
        pltpu.make_async_copy(error_in, error_ref, error_sem),
    ]
    for copy in copies:
        copy.start()
    used = iota((TRACK, PT_DEV), 0) < length_ref[...]
    route_ref[0:TRACK, :] = jnp.where(used, owner_of(index_ref[...]), OWNERS)

    step = 256
    upto = jnp.where(iota((step, step), 0) <= iota((step, step), 1), 1.0, 0.0).astype(BF16)
    before = jnp.zeros((OWNERS, step), F32)
    names = iota((OWNERS, step), 0)
    for s in range(TRACK):
        for chunk in range(PT_DEV // step):
            lanes = slice(chunk * step, (chunk + 1) * step)
            chosen = names == route_ref[s : s + 1, lanes]
            hot = jnp.where(chosen, 1.0, 0.0).astype(BF16)
            owned_ref[s, :, lanes] = hot
            counts = dot(hot, upto)
            rank = jnp.sum(jnp.where(chosen, counts + before, 0.0), axis=0, keepdims=True) - 1.0
            before = before + jnp.broadcast_to(counts[:, step - 1 : step], (OWNERS, step))
            route_ref[TRACK + s : TRACK + s + 1, lanes] = rank.astype(jnp.int32)

    owner = route_ref[0:TRACK, :]
    rank = route_ref[TRACK : 2 * TRACK, :]
    fits = (owner < OWNERS) & (rank < CAP)
    row_at = (rank * 171) >> 10
    place = (rank - row_at * GROUPS) * (OWNERS * ROWS) + owner * ROWS + row_at
    code = jnp.where(fits, place, GROUPS * OWNERS * ROWS)
    for chunk in range(PT_DEV // LANES):
        code_ref[chunk * TRACK : (chunk + 1) * TRACK, :] = code[:, chunk * LANES : (chunk + 1) * LANES]
    code_copy = pltpu.make_async_copy(code_ref, near_ref, code_sem)
    code_copy.start()
    most = jnp.max(jnp.max(before, axis=0, keepdims=True), axis=1, keepdims=True)
    lane = iota((OWNERS, LANES), 1)
    flag_ref[...] = jnp.where(lane > COUNT_AT, most, before[:, 0:LANES])
    for copy in copies:
        copy.wait()
    for chunk in range(PT_DEV // LANES):
        lanes = slice(chunk * LANES, (chunk + 1) * LANES)
        used = used_slots(length_ref, lanes)
        point = [
            [jnp.where(used, point_ref[3 * i + a, :, lanes], 0.0) for a in range(3)] for i in range(2)
        ]
        for i in range(2):
            for a in range(3):
                masked_ref[3 * i + a, :, lanes] = point[i][a]
        error = [jnp.where(used, error_ref[i, :, lanes], 0.0) for i in range(2)]

        def pair(a, b):
            return over_tracks(point[0][a] * point[0][b] + point[1][a] * point[1][b])

        s00, s01, s02 = 1.0 + pair(0, 0), pair(0, 1), pair(0, 2)
        s11, s12, s22 = 1.0 + pair(1, 1), pair(1, 2), 1.0 + pair(2, 2)
        c00 = s11 * s22 - s12 * s12
        c01 = s12 * s02 - s01 * s22
        c02 = s01 * s12 - s11 * s02
        c11 = s22 * s00 - s02 * s02
        c12 = s02 * s01 - s12 * s00
        c22 = s00 * s11 - s01 * s01
        determinant = s00 * c00 + s01 * c01 + s02 * c02
        scale = 1.0 / determinant
        inverse = [c * scale for c in (c00, c01, c02, c11, c12, c22)]
        gradient = [
            -over_tracks(point[0][a] * error[0] + point[1][a] * error[1]) for a in range(3)
        ]
        for at, value in enumerate(inverse + gradient):
            state_ref[at : at + 1, lanes] = value
        solved = times_inverse(inverse, gradient)
        u0 = times_inverse(inverse, point[0])
        u1 = times_inverse(inverse, point[1])

        def along(left, right):
            return left[0] * right[0] + left[1] * right[1] + left[2] * right[2]

        camera = index_ref[:, lanes]
        owner = owner_of(camera)
        local = camera - owner * CAM_DEV
        b01 = -along(u0, point[1])
        root0 = jnp.sqrt(1.0 - along(u0, point[0]))
        root1 = b01 / root0
        root2 = jnp.sqrt(1.0 - along(u1, point[1]) - root1 * root1)
        inverse0, inverse2 = 1.0 / root0, 1.0 / root2
        side0 = (error[0] + along(solved, point[0])) * inverse0
        side1 = (error[1] + along(solved, point[1]) - root1 * side0) * inverse2
        values = [root0 * camera_ref[j, :, lanes] + root1 * camera_ref[9 + j, :, lanes] for j in range(9)]
        values += [root2 * camera_ref[9 + j, :, lanes] for j in range(9)]
        values += [side0, side1, (local + 1).astype(F32)]
        for at, value in enumerate((inverse0, root1, inverse2)):
            root_ref[at * TRACK : (at + 1) * TRACK, lanes] = value
        for f in range(WIDTH):
            at = (chunk * WIDTH + f) * TRACK
            pay_ref[at : at + TRACK, :] = values[f]
    dispatch(near_ref, pay_ref, flag_ref, out_ref, slot_ref, block_ref, code_copy)


def dispatch(code_ref, pay_ref, flag_ref, out_ref, slot_ref, block_ref, code_copy):
    rows = OWNERS * ROWS
    zeros = jnp.zeros((8, LANES), F32)
    slots_ref = slot_ref.reshape(BLOCKS * LANES, LANES)
    blocks_ref = block_ref.reshape(GROUPS * rows + 8, LANES)

    share = -(-GROUPS * rows // (BLOCKS * 8)) * 8
    within = iota((LANES, LANES), 1) % WIDTH
    for first in range(0, BLOCKS, GROUPS):
        blocks = []
        for block in range(first, first + GROUPS):
            chunk, s = divmod(block, TRACK)
            if block < BLOCKS:
                blocks.append(pay_ref[pl.ds(chunk * WIDTH * TRACK + s, WIDTH, stride=TRACK), :])
            else:
                blocks.append(jnp.zeros((WIDTH, LANES), F32))
        turned = jnp.transpose(jnp.concatenate(blocks + [zeros[0 : LANES - COUNT_AT]], axis=0))
        for block in range(first, min(first + GROUPS, BLOCKS)):
            slots_ref[block * LANES : (block + 1) * LANES, :] = jnp.take_along_axis(
                turned, within + (block - first) * WIDTH, axis=1, mode="promise_in_bounds"
            )
            start = min(block * share, GROUPS * rows)
            count = min(share, GROUPS * rows - start)
            if count:
                blocks_ref[start : start + count, :] = jnp.zeros((count, LANES), F32)

    code_copy.wait()

    def place(block, carry):
        def load(start):
            columns = range(start, min(start + 16, LANES))
            return [(code_ref[block, j], slot_ref[block, j]) for j in columns]

        ready = load(0)
        for start in range(16, LANES + 16, 16):
            coming = load(start)
            for code, slot in ready:
                block_ref[code] = slot
            ready = coming
        return carry

    lax.fori_loop(0, BLOCKS, place, 0)
    group = iota((8, LANES), 1) // WIDTH

    def merge(at, carry):
        for j in range(8):
            start = pl.multiple_of(at * 64 + j * 8, 8)
            value = zeros
            for k in range(GROUPS):
                value = jnp.where(group == k, blocks_ref[pl.ds(k * rows + start, 8), :], value)
            out_ref[pl.ds(start, 8), :] = value
        return carry

    lax.fori_loop(0, rows // 64, merge, 0)
    lane = iota((OWNERS, LANES), 1)
    leading = pl.ds(0, OWNERS, stride=ROWS)
    out_ref[leading, :] = jnp.where(lane >= COUNT_AT, flag_ref[...], out_ref[leading, :])


def solve(factor, scales, vector):
    forward = []
    for i in range(9):
        value = vector[i]
        for j in range(i):
            value = value - factor[i, j] * forward[j]
        forward.append(value * scales[i])
    result = [None] * 9
    for i in reversed(range(9)):
        value = forward[i]
        for j in range(i + 1, 9):
            value = value - factor[j, i] * result[j]
        result[i] = value * scales[i]
    return result


def hot_cameras(feature_ref, hot_ref, block):
    names = iota((LANES, LANES), 0)
    for r in range(8):
        camera = feature_ref[pl.ds(CAMERA_AT * SPAN + block * 8 + r, 1), :].astype(jnp.int32) - 1
        hot = jnp.where(names == (camera & (LANES - 1)), 1.0, 0.0).astype(BF16)
        hot_ref[:, block * PT_DEV + r * LANES : block * PT_DEV + (r + 1) * LANES] = hot


def features_of(feature_ref, f, block):
    start = f * SPAN + block * 8
    return feature_ref[start : start + 8, :]


def image_slots(vector, feature_ref, table_ref, image_ref, many):
    for j in range(9):
        for c in range(3):
            at = (3 * j + c) * 8
            table_ref[at : at + 8, :] = jnp.broadcast_to(vector[j][c : c + 1, :], (8, LANES))

    def one(block):
        camera = features_of(feature_ref, CAMERA_AT, block).astype(jnp.int32) - 1
        third = camera >> 7
        lane = camera & (LANES - 1)
        images = [jnp.zeros((8, LANES), F32)] * 2
        for j in range(9):
            found = [
                jnp.take_along_axis(
                    table_ref[(3 * j + c) * 8 : (3 * j + c + 1) * 8, :],
                    lane,
                    axis=1,
                    mode="promise_in_bounds",
                )
                for c in range(3)
            ]
            value = jnp.where(third == 1, found[1], jnp.where(third == 2, found[2], found[0]))
            for i in range(2):
                images[i] = images[i] + features_of(feature_ref, 9 * i + j, block) * value
        for i in range(2):
            start = i * LANES + block * 8
            image_ref[start : start + 8, :] = images[i]

    for block in range(FEW // 8):
        one(block)

    @pl.when(many)
    def _():
        for block in range(FEW // 8, SPAN // 8):
            one(block)


def keep_parts(part_ref, feature_ref, parts_ref, block, count):
    for r in range(8):
        lanes = slice(block * PT_DEV + r * LANES, block * PT_DEV + (r + 1) * LANES)
        camera = feature_ref[pl.ds(CAMERA_AT * SPAN + block * 8 + r, 1), :].astype(jnp.int32) - 1
        value = part_ref[pl.ds(r, count, stride=8), :]
        high = value.astype(BF16).astype(F32)
        both = jnp.concatenate([high, value - high], axis=0).astype(BF16)
        third = jnp.broadcast_to(camera >> 7, (16, LANES))
        for c in range(3):
            inside = jnp.where(third == c, 1.0, 0.0).astype(BF16)
            inside = jnp.concatenate([inside] * (count // 8), axis=0)
            parts_ref[2 * c * count : 2 * (c + 1) * count, lanes] = both * inside


def camera_sums(terms, parts_ref, hot_ref, part_ref, sum_ref, count, many):
    def block_sums(block):
        terms(block)
        lanes = slice(block * PT_DEV, (block + 1) * PT_DEV)
        return dot_lanes(parts_ref[:, lanes], hot_ref[:, lanes])

    sums = block_sums(0)
    for block in range(1, FEW // 8):
        sums = sums + block_sums(block)
    sum_ref[...] = sums

    @pl.when(many)
    def _():
        for block in range(FEW // 8, SPAN // 8):
            sum_ref[...] += block_sums(block)

    part_ref[...] = jnp.zeros(part_ref.shape, F32)
    for c in range(3):
        at = 2 * c * count
        part_ref[pl.ds(c, count, stride=8), :] = (
            sum_ref[at : at + count, :] + sum_ref[at + count : at + 2 * count, :]
        )


def turn_in(got_ref, i):
    return jnp.transpose(got_ref[pl.ds(i, OWNERS, stride=2), :])


def turn_out(image_ref, out_ref):
    for i in range(2):
        out_ref[pl.ds(i, OWNERS, stride=2), :] = jnp.transpose(
            image_ref[i * LANES : (i + 1) * LANES, :]
        )


def first_camera_kernel(got_ref, feature_ref, factor_ref, first_ref, out_ref, flag_ref, hot_ref, parts_ref, table_ref, image_ref, sum_ref, part_ref):
    image_ref[...] = jnp.zeros((2 * LANES, LANES), F32)
    feature_ref[...] = jnp.zeros(feature_ref.shape, F32)

    def take_row(q):
        turned = jnp.transpose(got_ref[pl.ds(q, OWNERS, stride=ROWS), :])
        for k in range(GROUPS):
            feature_ref[pl.ds(q * GROUPS + k, WIDTH, stride=SPAN), :] = turned[
                k * WIDTH : (k + 1) * WIDTH, :
            ]
        return turned

    turned = take_row(0)
    worst = jnp.max(turned[COUNT_AT + 1 : COUNT_AT + 2, :])
    flag_ref[0, 0] = jnp.where(worst > CAP, 1, 0)
    most = jnp.max(turned[COUNT_AT : COUNT_AT + 1, :])
    many = most > FEW
    few_rows = -(-FEW // GROUPS)
    for q in range(1, few_rows):
        take_row(q)

    @pl.when(many)
    def _():
        for q in range(few_rows, ROWS):
            take_row(q)

    part_ref[...] = jnp.zeros((ENTRIES * 8, LANES), F32)

    def gather_terms(block):
        hot_cameras(feature_ref, hot_ref, block)
        f = [features_of(feature_ref, at, block) for at in range(20)]
        for at, (j, k) in enumerate(block_pairs):
            part_ref[at * 8 : (at + 1) * 8, :] = f[j] * f[k] + f[9 + j] * f[9 + k]
        for j in range(9):
            part_ref[(45 + j) * 8 : (46 + j) * 8, :] = -(f[j] * f[18] + f[9 + j] * f[19])
        keep_parts(part_ref, feature_ref, parts_ref, block, ENTRIES)

    camera_sums(gather_terms, parts_ref, hot_ref, part_ref, sum_ref, ENTRIES, many)
    matrix = {}
    for at, (j, k) in enumerate(block_pairs):
        entry = part_ref[at * 8 : (at + 1) * 8, :]
        matrix[k, j] = entry + 1.0 if j == k else entry
    side = [part_ref[(45 + j) * 8 : (46 + j) * 8, :] for j in range(9)]
    factor, scales = {}, []
    for j in range(9):
        pivot = matrix[j, j]
        for m in range(j):
            pivot = pivot - factor[j, m] * factor[j, m]
        scales.append(1.0 / jnp.sqrt(pivot))
        for i in range(j + 1, 9):
            running = matrix[i, j]
            for m in range(j):
                running = running - factor[i, m] * factor[j, m]
            factor[i, j] = running * scales[j]
    for at, (j, k) in enumerate(block_pairs):
        factor_ref[at * 8 : (at + 1) * 8, :] = scales[j] if j == k else factor[k, j]
    first = solve(factor, scales, side)
    energy = side[0] * first[0]
    for j in range(1, 9):
        energy = energy + side[j] * first[j]
    for j in range(9):
        first_ref[j * 8 : (j + 1) * 8, :] = first[j]
    first_ref[72:80, :] = energy
    first_ref[80:88, :] = jnp.broadcast_to(jnp.max(turned[COUNT_AT : COUNT_AT + 1, :], axis=1, keepdims=True), (8, LANES))
    image_slots(first, feature_ref, table_ref, image_ref, many)
    turn_out(image_ref, out_ref)


def either_span(flag_ref, work):
    many = jnp.max(flag_ref[0:8, :]) > FEW
    pl.when(many)(lambda: work(SPAN))
    pl.when(jnp.logical_not(many))(lambda: work(FEW))


def pull_slots(got_ref, route_ref, masked_ref, state_ref, root_ref, owned_ref, value_ref, pulled_ref, curve_ref, span, back):
    images = []
    for i in range(2):
        images.append(turn_in(got_ref, i)[0:span, :])
    high, low = two_parts(jnp.concatenate(images, axis=0))
    parts = jnp.concatenate([high, low], axis=1)
    ranks = iota((span, PT_DEV), 0)
    for s in range(TRACK):
        hot = owned_ref[s]
        got = dot(parts, jnp.concatenate([hot, hot], axis=0))
        here = ranks == route_ref[TRACK + s : TRACK + s + 1, :]
        for i in range(2):
            value_ref[i * TRACK + s : i * TRACK + s + 1, :] = jnp.sum(
                jnp.where(here, got[i * span : (i + 1) * span, :], 0.0), axis=0, keepdims=True
            )
    curve = jnp.zeros((TRACK, LANES), F32)
    for chunk in range(PT_DEV // LANES):
        lanes = slice(chunk * LANES, (chunk + 1) * LANES)
        point = [[masked_ref[3 * i + a, :, lanes] for a in range(3)] for i in range(2)]
        root = [root_ref[at * TRACK : (at + 1) * TRACK, lanes] for at in range(3)]
        image1 = value_ref[TRACK : 2 * TRACK, lanes] * root[2]
        image = [(value_ref[0:TRACK, lanes] - root[1] * image1) * root[0], image1]
        pulled = [over_tracks(point[0][a] * image[0] + point[1][a] * image[1]) for a in range(3)]
        inverse = [state_ref[at : at + 1, lanes] for at in range(6)]
        solved = times_inverse(inverse, pulled)
        for a in range(3):
            pulled_ref[a : a + 1, lanes] = pulled[a]
        result = [
            image[i] - (point[i][0] * solved[0] + point[i][1] * solved[1] + point[i][2] * solved[2])
            for i in range(2)
        ]
        if back:
            result0 = result[0] * root[0]
            value_ref[0:TRACK, lanes] = result0
            value_ref[TRACK : 2 * TRACK, lanes] = (result[1] - root[1] * result0) * root[2]
        else:
            curve = curve + image[0] * result[0] + image[1] * result[1]
    if not back:
        curve_ref[...] = curve


def first_point_kernel(got_ref, route_ref, masked_ref, state_ref, root_ref, flag_ref, owned_ref, pulled_ref, out_ref, value_ref, image_ref):
    image_ref[...] = jnp.zeros((2 * LANES, LANES), F32)

    def work(span):
        pull_slots(got_ref, route_ref, masked_ref, state_ref, root_ref, owned_ref, value_ref, pulled_ref, None, span, True)
        ranks = iota((span, PT_DEV), 0)
        sums = jnp.zeros((4 * span, OWNERS), F32)
        for s in range(TRACK):
            here = ranks == route_ref[TRACK + s : TRACK + s + 1, :]
            spread = []
            for i in range(2):
                value = value_ref[i * TRACK + s : i * TRACK + s + 1, :]
                spread.append(jnp.where(here, value, 0.0))
            high, low = two_parts(jnp.concatenate(spread, axis=0))
            sums = sums + dot_lanes(jnp.concatenate([high, low], axis=0), owned_ref[s])
        sums = sums[0 : 2 * span] + sums[2 * span :]
        for i in range(2):
            image_ref[i * LANES : i * LANES + span, :] = sums[i * span : (i + 1) * span, :]

    either_span(flag_ref, work)
    turn_out(image_ref, out_ref)


def second_point_kernel(got_ref, route_ref, masked_ref, state_ref, root_ref, flag_ref, owned_ref, pulled_ref, out_ref, scalar_ref, value_ref, curve_ref):
    def work(span):
        pull_slots(got_ref, route_ref, masked_ref, state_ref, root_ref, owned_ref, value_ref, pulled_ref, curve_ref, span, False)

    either_span(flag_ref, work)
    out_ref[...] = jnp.broadcast_to(total(curve_ref[...]), (OWNERS, LANES))
    scalar_ref[...] = jnp.broadcast_to(
        jnp.sum(got_ref[pl.ds(0, OWNERS, stride=2), :], axis=0, keepdims=True), (8, LANES)
    )


def second_camera_kernel(got_ref, feature_ref, factor_ref, first_ref, second_ref, out_ref, hot_ref, parts_ref, table_ref, image_ref, sum_ref, wide_ref):
    for i in range(2):
        image_ref[i * LANES : (i + 1) * LANES, :] = turn_in(got_ref, i)
    many = jnp.max(first_ref[80:88, :]) > FEW
    wide_ref[...] = jnp.zeros((LANES, LANES), F32)

    def gather_terms(block):
        hot_cameras(feature_ref, hot_ref, block)
        back = [
            image_ref[i * LANES + block * 8 : i * LANES + (block + 1) * 8, :] for i in range(2)
        ]
        for j in range(9):
            wide_ref[j * 8 : (j + 1) * 8, :] = (
                features_of(feature_ref, j, block) * back[0]
                + features_of(feature_ref, 9 + j, block) * back[1]
            )
        keep_parts(wide_ref, feature_ref, parts_ref, block, 16)

    camera_sums(gather_terms, parts_ref, hot_ref, wide_ref, sum_ref, 16, many)
    first = [first_ref[j * 8 : (j + 1) * 8, :] for j in range(9)]
    image = [first[j] + wide_ref[j * 8 : (j + 1) * 8, :] for j in range(9)]
    factor, scales = {}, []
    for at, (j, k) in enumerate(block_pairs):
        entry = factor_ref[at * 8 : (at + 1) * 8, :]
        if j == k:
            scales.append(entry)
        else:
            factor[k, j] = entry
    second = solve(factor, scales, image)
    for j in range(9):
        second_ref[j * 8 : (j + 1) * 8, :] = second[j]

    def inner(left, right):
        value = left[0] * right[0]
        for j in range(1, 9):
            value = value + left[j] * right[j]
        return value

    image_slots(second, feature_ref, table_ref, image_ref, many)
    scalars = [first_ref[72:80, :], inner(first, image), inner(image, second), inner(second, second)]
    for at, value in enumerate(scalars):
        image_ref[SPAN + at : SPAN + at + 1, :] = jnp.broadcast_to(total(value), (1, LANES))
    turn_out(image_ref, out_ref)


def finish_kernel(curve_ref, scalar_ref, first_ref, second_ref, state_ref, first_pulled_ref, second_pulled_ref, camera_out, point_out, camera_ref, point_ref, camera_sem, point_sem):
    own = jnp.sum(curve_ref[...], axis=0, keepdims=True)[:, 0:1]
    energy, curvature, crossed, square = [
        scalar_ref[0:1, SPAN + at : SPAN + at + 1] for at in range(4)
    ]
    step_size = energy / curvature
    renewed = step_size * step_size * crossed - energy
    ratio = 1.0 + renewed / energy
    second_step = renewed / (
        ratio * ratio * curvature
        - 2.0 * step_size * ratio * crossed
        + step_size * step_size * (square + own)
    )
    first_weight = step_size + second_step * ratio
    second_weight = -second_step * step_size
    for c in range(3):
        camera_ref[:, c * LANES : (c + 1) * LANES] = (
            first_weight * first_ref[pl.ds(c, 9, stride=8), :]
            + second_weight * second_ref[pl.ds(c, 9, stride=8), :]
        )
    camera_copy = pltpu.make_async_copy(camera_ref, camera_out, camera_sem)
    camera_copy.start()
    left = [
        state_ref[6 + a : 7 + a, :]
        - first_weight * first_pulled_ref[a : a + 1, :]
        - second_weight * second_pulled_ref[a : a + 1, :]
        for a in range(3)
    ]
    moved = times_inverse([state_ref[at : at + 1, :] for at in range(6)], left)
    for a in range(3):
        point_ref[a : a + 1, :] = moved[a]
    point_copy = pltpu.make_async_copy(point_ref, point_out, point_sem)
    point_copy.start()
    camera_copy.wait()
    point_copy.wait()


def call(kernel, outs, scratch, operands, in_scalar=0):
    specs = [
        pl.BlockSpec(memory_space=pltpu.SMEM if at < in_scalar else pltpu.VMEM)
        for at in range(len(operands))
    ]
    return pl.pallas_call(
        kernel,
        out_shape=[jax.ShapeDtypeStruct(shape, dtype) for shape, dtype in outs],
        in_specs=specs,
        out_specs=[
            pl.BlockSpec(memory_space=pltpu.SMEM if shape == (1, 1) else pltpu.VMEM)
            for shape, unused in outs
        ],
        scratch_shapes=[pltpu.VMEM(shape, dtype) for shape, dtype in scratch],
        compiler_params=PARAMS,
    )(*operands)


def exchange(rows):
    blocks = rows.reshape(OWNERS, 1, -1)
    blocks = lax.all_to_all(blocks, ("row", "col"), split_axis=0, concat_axis=0, tiled=True)
    return blocks.reshape(rows.shape)


def by_slots(camera_jacobian, point_jacobian, residuals, observed_camera, track_length):
    lengths = track_length.reshape(1, PT_DEV)
    in_vmem = [pl.BlockSpec(memory_space=pltpu.VMEM)]
    held = [(18, TRACK, PT_DEV), (6, TRACK, PT_DEV), (2, TRACK, PT_DEV)]
    outs = [
        ((OWNERS * ROWS, LANES), F32),
        ((2 * TRACK, PT_DEV), jnp.int32),
        ((16, PT_DEV), F32),
        ((3 * TRACK, PT_DEV), F32),
        ((OWNERS, LANES), F32),
        ((TRACK, OWNERS, PT_DEV), BF16),
        ((6, TRACK, PT_DEV), F32),
    ]
    sent, route, state, root, flag, owned, masked = pl.pallas_call(
        prepare_kernel,
        out_shape=[jax.ShapeDtypeStruct(shape, dtype) for shape, dtype in outs],
        in_specs=[pl.BlockSpec(memory_space=pl.ANY)] * 3 + in_vmem * 2,
        out_specs=in_vmem * len(outs),
        scratch_shapes=[pltpu.VMEM(shape, F32) for shape in held]
        + [
            pltpu.VMEM((WIDTH * BLOCKS, LANES), F32),
            pltpu.VMEM((BLOCKS, LANES), jnp.int32),
            pltpu.SMEM((BLOCKS, LANES), jnp.int32),
            pltpu.VMEM((BLOCKS, LANES, 1, LANES), F32),
            pltpu.VMEM((GROUPS * OWNERS * ROWS + 8, 1, LANES), F32),
        ]
        + [pltpu.SemaphoreType.DMA] * 4,
        compiler_params=PARAMS,
    )(camera_jacobian, point_jacobian, residuals, observed_camera, lengths)
    hot = ((LANES, SPAN * LANES), BF16)
    table = ((27 * 8, LANES), F32)
    image = ((2 * LANES, LANES), F32)
    pair = ((2 * OWNERS, LANES), F32)
    features, factor, first, out, overflow = call(
        first_camera_kernel,
        [((WIDTH * SPAN, LANES), F32), ((45 * 8, LANES), F32), ((88, LANES), F32), pair, ((1, 1), jnp.int32)],
        [hot, ((6 * ENTRIES, SPAN * LANES), BF16), table, image, ((6 * ENTRIES, LANES), F32), ((ENTRIES * 8, LANES), F32)],
        (exchange(sent),),
    )
    first_pulled, out = call(
        first_point_kernel,
        [((8, PT_DEV), F32), pair],
        [((2 * TRACK, PT_DEV), F32), image],
        (exchange(out), route, masked, state, root, flag, owned),
    )
    second, out = call(
        second_camera_kernel,
        [((72, LANES), F32), pair],
        [hot, ((96, SPAN * LANES), BF16), table, image, ((96, LANES), F32), ((LANES, LANES), F32)],
        (exchange(out), features, factor, first),
    )
    second_pulled, curve, scalars = call(
        second_point_kernel,
        [((8, PT_DEV), F32), ((OWNERS, LANES), F32), ((8, LANES), F32)],
        [((2 * TRACK, PT_DEV), F32), ((TRACK, LANES), F32)],
        (exchange(out), route, masked, state, root, flag, owned),
    )
    return overflow[0, 0], (exchange(curve), scalars, first, second, state, first_pulled, second_pulled)


def finish(*operands):
    shapes = [(9, CAM_DEV), (3, PT_DEV)]
    return tuple(
        pl.pallas_call(
            finish_kernel,
            out_shape=[jax.ShapeDtypeStruct(shape, F32) for shape in shapes],
            in_specs=[pl.BlockSpec(memory_space=pltpu.VMEM)] * len(operands),
            out_specs=[pl.BlockSpec(memory_space=pltpu.HBM)] * 2,
            scratch_shapes=[pltpu.VMEM(shape, F32) for shape in shapes]
            + [pltpu.SemaphoreType.DMA] * 2,
            compiler_params=PARAMS,
        )(*operands)
    )


damping = 1.0


def inverse_small(matrix):
    entries = [[matrix[row_at, col_at] for col_at in range(3)] for row_at in range(3)]
    cofactor = [
        [
            entries[(row_at + 1) % 3][(col_at + 1) % 3]
            * entries[(row_at + 2) % 3][(col_at + 2) % 3]
            - entries[(row_at + 1) % 3][(col_at + 2) % 3]
            * entries[(row_at + 2) % 3][(col_at + 1) % 3]
            for col_at in range(3)
        ]
        for row_at in range(3)
    ]
    determinant = (
        entries[0][0] * cofactor[0][0]
        + entries[0][1] * cofactor[0][1]
        + entries[0][2] * cofactor[0][2]
    )
    return jnp.stack(
        [
            jnp.stack([cofactor[col_at][row_at] / determinant for col_at in range(3)])
            for row_at in range(3)
        ]
    )


def block_inverse(matrix):
    factor = {}
    for col_at in range(9):
        pivot_value = matrix[col_at, col_at]
        for middle in range(col_at):
            pivot_value = pivot_value - factor[col_at, middle] * factor[col_at, middle]
        diagonal_root = jnp.sqrt(pivot_value)
        factor[col_at, col_at] = diagonal_root
        for row_at in range(col_at + 1, 9):
            running = matrix[row_at, col_at]
            for middle in range(col_at):
                running = running - factor[row_at, middle] * factor[col_at, middle]
            factor[row_at, col_at] = running / diagonal_root
    factor_inverse = {}
    for row_at in range(9):
        factor_inverse[row_at, row_at] = 1.0 / factor[row_at, row_at]
        for col_at in range(row_at):
            running = factor[row_at, col_at] * factor_inverse[col_at, col_at]
            for middle in range(col_at + 1, row_at):
                running = running + factor[row_at, middle] * factor_inverse[middle, col_at]
            factor_inverse[row_at, col_at] = -running / factor[row_at, row_at]
    result_rows = []
    for row_at in range(9):
        entries = []
        for col_at in range(9):
            running = (
                factor_inverse[max(row_at, col_at), row_at]
                * factor_inverse[max(row_at, col_at), col_at]
            )
            for middle in range(max(row_at, col_at) + 1, 9):
                running = running + factor_inverse[middle, row_at] * factor_inverse[middle, col_at]
            entries.append(running)
        result_rows.append(jnp.stack(entries))
    return jnp.stack(result_rows)


def assemble(packed):
    positions = {}
    for index_at, pair in enumerate(block_pairs):
        positions[pair[0], pair[1]] = index_at
        positions[pair[1], pair[0]] = index_at
    return jnp.stack(
        [
            jnp.stack(
                [
                    packed[positions[row_at, col_at]] + (damping if row_at == col_at else 0.0)
                    for col_at in range(9)
                ]
            )
            for row_at in range(9)
        ]
    )


def apply_blocks(inverse_blocks, vector):
    return jnp.sum(inverse_blocks * vector[None], axis=1)


def slot_basics(camera_jacobian, point_jacobian, residuals, track_length):
    tracks = camera_jacobian.shape[1]
    in_track = (jnp.arange(tracks, dtype=jnp.int32)[:, None] < track_length[None, :]).astype(
        jnp.float32
    )
    camera_blocks = camera_jacobian.reshape(2, 9, tracks, -1) * in_track
    point_blocks = point_jacobian.reshape(2, 3, tracks, -1) * in_track
    errors = residuals * in_track
    coupling = jnp.sum(camera_blocks[:, :, None] * point_blocks[:, None], axis=0)
    point_system = jnp.sum(point_blocks[:, :, None] * point_blocks[:, None], axis=(0, 3))
    point_system = point_system + damping * jnp.eye(3, dtype=jnp.float32)[:, :, None]
    point_inverse = inverse_small(point_system)
    point_gradient = -jnp.sum(point_blocks * errors[:, None], axis=(0, 2))
    return (camera_blocks, errors, coupling, point_inverse, point_gradient)


def camera_terms(camera_blocks, errors, coupling, point_inverse, point_gradient):
    solved = jnp.sum(point_inverse * point_gradient[None], axis=1)
    scaled = coupling[:, 0][:, None] * point_inverse[0][None, :, None, :]
    for middle in range(1, 3):
        scaled = scaled + coupling[:, middle][:, None] * point_inverse[middle][None, :, None, :]
    packed = []
    for leading, trailing in block_pairs:
        packed.append(
            jnp.sum(camera_blocks[:, leading] * camera_blocks[:, trailing], axis=0)
            - jnp.sum(scaled[leading] * coupling[trailing], axis=0)
        )
    right_side = -jnp.sum(camera_blocks * errors[:, None], axis=0) - jnp.sum(
        coupling * solved[None, :, None], axis=1
    )
    return jnp.concatenate([jnp.stack(packed), right_side], axis=0)


def slot_product(camera_blocks, coupling, point_inverse, gathered):
    projected = jnp.sum(camera_blocks * gathered[None], axis=1)
    pulled = jnp.sum(coupling * gathered[:, None], axis=(0, 2))
    solved = jnp.sum(point_inverse * pulled[None], axis=1)
    return jnp.sum(camera_blocks * projected[:, None], axis=0) - jnp.sum(
        coupling * solved[None, :, None], axis=1
    )


def by_dense(camera_jacobian, point_jacobian, residuals, observed_camera, track_length):
    camera_blocks, errors, coupling, point_inverse, point_gradient = slot_basics(
        camera_jacobian, point_jacobian, residuals, track_length
    )
    tracks, points = observed_camera.shape
    rows, cols = lax.axis_size("row"), lax.axis_size("col")
    cameras = CAM_DEV * rows * cols
    flat_cameras = observed_camera.reshape(-1)

    def into_cameras(values):
        width = values.shape[0]
        by_camera = (
            jnp.zeros((cameras, width), jnp.float32).at[flat_cameras].add(jnp.transpose(values))
        )
        return jnp.transpose(by_camera)

    def pick_slots(whole):
        slot_rows = jnp.transpose(whole)[flat_cameras]
        return jnp.transpose(slot_rows).reshape(9, tracks, points)

    def spread_out(value):
        copies = jnp.broadcast_to(value[:, None], (9, OWNERS, CAM_DEV)).reshape(9, cameras)
        return lax.all_to_all(copies, ("row", "col"), split_axis=1, concat_axis=1, tiled=True)

    term_values = camera_terms(
        camera_blocks, errors, coupling, point_inverse, point_gradient
    ).reshape(54, -1)
    local_terms = into_cameras(term_values).reshape(54, rows * cols, CAM_DEV)
    own_terms = jnp.sum(
        lax.all_to_all(local_terms, ("row", "col"), split_axis=1, concat_axis=1, tiled=True), axis=1
    )
    inverse_blocks = block_inverse(assemble(own_terms[:45]))
    right_side = own_terms[45:]

    first = apply_blocks(inverse_blocks, right_side)
    first_slots = pick_slots(spread_out(first))
    first_pulled = jnp.sum(coupling * first_slots[:, None], axis=(0, 2))
    contrib = slot_product(camera_blocks, coupling, point_inverse, first_slots)
    local_image = into_cameras(contrib.reshape(9, -1)).reshape(9, OWNERS, CAM_DEV)
    gathered_image = lax.all_to_all(
        local_image, ("row", "col"), split_axis=1, concat_axis=1, tiled=True
    )
    first_image = damping * first + jnp.sum(gathered_image, axis=1)

    second = apply_blocks(inverse_blocks, first_image)
    second_slots = pick_slots(spread_out(second))
    second_pulled = jnp.sum(coupling * second_slots[:, None], axis=(0, 2))
    projected = jnp.sum(camera_blocks * second_slots[None], axis=1)
    solved = jnp.sum(point_inverse * second_pulled[None], axis=1)
    own_sums = jnp.stack(
        [
            jnp.sum(right_side * first),
            jnp.sum(first * first_image),
            jnp.sum(first_image * second),
            jnp.sum(second * second)
            + jnp.sum(projected * projected)
            - jnp.sum(second_pulled * solved),
        ]
    )
    spread = jnp.broadcast_to(own_sums[None], (OWNERS, 4))
    energy, curvature, crossed, second_curvature = jnp.sum(exchange(spread), axis=0)
    step_size = energy / curvature
    renewed = step_size * step_size * crossed - energy
    ratio = 1.0 + renewed / energy
    second_step = renewed / (
        ratio * ratio * curvature
        - 2.0 * step_size * ratio * crossed
        + step_size * step_size * second_curvature
    )
    first_weight = step_size + second_step * ratio
    second_weight = -second_step * step_size
    camera_move = first_weight * first + second_weight * second
    pulled = first_weight * first_pulled + second_weight * second_pulled
    point_move = jnp.sum(point_inverse * (point_gradient - pulled)[None], axis=1)
    return (camera_move, point_move)


def on_device(camera_jacobian, point_jacobian, residuals, observed_camera, track_length):
    operands = (camera_jacobian, point_jacobian, residuals, observed_camera, track_length)
    overflow, kept = by_slots(*operands)
    return lax.cond(
        overflow > 0,
        lambda given, unused: by_dense(*given),
        lambda unused, found: finish(*found),
        operands,
        kept,
    )


def solution(mesh):
    in_specs = (
        P(None, None, ("row", "col")),
        P(None, None, ("row", "col")),
        P(None, None, ("row", "col")),
        P(None, ("row", "col")),
        P(("row", "col")),
    )
    out_specs = (P(None, ("row", "col")), P(None, ("row", "col")))
    return jax.shard_map(
        on_device, mesh=mesh, in_specs=in_specs, out_specs=out_specs, check_vma=False
    )
```

```python
import jax
import jax.numpy as jnp
from jax import lax
from jax.experimental import pallas as pl
from jax.experimental.pallas import tpu as pltpu
from jax.sharding import PartitionSpec as P

CAM_DEV = 384
TRACK = 8
PT_DEV = 1024
OWNERS = 128
LANES = 128
WIDTH = 21
GROUPS = 6
ROWS = 13
CAP = GROUPS * ROWS
SPAN = 80
FEW = 64
CAMERA_AT = 20
ENTRIES = 56
COUNT_AT = GROUPS * WIDTH
BLOCKS = TRACK * PT_DEV // LANES

F32 = jnp.float32
BF16 = jnp.bfloat16
PARAMS = pltpu.CompilerParams(vmem_limit_bytes=48 * 2**20)
block_pairs = [(leading, trailing) for leading in range(9) for trailing in range(leading, 9)]


def iota(shape, axis):
    return lax.broadcasted_iota(jnp.int32, shape, axis)


def two_parts(value):
    high = value.astype(BF16)
    low = (value - high.astype(F32)).astype(BF16)
    return high, low


def dot(left, right):
    return jnp.dot(left, right, preferred_element_type=F32)


def dot_lanes(left, right):
    return lax.dot_general(left, right, (((1,), (1,)), ((), ())), preferred_element_type=F32)


def total(value):
    return jnp.sum(jnp.sum(value, axis=0, keepdims=True), axis=1, keepdims=True)


def over_tracks(value):
    return jnp.sum(value, axis=0, keepdims=True)


def used_slots(length_ref, lanes):
    return iota((TRACK, LANES), 0) < length_ref[:, lanes]


def times_inverse(inverse, vector):
    v00, v01, v02, v11, v12, v22 = inverse
    x, y, z = vector
    return [v00 * x + v01 * y + v02 * z, v01 * x + v11 * y + v12 * z, v02 * x + v12 * y + v22 * z]


def owner_of(camera):
    return ((camera >> 7) * 171) >> 9


def prepare_kernel(camera_in, point_in, error_in, index_ref, length_ref, out_ref, route_ref, state_ref, root_ref, flag_ref, owned_ref, masked_ref, camera_ref, point_ref, error_ref, pay_ref, code_ref, near_ref, slot_ref, block_ref, camera_sem, point_sem, error_sem, code_sem):
    copies = [
        pltpu.make_async_copy(camera_in, camera_ref, camera_sem),
        pltpu.make_async_copy(point_in, point_ref, point_sem),
        pltpu.make_async_copy(error_in, error_ref, error_sem),
    ]
    for copy in copies:
        copy.start()
    used = iota((TRACK, PT_DEV), 0) < length_ref[...]
    route_ref[0:TRACK, :] = jnp.where(used, owner_of(index_ref[...]), OWNERS)

    step = 256
    upto = jnp.where(iota((step, step), 0) <= iota((step, step), 1), 1.0, 0.0).astype(BF16)
    before = jnp.zeros((OWNERS, step), F32)
    names = iota((OWNERS, step), 0)
    for chunk in range(PT_DEV // step):
        lanes = slice(chunk * step, (chunk + 1) * step)
        chosen = [names == route_ref[s : s + 1, lanes] for s in range(TRACK)]
        hot = [jnp.where(here, 1.0, 0.0).astype(BF16) for here in chosen]
        for s in range(TRACK):
            owned_ref[s, :, lanes] = hot[s]
        counts = dot(jnp.concatenate(hot, axis=0), upto)
        for s in range(TRACK):
            own = counts[s * OWNERS : (s + 1) * OWNERS, :]
            rank = jnp.sum(jnp.where(chosen[s], own + before, 0.0), axis=0, keepdims=True) - 1.0
            before = before + jnp.broadcast_to(own[:, step - 1 : step], (OWNERS, step))
            route_ref[TRACK + s : TRACK + s + 1, lanes] = rank.astype(jnp.int32)

    owner = route_ref[0:TRACK, :]
    rank = route_ref[TRACK : 2 * TRACK, :]
    fits = (owner < OWNERS) & (rank < CAP)
    row_at = (rank * 171) >> 10
    place = (rank - row_at * GROUPS) * (OWNERS * ROWS) + owner * ROWS + row_at
    code = jnp.where(fits, place, GROUPS * OWNERS * ROWS)
    for chunk in range(PT_DEV // LANES):
        code_ref[chunk * TRACK : (chunk + 1) * TRACK, :] = code[:, chunk * LANES : (chunk + 1) * LANES]
    code_copy = pltpu.make_async_copy(code_ref, near_ref, code_sem)
    code_copy.start()
    most = jnp.max(jnp.max(before, axis=0, keepdims=True), axis=1, keepdims=True)
    lane = iota((OWNERS, LANES), 1)
    flag_ref[...] = jnp.where(lane > COUNT_AT, most, before[:, 0:LANES])
    for copy in copies:
        copy.wait()
    for chunk in range(PT_DEV // LANES):
        lanes = slice(chunk * LANES, (chunk + 1) * LANES)
        used = used_slots(length_ref, lanes)
        point = [
            [jnp.where(used, point_ref[3 * i + a, :, lanes], 0.0) for a in range(3)] for i in range(2)
        ]
        for i in range(2):
            for a in range(3):
                masked_ref[3 * i + a, :, lanes] = point[i][a]
        error = [jnp.where(used, error_ref[i, :, lanes], 0.0) for i in range(2)]

        def pair(a, b):
            return over_tracks(point[0][a] * point[0][b] + point[1][a] * point[1][b])

        s00, s01, s02 = 1.0 + pair(0, 0), pair(0, 1), pair(0, 2)
        s11, s12, s22 = 1.0 + pair(1, 1), pair(1, 2), 1.0 + pair(2, 2)
        c00 = s11 * s22 - s12 * s12
        c01 = s12 * s02 - s01 * s22
        c02 = s01 * s12 - s11 * s02
        c11 = s22 * s00 - s02 * s02
        c12 = s02 * s01 - s12 * s00
        c22 = s00 * s11 - s01 * s01
        determinant = s00 * c00 + s01 * c01 + s02 * c02
        scale = 1.0 / determinant
        inverse = [c * scale for c in (c00, c01, c02, c11, c12, c22)]
        gradient = [
            -over_tracks(point[0][a] * error[0] + point[1][a] * error[1]) for a in range(3)
        ]
        for at, value in enumerate(inverse + gradient):
            state_ref[at : at + 1, lanes] = value
        solved = times_inverse(inverse, gradient)
        u0 = times_inverse(inverse, point[0])
        u1 = times_inverse(inverse, point[1])

        def along(left, right):
            return left[0] * right[0] + left[1] * right[1] + left[2] * right[2]

        camera = index_ref[:, lanes]
        owner = owner_of(camera)
        local = camera - owner * CAM_DEV
        b01 = -along(u0, point[1])
        root0 = jnp.sqrt(1.0 - along(u0, point[0]))
        root1 = b01 / root0
        root2 = jnp.sqrt(1.0 - along(u1, point[1]) - root1 * root1)
        inverse0, inverse2 = 1.0 / root0, 1.0 / root2
        side0 = (error[0] + along(solved, point[0])) * inverse0
        side1 = (error[1] + along(solved, point[1]) - root1 * side0) * inverse2
        values = [root0 * camera_ref[j, :, lanes] + root1 * camera_ref[9 + j, :, lanes] for j in range(9)]
        values += [root2 * camera_ref[9 + j, :, lanes] for j in range(9)]
        values += [side0, side1, (local + 1).astype(F32)]
        for at, value in enumerate((inverse0, root1, inverse2)):
            root_ref[at * TRACK : (at + 1) * TRACK, lanes] = value
        for f in range(WIDTH):
            at = (chunk * WIDTH + f) * TRACK
            pay_ref[at : at + TRACK, :] = values[f]
    dispatch(near_ref, pay_ref, flag_ref, out_ref, slot_ref, block_ref, code_copy)


def dispatch(code_ref, pay_ref, flag_ref, out_ref, slot_ref, block_ref, code_copy):
    rows = OWNERS * ROWS
    zeros = jnp.zeros((8, LANES), F32)
    slots_ref = slot_ref.reshape(BLOCKS * LANES, LANES)
    blocks_ref = block_ref.reshape(GROUPS * rows + 8, LANES)

    share = -(-GROUPS * rows // (BLOCKS * 8)) * 8
    within = iota((LANES, LANES), 1) % WIDTH
    for first in range(0, BLOCKS, GROUPS):
        blocks = []
        for block in range(first, first + GROUPS):
            chunk, s = divmod(block, TRACK)
            if block < BLOCKS:
                blocks.append(pay_ref[pl.ds(chunk * WIDTH * TRACK + s, WIDTH, stride=TRACK), :])
            else:
                blocks.append(jnp.zeros((WIDTH, LANES), F32))
        turned = jnp.transpose(jnp.concatenate(blocks + [zeros[0 : LANES - COUNT_AT]], axis=0))
        for block in range(first, min(first + GROUPS, BLOCKS)):
            slots_ref[block * LANES : (block + 1) * LANES, :] = jnp.take_along_axis(
                turned, within + (block - first) * WIDTH, axis=1, mode="promise_in_bounds"
            )
            start = min(block * share, GROUPS * rows)
            count = min(share, GROUPS * rows - start)
            if count:
                blocks_ref[start : start + count, :] = jnp.zeros((count, LANES), F32)

    code_copy.wait()

    def place(block, carry):
        def load(start):
            columns = range(start, min(start + 16, LANES))
            return [(code_ref[block, j], slot_ref[block, j]) for j in columns]

        ready = load(0)
        for start in range(16, LANES + 16, 16):
            coming = load(start)
            for code, slot in ready:
                block_ref[code] = slot
            ready = coming
        return carry

    lax.fori_loop(0, BLOCKS, place, 0)
    group = iota((8, LANES), 1) // WIDTH

    def merge(at, carry):
        for j in range(8):
            start = pl.multiple_of(at * 64 + j * 8, 8)
            value = zeros
            for k in range(GROUPS):
                value = jnp.where(group == k, blocks_ref[pl.ds(k * rows + start, 8), :], value)
            out_ref[pl.ds(start, 8), :] = value
        return carry

    lax.fori_loop(0, rows // 64, merge, 0)
    lane = iota((OWNERS, LANES), 1)
    leading = pl.ds(0, OWNERS, stride=ROWS)
    out_ref[leading, :] = jnp.where(lane >= COUNT_AT, flag_ref[...], out_ref[leading, :])


def solve(factor, scales, vector):
    forward = []
    for i in range(9):
        value = vector[i]
        for j in range(i):
            value = value - factor[i, j] * forward[j]
        forward.append(value * scales[i])
    result = [None] * 9
    for i in reversed(range(9)):
        value = forward[i]
        for j in range(i + 1, 9):
            value = value - factor[j, i] * result[j]
        result[i] = value * scales[i]
    return result


def hot_cameras(feature_ref, hot_ref, block):
    names = iota((LANES, LANES), 0)
    for r in range(8):
        camera = feature_ref[pl.ds(CAMERA_AT * SPAN + block * 8 + r, 1), :].astype(jnp.int32) - 1
        hot = jnp.where(names == (camera & (LANES - 1)), 1.0, 0.0).astype(BF16)
        hot_ref[:, block * PT_DEV + r * LANES : block * PT_DEV + (r + 1) * LANES] = hot


def features_of(feature_ref, f, block):
    start = f * SPAN + block * 8
    return feature_ref[start : start + 8, :]


def image_slots(vector, feature_ref, table_ref, image_ref, many):
    for j in range(9):
        for c in range(3):
            at = (3 * j + c) * 8
            table_ref[at : at + 8, :] = jnp.broadcast_to(vector[j][c : c + 1, :], (8, LANES))

    def one(block):
        camera = features_of(feature_ref, CAMERA_AT, block).astype(jnp.int32) - 1
        third = camera >> 7
        lane = camera & (LANES - 1)
        images = [jnp.zeros((8, LANES), F32)] * 2
        for j in range(9):
            found = [
                jnp.take_along_axis(
                    table_ref[(3 * j + c) * 8 : (3 * j + c + 1) * 8, :],
                    lane,
                    axis=1,
                    mode="promise_in_bounds",
                )
                for c in range(3)
            ]
            value = jnp.where(third == 1, found[1], jnp.where(third == 2, found[2], found[0]))
            for i in range(2):
                images[i] = images[i] + features_of(feature_ref, 9 * i + j, block) * value
        for i in range(2):
            start = i * LANES + block * 8
            image_ref[start : start + 8, :] = images[i]

    for block in range(FEW // 8):
        one(block)

    @pl.when(many)
    def _():
        for block in range(FEW // 8, SPAN // 8):
            one(block)


def keep_parts(part_ref, feature_ref, parts_ref, block, count):
    for r in range(8):
        lanes = slice(block * PT_DEV + r * LANES, block * PT_DEV + (r + 1) * LANES)
        camera = feature_ref[pl.ds(CAMERA_AT * SPAN + block * 8 + r, 1), :].astype(jnp.int32) - 1
        value = part_ref[pl.ds(r, count, stride=8), :]
        high = value.astype(BF16).astype(F32)
        both = jnp.concatenate([high, value - high], axis=0).astype(BF16)
        third = jnp.broadcast_to(camera >> 7, (16, LANES))
        for c in range(3):
            inside = jnp.where(third == c, 1.0, 0.0).astype(BF16)
            inside = jnp.concatenate([inside] * (count // 8), axis=0)
            parts_ref[2 * c * count : 2 * (c + 1) * count, lanes] = both * inside


def camera_sums(terms, parts_ref, hot_ref, part_ref, sum_ref, count, many):
    def block_sums(block):
        terms(block)
        lanes = slice(block * PT_DEV, (block + 1) * PT_DEV)
        return dot_lanes(parts_ref[:, lanes], hot_ref[:, lanes])

    sums = block_sums(0)
    for block in range(1, FEW // 8):
        sums = sums + block_sums(block)
    sum_ref[...] = sums

    @pl.when(many)
    def _():
        for block in range(FEW // 8, SPAN // 8):
            sum_ref[...] += block_sums(block)

    part_ref[...] = jnp.zeros(part_ref.shape, F32)
    for c in range(3):
        at = 2 * c * count
        part_ref[pl.ds(c, count, stride=8), :] = (
            sum_ref[at : at + count, :] + sum_ref[at + count : at + 2 * count, :]
        )


def turn_in(got_ref, i):
    return jnp.transpose(got_ref[pl.ds(i, OWNERS, stride=2), :])


def turn_out(image_ref, out_ref):
    for i in range(2):
        out_ref[pl.ds(i, OWNERS, stride=2), :] = jnp.transpose(
            image_ref[i * LANES : (i + 1) * LANES, :]
        )


def first_camera_kernel(got_ref, feature_ref, factor_ref, first_ref, out_ref, flag_ref, hot_ref, parts_ref, table_ref, image_ref, sum_ref, part_ref):
    image_ref[...] = jnp.zeros((2 * LANES, LANES), F32)
    feature_ref[...] = jnp.zeros(feature_ref.shape, F32)

    def take_row(q):
        turned = jnp.transpose(got_ref[pl.ds(q, OWNERS, stride=ROWS), :])
        for k in range(GROUPS):
            feature_ref[pl.ds(q * GROUPS + k, WIDTH, stride=SPAN), :] = turned[
                k * WIDTH : (k + 1) * WIDTH, :
            ]
        return turned

    turned = take_row(0)
    worst = jnp.max(turned[COUNT_AT + 1 : COUNT_AT + 2, :])
    flag_ref[0, 0] = jnp.where(worst > CAP, 1, 0)
    most = jnp.max(turned[COUNT_AT : COUNT_AT + 1, :])
    many = most > FEW
    few_rows = -(-FEW // GROUPS)
    for q in range(1, few_rows):
        take_row(q)

    @pl.when(many)
    def _():
        for q in range(few_rows, ROWS):
            take_row(q)

    part_ref[...] = jnp.zeros((ENTRIES * 8, LANES), F32)

    def gather_terms(block):
        hot_cameras(feature_ref, hot_ref, block)
        f = [features_of(feature_ref, at, block) for at in range(20)]
        for at, (j, k) in enumerate(block_pairs):
            part_ref[at * 8 : (at + 1) * 8, :] = f[j] * f[k] + f[9 + j] * f[9 + k]
        for j in range(9):
            part_ref[(45 + j) * 8 : (46 + j) * 8, :] = -(f[j] * f[18] + f[9 + j] * f[19])
        keep_parts(part_ref, feature_ref, parts_ref, block, ENTRIES)

    camera_sums(gather_terms, parts_ref, hot_ref, part_ref, sum_ref, ENTRIES, many)
    matrix = {}
    for at, (j, k) in enumerate(block_pairs):
        entry = part_ref[at * 8 : (at + 1) * 8, :]
        matrix[k, j] = entry + 1.0 if j == k else entry
    side = [part_ref[(45 + j) * 8 : (46 + j) * 8, :] for j in range(9)]
    factor, scales = {}, []
    for j in range(9):
        pivot = matrix[j, j]
        for m in range(j):
            pivot = pivot - factor[j, m] * factor[j, m]
        scales.append(1.0 / jnp.sqrt(pivot))
        for i in range(j + 1, 9):
            running = matrix[i, j]
            for m in range(j):
                running = running - factor[i, m] * factor[j, m]
            factor[i, j] = running * scales[j]
    for at, (j, k) in enumerate(block_pairs):
        factor_ref[at * 8 : (at + 1) * 8, :] = scales[j] if j == k else factor[k, j]
    first = solve(factor, scales, side)
    energy = side[0] * first[0]
    for j in range(1, 9):
        energy = energy + side[j] * first[j]
    for j in range(9):
        first_ref[j * 8 : (j + 1) * 8, :] = first[j]
    first_ref[72:80, :] = energy
    first_ref[80:88, :] = jnp.where(
        iota((8, LANES), 0) < 4,
        jnp.max(turned[COUNT_AT : COUNT_AT + 1, :], axis=1, keepdims=True),
        jnp.max(turned[COUNT_AT + 1 : COUNT_AT + 2, :], axis=1, keepdims=True),
    )
    image_slots(first, feature_ref, table_ref, image_ref, many)
    turn_out(image_ref, out_ref)


def either_span(flag_ref, work):
    many = jnp.max(flag_ref[0:8, :]) > FEW
    pl.when(many)(lambda: work(SPAN))
    pl.when(jnp.logical_not(many))(lambda: work(FEW))


def pull_slots(got_ref, route_ref, masked_ref, state_ref, root_ref, owned_ref, value_ref, pulled_ref, curve_ref, span, back):
    images = []
    for i in range(2):
        images.append(turn_in(got_ref, i)[0:span, :])
    high, low = two_parts(jnp.concatenate(images, axis=0))
    parts = jnp.concatenate([high, low], axis=1)
    ranks = iota((span, PT_DEV), 0)
    for s in range(TRACK):
        hot = owned_ref[s]
        got = dot(parts, jnp.concatenate([hot, hot], axis=0))
        here = ranks == route_ref[TRACK + s : TRACK + s + 1, :]
        for i in range(2):
            value_ref[i * TRACK + s : i * TRACK + s + 1, :] = jnp.sum(
                jnp.where(here, got[i * span : (i + 1) * span, :], 0.0), axis=0, keepdims=True
            )
    curve = jnp.zeros((TRACK, LANES), F32)
    for chunk in range(PT_DEV // LANES):
        lanes = slice(chunk * LANES, (chunk + 1) * LANES)
        point = [[masked_ref[3 * i + a, :, lanes] for a in range(3)] for i in range(2)]
        root = [root_ref[at * TRACK : (at + 1) * TRACK, lanes] for at in range(3)]
        image1 = value_ref[TRACK : 2 * TRACK, lanes] * root[2]
        image = [(value_ref[0:TRACK, lanes] - root[1] * image1) * root[0], image1]
        pulled = [over_tracks(point[0][a] * image[0] + point[1][a] * image[1]) for a in range(3)]
        inverse = [state_ref[at : at + 1, lanes] for at in range(6)]
        solved = times_inverse(inverse, pulled)
        for a in range(3):
            pulled_ref[a : a + 1, lanes] = pulled[a]
        result = [
            image[i] - (point[i][0] * solved[0] + point[i][1] * solved[1] + point[i][2] * solved[2])
            for i in range(2)
        ]
        if back:
            result0 = result[0] * root[0]
            value_ref[0:TRACK, lanes] = result0
            value_ref[TRACK : 2 * TRACK, lanes] = (result[1] - root[1] * result0) * root[2]
        else:
            curve = curve + image[0] * result[0] + image[1] * result[1]
    if not back:
        curve_ref[...] = curve


def first_point_kernel(got_ref, route_ref, masked_ref, state_ref, root_ref, flag_ref, owned_ref, pulled_ref, out_ref, value_ref, image_ref):
    image_ref[...] = jnp.zeros((2 * LANES, LANES), F32)

    def work(span):
        pull_slots(got_ref, route_ref, masked_ref, state_ref, root_ref, owned_ref, value_ref, pulled_ref, None, span, True)
        ranks = iota((span, PT_DEV), 0)
        sums = jnp.zeros((4 * span, OWNERS), F32)
        for s in range(TRACK):
            here = ranks == route_ref[TRACK + s : TRACK + s + 1, :]
            spread = []
            for i in range(2):
                value = value_ref[i * TRACK + s : i * TRACK + s + 1, :]
                spread.append(jnp.where(here, value, 0.0))
            high, low = two_parts(jnp.concatenate(spread, axis=0))
            sums = sums + dot_lanes(jnp.concatenate([high, low], axis=0), owned_ref[s])
        sums = sums[0 : 2 * span] + sums[2 * span :]
        for i in range(2):
            image_ref[i * LANES : i * LANES + span, :] = sums[i * span : (i + 1) * span, :]

    either_span(flag_ref, work)
    turn_out(image_ref, out_ref)


def second_point_kernel(got_ref, route_ref, masked_ref, state_ref, root_ref, flag_ref, owned_ref, pulled_ref, out_ref, scalar_ref, value_ref, curve_ref):
    def work(span):
        pull_slots(got_ref, route_ref, masked_ref, state_ref, root_ref, owned_ref, value_ref, pulled_ref, curve_ref, span, False)

    either_span(flag_ref, work)
    out_ref[...] = jnp.broadcast_to(total(curve_ref[...]), (OWNERS, LANES))
    scalar_ref[...] = jnp.broadcast_to(
        jnp.sum(got_ref[pl.ds(0, OWNERS, stride=2), :], axis=0, keepdims=True), (8, LANES)
    )


def second_camera_kernel(got_ref, feature_ref, factor_ref, first_ref, second_ref, out_ref, hot_ref, parts_ref, table_ref, image_ref, sum_ref, wide_ref):
    for i in range(2):
        image_ref[i * LANES : (i + 1) * LANES, :] = turn_in(got_ref, i)
    many = jnp.max(first_ref[80:84, :]) > FEW
    wide_ref[...] = jnp.zeros((LANES, LANES), F32)

    def gather_terms(block):
        hot_cameras(feature_ref, hot_ref, block)
        back = [
            image_ref[i * LANES + block * 8 : i * LANES + (block + 1) * 8, :] for i in range(2)
        ]
        for j in range(9):
            wide_ref[j * 8 : (j + 1) * 8, :] = (
                features_of(feature_ref, j, block) * back[0]
                + features_of(feature_ref, 9 + j, block) * back[1]
            )
        keep_parts(wide_ref, feature_ref, parts_ref, block, 16)

    camera_sums(gather_terms, parts_ref, hot_ref, wide_ref, sum_ref, 16, many)
    first = [first_ref[j * 8 : (j + 1) * 8, :] for j in range(9)]
    image = [first[j] + wide_ref[j * 8 : (j + 1) * 8, :] for j in range(9)]
    factor, scales = {}, []
    for at, (j, k) in enumerate(block_pairs):
        entry = factor_ref[at * 8 : (at + 1) * 8, :]
        if j == k:
            scales.append(entry)
        else:
            factor[k, j] = entry
    second = solve(factor, scales, image)
    for j in range(9):
        second_ref[j * 8 : (j + 1) * 8, :] = second[j]

    def inner(left, right):
        value = left[0] * right[0]
        for j in range(1, 9):
            value = value + left[j] * right[j]
        return value

    image_slots(second, feature_ref, table_ref, image_ref, many)
    scalars = [first_ref[72:80, :], inner(first, image), inner(image, second), inner(second, second)]
    for at, value in enumerate(scalars):
        image_ref[SPAN + at : SPAN + at + 1, :] = jnp.broadcast_to(total(value), (1, LANES))
    turn_out(image_ref, out_ref)


def finish_kernel(curve_ref, scalar_ref, first_ref, second_ref, state_ref, first_pulled_ref, second_pulled_ref, dense_camera, dense_point, camera_out, point_out, camera_ref, point_ref, camera_sem, point_sem):
    own = jnp.sum(curve_ref[...], axis=0, keepdims=True)[:, 0:1]
    energy, curvature, crossed, square = [
        scalar_ref[0:1, SPAN + at : SPAN + at + 1] for at in range(4)
    ]
    step_size = energy / curvature
    renewed = step_size * step_size * crossed - energy
    ratio = 1.0 + renewed / energy
    second_step = renewed / (
        ratio * ratio * curvature
        - 2.0 * step_size * ratio * crossed
        + step_size * step_size * (square + own)
    )
    first_weight = step_size + second_step * ratio
    second_weight = -second_step * step_size
    for c in range(3):
        camera_ref[:, c * LANES : (c + 1) * LANES] = (
            first_weight * first_ref[pl.ds(c, 9, stride=8), :]
            + second_weight * second_ref[pl.ds(c, 9, stride=8), :]
        )
    left = [
        state_ref[6 + a : 7 + a, :]
        - first_weight * first_pulled_ref[a : a + 1, :]
        - second_weight * second_pulled_ref[a : a + 1, :]
        for a in range(3)
    ]
    moved = times_inverse([state_ref[at : at + 1, :] for at in range(6)], left)
    for a in range(3):
        point_ref[a : a + 1, :] = moved[a]

    def send(camera, point):
        copies = [
            pltpu.make_async_copy(camera, camera_out, camera_sem),
            pltpu.make_async_copy(point, point_out, point_sem),
        ]
        for copy in copies:
            copy.start()
        for copy in copies:
            copy.wait()

    over = jnp.max(first_ref[84:88, :]) > CAP
    pl.when(over)(lambda: send(dense_camera, dense_point))
    pl.when(jnp.logical_not(over))(lambda: send(camera_ref, point_ref))


def call(kernel, outs, scratch, operands, in_scalar=0):
    specs = [
        pl.BlockSpec(memory_space=pltpu.SMEM if at < in_scalar else pltpu.VMEM)
        for at in range(len(operands))
    ]
    return pl.pallas_call(
        kernel,
        out_shape=[jax.ShapeDtypeStruct(shape, dtype) for shape, dtype in outs],
        in_specs=specs,
        out_specs=[
            pl.BlockSpec(memory_space=pltpu.SMEM if shape == (1, 1) else pltpu.VMEM)
            for shape, unused in outs
        ],
        scratch_shapes=[pltpu.VMEM(shape, dtype) for shape, dtype in scratch],
        compiler_params=PARAMS,
    )(*operands)


def exchange(rows):
    blocks = rows.reshape(OWNERS, 1, -1)
    blocks = lax.all_to_all(blocks, ("row", "col"), split_axis=0, concat_axis=0, tiled=True)
    return blocks.reshape(rows.shape)


def by_slots(camera_jacobian, point_jacobian, residuals, observed_camera, track_length):
    lengths = track_length.reshape(1, PT_DEV)
    in_vmem = [pl.BlockSpec(memory_space=pltpu.VMEM)]
    held = [(18, TRACK, PT_DEV), (6, TRACK, PT_DEV), (2, TRACK, PT_DEV)]
    outs = [
        ((OWNERS * ROWS, LANES), F32),
        ((2 * TRACK, PT_DEV), jnp.int32),
        ((16, PT_DEV), F32),
        ((3 * TRACK, PT_DEV), F32),
        ((OWNERS, LANES), F32),
        ((TRACK, OWNERS, PT_DEV), BF16),
        ((6, TRACK, PT_DEV), F32),
    ]
    sent, route, state, root, flag, owned, masked = pl.pallas_call(
        prepare_kernel,
        out_shape=[jax.ShapeDtypeStruct(shape, dtype) for shape, dtype in outs],
        in_specs=[pl.BlockSpec(memory_space=pl.ANY)] * 3 + in_vmem * 2,
        out_specs=in_vmem * len(outs),
        scratch_shapes=[pltpu.VMEM(shape, F32) for shape in held]
        + [
            pltpu.VMEM((WIDTH * BLOCKS, LANES), F32),
            pltpu.VMEM((BLOCKS, LANES), jnp.int32),
            pltpu.SMEM((BLOCKS, LANES), jnp.int32),
            pltpu.VMEM((BLOCKS, LANES, 1, LANES), F32),
            pltpu.VMEM((GROUPS * OWNERS * ROWS + 8, 1, LANES), F32),
        ]
        + [pltpu.SemaphoreType.DMA] * 4,
        compiler_params=PARAMS,
    )(camera_jacobian, point_jacobian, residuals, observed_camera, lengths)
    hot = ((LANES, SPAN * LANES), BF16)
    table = ((27 * 8, LANES), F32)
    image = ((2 * LANES, LANES), F32)
    pair = ((2 * OWNERS, LANES), F32)
    features, factor, first, out, overflow = call(
        first_camera_kernel,
        [((WIDTH * SPAN, LANES), F32), ((45 * 8, LANES), F32), ((88, LANES), F32), pair, ((1, 1), jnp.int32)],
        [hot, ((6 * ENTRIES, SPAN * LANES), BF16), table, image, ((6 * ENTRIES, LANES), F32), ((ENTRIES * 8, LANES), F32)],
        (exchange(sent),),
    )
    first_pulled, out = call(
        first_point_kernel,
        [((8, PT_DEV), F32), pair],
        [((2 * TRACK, PT_DEV), F32), image],
        (exchange(out), route, masked, state, root, flag, owned),
    )
    second, out = call(
        second_camera_kernel,
        [((72, LANES), F32), pair],
        [hot, ((96, SPAN * LANES), BF16), table, image, ((96, LANES), F32), ((LANES, LANES), F32)],
        (exchange(out), features, factor, first),
    )
    second_pulled, curve, scalars = call(
        second_point_kernel,
        [((8, PT_DEV), F32), ((OWNERS, LANES), F32), ((8, LANES), F32)],
        [((2 * TRACK, PT_DEV), F32), ((TRACK, LANES), F32)],
        (exchange(out), route, masked, state, root, flag, owned),
    )
    overflow, curve = lax.optimization_barrier((overflow, exchange(curve)))
    return overflow[0, 0], (curve, scalars, first, second, state, first_pulled, second_pulled)


def finish(*operands):
    shapes = [(9, CAM_DEV), (3, PT_DEV)]
    return tuple(
        pl.pallas_call(
            finish_kernel,
            out_shape=[jax.ShapeDtypeStruct(shape, F32) for shape in shapes],
            in_specs=[pl.BlockSpec(memory_space=pltpu.VMEM)] * (len(operands) - 2)
            + [pl.BlockSpec(memory_space=pl.ANY)] * 2,
            out_specs=[pl.BlockSpec(memory_space=pltpu.HBM)] * 2,
            scratch_shapes=[pltpu.VMEM(shape, F32) for shape in shapes]
            + [pltpu.SemaphoreType.DMA] * 2,
            compiler_params=PARAMS,
        )(*operands)
    )


damping = 1.0


def inverse_small(matrix):
    entries = [[matrix[row_at, col_at] for col_at in range(3)] for row_at in range(3)]
    cofactor = [
        [
            entries[(row_at + 1) % 3][(col_at + 1) % 3]
            * entries[(row_at + 2) % 3][(col_at + 2) % 3]
            - entries[(row_at + 1) % 3][(col_at + 2) % 3]
            * entries[(row_at + 2) % 3][(col_at + 1) % 3]
            for col_at in range(3)
        ]
        for row_at in range(3)
    ]
    determinant = (
        entries[0][0] * cofactor[0][0]
        + entries[0][1] * cofactor[0][1]
        + entries[0][2] * cofactor[0][2]
    )
    return jnp.stack(
        [
            jnp.stack([cofactor[col_at][row_at] / determinant for col_at in range(3)])
            for row_at in range(3)
        ]
    )


def block_inverse(matrix):
    factor = {}
    for col_at in range(9):
        pivot_value = matrix[col_at, col_at]
        for middle in range(col_at):
            pivot_value = pivot_value - factor[col_at, middle] * factor[col_at, middle]
        diagonal_root = jnp.sqrt(pivot_value)
        factor[col_at, col_at] = diagonal_root
        for row_at in range(col_at + 1, 9):
            running = matrix[row_at, col_at]
            for middle in range(col_at):
                running = running - factor[row_at, middle] * factor[col_at, middle]
            factor[row_at, col_at] = running / diagonal_root
    factor_inverse = {}
    for row_at in range(9):
        factor_inverse[row_at, row_at] = 1.0 / factor[row_at, row_at]
        for col_at in range(row_at):
            running = factor[row_at, col_at] * factor_inverse[col_at, col_at]
            for middle in range(col_at + 1, row_at):
                running = running + factor[row_at, middle] * factor_inverse[middle, col_at]
            factor_inverse[row_at, col_at] = -running / factor[row_at, row_at]
    result_rows = []
    for row_at in range(9):
        entries = []
        for col_at in range(9):
            running = (
                factor_inverse[max(row_at, col_at), row_at]
                * factor_inverse[max(row_at, col_at), col_at]
            )
            for middle in range(max(row_at, col_at) + 1, 9):
                running = running + factor_inverse[middle, row_at] * factor_inverse[middle, col_at]
            entries.append(running)
        result_rows.append(jnp.stack(entries))
    return jnp.stack(result_rows)


def assemble(packed):
    positions = {}
    for index_at, pair in enumerate(block_pairs):
        positions[pair[0], pair[1]] = index_at
        positions[pair[1], pair[0]] = index_at
    return jnp.stack(
        [
            jnp.stack(
                [
                    packed[positions[row_at, col_at]] + (damping if row_at == col_at else 0.0)
                    for col_at in range(9)
                ]
            )
            for row_at in range(9)
        ]
    )


def apply_blocks(inverse_blocks, vector):
    return jnp.sum(inverse_blocks * vector[None], axis=1)


def slot_basics(camera_jacobian, point_jacobian, residuals, track_length):
    tracks = camera_jacobian.shape[1]
    in_track = (jnp.arange(tracks, dtype=jnp.int32)[:, None] < track_length[None, :]).astype(
        jnp.float32
    )
    camera_blocks = camera_jacobian.reshape(2, 9, tracks, -1) * in_track
    point_blocks = point_jacobian.reshape(2, 3, tracks, -1) * in_track
    errors = residuals * in_track
    coupling = jnp.sum(camera_blocks[:, :, None] * point_blocks[:, None], axis=0)
    point_system = jnp.sum(point_blocks[:, :, None] * point_blocks[:, None], axis=(0, 3))
    point_system = point_system + damping * jnp.eye(3, dtype=jnp.float32)[:, :, None]
    point_inverse = inverse_small(point_system)
    point_gradient = -jnp.sum(point_blocks * errors[:, None], axis=(0, 2))
    return (camera_blocks, errors, coupling, point_inverse, point_gradient)


def camera_terms(camera_blocks, errors, coupling, point_inverse, point_gradient):
    solved = jnp.sum(point_inverse * point_gradient[None], axis=1)
    scaled = coupling[:, 0][:, None] * point_inverse[0][None, :, None, :]
    for middle in range(1, 3):
        scaled = scaled + coupling[:, middle][:, None] * point_inverse[middle][None, :, None, :]
    packed = []
    for leading, trailing in block_pairs:
        packed.append(
            jnp.sum(camera_blocks[:, leading] * camera_blocks[:, trailing], axis=0)
            - jnp.sum(scaled[leading] * coupling[trailing], axis=0)
        )
    right_side = -jnp.sum(camera_blocks * errors[:, None], axis=0) - jnp.sum(
        coupling * solved[None, :, None], axis=1
    )
    return jnp.concatenate([jnp.stack(packed), right_side], axis=0)


def slot_product(camera_blocks, coupling, point_inverse, gathered):
    projected = jnp.sum(camera_blocks * gathered[None], axis=1)
    pulled = jnp.sum(coupling * gathered[:, None], axis=(0, 2))
    solved = jnp.sum(point_inverse * pulled[None], axis=1)
    return jnp.sum(camera_blocks * projected[:, None], axis=0) - jnp.sum(
        coupling * solved[None, :, None], axis=1
    )


def by_dense(camera_jacobian, point_jacobian, residuals, observed_camera, track_length):
    camera_blocks, errors, coupling, point_inverse, point_gradient = slot_basics(
        camera_jacobian, point_jacobian, residuals, track_length
    )
    tracks, points = observed_camera.shape
    rows, cols = lax.axis_size("row"), lax.axis_size("col")
    cameras = CAM_DEV * rows * cols
    flat_cameras = observed_camera.reshape(-1)

    def into_cameras(values):
        width = values.shape[0]
        by_camera = (
            jnp.zeros((cameras, width), jnp.float32).at[flat_cameras].add(jnp.transpose(values))
        )
        return jnp.transpose(by_camera)

    def pick_slots(whole):
        slot_rows = jnp.transpose(whole)[flat_cameras]
        return jnp.transpose(slot_rows).reshape(9, tracks, points)

    def spread_out(value):
        copies = jnp.broadcast_to(value[:, None], (9, OWNERS, CAM_DEV)).reshape(9, cameras)
        return lax.all_to_all(copies, ("row", "col"), split_axis=1, concat_axis=1, tiled=True)

    term_values = camera_terms(
        camera_blocks, errors, coupling, point_inverse, point_gradient
    ).reshape(54, -1)
    local_terms = into_cameras(term_values).reshape(54, rows * cols, CAM_DEV)
    own_terms = jnp.sum(
        lax.all_to_all(local_terms, ("row", "col"), split_axis=1, concat_axis=1, tiled=True), axis=1
    )
    inverse_blocks = block_inverse(assemble(own_terms[:45]))
    right_side = own_terms[45:]

    first = apply_blocks(inverse_blocks, right_side)
    first_slots = pick_slots(spread_out(first))
    first_pulled = jnp.sum(coupling * first_slots[:, None], axis=(0, 2))
    contrib = slot_product(camera_blocks, coupling, point_inverse, first_slots)
    local_image = into_cameras(contrib.reshape(9, -1)).reshape(9, OWNERS, CAM_DEV)
    gathered_image = lax.all_to_all(
        local_image, ("row", "col"), split_axis=1, concat_axis=1, tiled=True
    )
    first_image = damping * first + jnp.sum(gathered_image, axis=1)

    second = apply_blocks(inverse_blocks, first_image)
    second_slots = pick_slots(spread_out(second))
    second_pulled = jnp.sum(coupling * second_slots[:, None], axis=(0, 2))
    projected = jnp.sum(camera_blocks * second_slots[None], axis=1)
    solved = jnp.sum(point_inverse * second_pulled[None], axis=1)
    own_sums = jnp.stack(
        [
            jnp.sum(right_side * first),
            jnp.sum(first * first_image),
            jnp.sum(first_image * second),
            jnp.sum(second * second)
            + jnp.sum(projected * projected)
            - jnp.sum(second_pulled * solved),
        ]
    )
    spread = jnp.broadcast_to(own_sums[None], (OWNERS, 4))
    energy, curvature, crossed, second_curvature = jnp.sum(exchange(spread), axis=0)
    step_size = energy / curvature
    renewed = step_size * step_size * crossed - energy
    ratio = 1.0 + renewed / energy
    second_step = renewed / (
        ratio * ratio * curvature
        - 2.0 * step_size * ratio * crossed
        + step_size * step_size * second_curvature
    )
    first_weight = step_size + second_step * ratio
    second_weight = -second_step * step_size
    camera_move = first_weight * first + second_weight * second
    pulled = first_weight * first_pulled + second_weight * second_pulled
    point_move = jnp.sum(point_inverse * (point_gradient - pulled)[None], axis=1)
    return (camera_move, point_move)


def on_device(camera_jacobian, point_jacobian, residuals, observed_camera, track_length):
    operands = (camera_jacobian, point_jacobian, residuals, observed_camera, track_length)
    overflow, kept = by_slots(*operands)
    dense = lax.cond(
        overflow > 0,
        lambda *given: by_dense(*given),
        lambda *given: (jnp.zeros((9, CAM_DEV), F32), jnp.zeros((3, PT_DEV), F32)),
        *operands,
    )
    return finish(*kept, *dense)


def solution(mesh):
    in_specs = (
        P(None, None, ("row", "col")),
        P(None, None, ("row", "col")),
        P(None, None, ("row", "col")),
        P(None, ("row", "col")),
        P(("row", "col")),
    )
    out_specs = (P(None, ("row", "col")), P(None, ("row", "col")))
    return jax.shard_map(
        on_device, mesh=mesh, in_specs=in_specs, out_specs=out_specs, check_vma=False
    )
```

```python
import jax
import jax.numpy as jnp
from jax import lax
from jax.experimental import pallas as pl
from jax.experimental.pallas import tpu as pltpu
from jax.sharding import PartitionSpec as P

CAM_DEV = 384
TRACK = 8
PT_DEV = 1024
OWNERS = 128
LANES = 128
WIDTH = 21
GROUPS = 6
ROWS = 13
CAP = GROUPS * ROWS
SPAN = 80
FEW = 64
CAMERA_AT = 20
ENTRIES = 56
COUNT_AT = GROUPS * WIDTH
BLOCKS = TRACK * PT_DEV // LANES

F32 = jnp.float32
BF16 = jnp.bfloat16
PARAMS = pltpu.CompilerParams(vmem_limit_bytes=48 * 2**20)
block_pairs = [(leading, trailing) for leading in range(9) for trailing in range(leading, 9)]


def iota(shape, axis):
    return lax.broadcasted_iota(jnp.int32, shape, axis)


def two_parts(value):
    high = value.astype(BF16)
    low = (value - high.astype(F32)).astype(BF16)
    return high, low


def dot(left, right):
    return jnp.dot(left, right, preferred_element_type=F32)


def dot_lanes(left, right):
    return lax.dot_general(left, right, (((1,), (1,)), ((), ())), preferred_element_type=F32)


def total(value):
    return jnp.sum(jnp.sum(value, axis=0, keepdims=True), axis=1, keepdims=True)


def over_tracks(value):
    return jnp.sum(value, axis=0, keepdims=True)


def used_slots(length_ref, lanes):
    return iota((TRACK, LANES), 0) < length_ref[:, lanes]


def times_inverse(inverse, vector):
    v00, v01, v02, v11, v12, v22 = inverse
    x, y, z = vector
    return [v00 * x + v01 * y + v02 * z, v01 * x + v11 * y + v12 * z, v02 * x + v12 * y + v22 * z]


def owner_of(camera):
    return ((camera >> 7) * 171) >> 9


def prepare_kernel(camera_in, point_in, error_in, index_ref, length_ref, out_ref, route_ref, state_ref, root_ref, flag_ref, owned_ref, masked_ref, camera_ref, point_ref, error_ref, pay_ref, code_ref, near_ref, slot_ref, block_ref, camera_sem, point_sem, error_sem, code_sem):
    copies = [
        pltpu.make_async_copy(camera_in, camera_ref, camera_sem),
        pltpu.make_async_copy(point_in, point_ref, point_sem),
        pltpu.make_async_copy(error_in, error_ref, error_sem),
    ]
    for copy in copies:
        copy.start()
    used = iota((TRACK, PT_DEV), 0) < length_ref[...]
    route_ref[0:TRACK, :] = jnp.where(used, owner_of(index_ref[...]), OWNERS)

    step = 256
    upto = jnp.where(iota((step, step), 0) <= iota((step, step), 1), 1.0, 0.0).astype(BF16)
    before = jnp.zeros((OWNERS, step), F32)
    names = iota((OWNERS, step), 0)
    for s in range(TRACK):
        for chunk in range(PT_DEV // step):
            lanes = slice(chunk * step, (chunk + 1) * step)
            chosen = names == route_ref[s : s + 1, lanes]
            hot = jnp.where(chosen, 1.0, 0.0).astype(BF16)
            owned_ref[s, :, lanes] = hot
            counts = dot(hot, upto)
            rank = jnp.sum(jnp.where(chosen, counts + before, 0.0), axis=0, keepdims=True) - 1.0
            before = before + jnp.broadcast_to(counts[:, step - 1 : step], (OWNERS, step))
            route_ref[TRACK + s : TRACK + s + 1, lanes] = rank.astype(jnp.int32)

    owner = route_ref[0:TRACK, :]
    rank = route_ref[TRACK : 2 * TRACK, :]
    fits = (owner < OWNERS) & (rank < CAP)
    row_at = (rank * 171) >> 10
    place = (rank - row_at * GROUPS) * (OWNERS * ROWS) + owner * ROWS + row_at
    code = jnp.where(fits, place, GROUPS * OWNERS * ROWS)
    for chunk in range(PT_DEV // LANES):
        code_ref[chunk * TRACK : (chunk + 1) * TRACK, :] = code[:, chunk * LANES : (chunk + 1) * LANES]
    code_copy = pltpu.make_async_copy(code_ref, near_ref, code_sem)
    code_copy.start()
    most = jnp.max(jnp.max(before, axis=0, keepdims=True), axis=1, keepdims=True)
    lane = iota((OWNERS, LANES), 1)
    flag_ref[...] = jnp.where(lane > COUNT_AT, most, before[:, 0:LANES])
    for copy in copies:
        copy.wait()
    for chunk in range(PT_DEV // LANES):
        lanes = slice(chunk * LANES, (chunk + 1) * LANES)
        used = used_slots(length_ref, lanes)
        point = [
            [jnp.where(used, point_ref[3 * i + a, :, lanes], 0.0) for a in range(3)] for i in range(2)
        ]
        for i in range(2):
            for a in range(3):
                masked_ref[3 * i + a, :, lanes] = point[i][a]
        error = [jnp.where(used, error_ref[i, :, lanes], 0.0) for i in range(2)]

        def pair(a, b):
            return over_tracks(point[0][a] * point[0][b] + point[1][a] * point[1][b])

        s00, s01, s02 = 1.0 + pair(0, 0), pair(0, 1), pair(0, 2)
        s11, s12, s22 = 1.0 + pair(1, 1), pair(1, 2), 1.0 + pair(2, 2)
        c00 = s11 * s22 - s12 * s12
        c01 = s12 * s02 - s01 * s22
        c02 = s01 * s12 - s11 * s02
        c11 = s22 * s00 - s02 * s02
        c12 = s02 * s01 - s12 * s00
        c22 = s00 * s11 - s01 * s01
        determinant = s00 * c00 + s01 * c01 + s02 * c02
        scale = 1.0 / determinant
        inverse = [c * scale for c in (c00, c01, c02, c11, c12, c22)]
        gradient = [
            -over_tracks(point[0][a] * error[0] + point[1][a] * error[1]) for a in range(3)
        ]
        for at, value in enumerate(inverse + gradient):
            state_ref[at : at + 1, lanes] = value
        solved = times_inverse(inverse, gradient)
        u0 = times_inverse(inverse, point[0])
        u1 = times_inverse(inverse, point[1])

        def along(left, right):
            return left[0] * right[0] + left[1] * right[1] + left[2] * right[2]

        camera = index_ref[:, lanes]
        owner = owner_of(camera)
        local = camera - owner * CAM_DEV
        b01 = -along(u0, point[1])
        root0 = jnp.sqrt(1.0 - along(u0, point[0]))
        root1 = b01 / root0
        root2 = jnp.sqrt(1.0 - along(u1, point[1]) - root1 * root1)
        inverse0, inverse2 = 1.0 / root0, 1.0 / root2
        side0 = (error[0] + along(solved, point[0])) * inverse0
        side1 = (error[1] + along(solved, point[1]) - root1 * side0) * inverse2
        values = [root0 * camera_ref[j, :, lanes] + root1 * camera_ref[9 + j, :, lanes] for j in range(9)]
        values += [root2 * camera_ref[9 + j, :, lanes] for j in range(9)]
        values += [side0, side1, (local + 1).astype(F32)]
        for at, value in enumerate((inverse0, root1, inverse2)):
            root_ref[at * TRACK : (at + 1) * TRACK, lanes] = value
        for f in range(WIDTH):
            at = (chunk * WIDTH + f) * TRACK
            pay_ref[at : at + TRACK, :] = values[f]
    dispatch(near_ref, pay_ref, flag_ref, out_ref, slot_ref, block_ref, code_copy)


def dispatch(code_ref, pay_ref, flag_ref, out_ref, slot_ref, block_ref, code_copy):
    rows = OWNERS * ROWS
    zeros = jnp.zeros((8, LANES), F32)
    slots_ref = slot_ref.reshape(BLOCKS * LANES, LANES)
    blocks_ref = block_ref.reshape(GROUPS * rows + 8, LANES)

    share = -(-GROUPS * rows // (BLOCKS * 8)) * 8
    within = iota((LANES, LANES), 1) % WIDTH
    for first in range(0, BLOCKS, GROUPS):
        blocks = []
        for block in range(first, first + GROUPS):
            chunk, s = divmod(block, TRACK)
            if block < BLOCKS:
                blocks.append(pay_ref[pl.ds(chunk * WIDTH * TRACK + s, WIDTH, stride=TRACK), :])
            else:
                blocks.append(jnp.zeros((WIDTH, LANES), F32))
        turned = jnp.transpose(jnp.concatenate(blocks + [zeros[0 : LANES - COUNT_AT]], axis=0))
        for block in range(first, min(first + GROUPS, BLOCKS)):
            slots_ref[block * LANES : (block + 1) * LANES, :] = jnp.take_along_axis(
                turned, within + (block - first) * WIDTH, axis=1, mode="promise_in_bounds"
            )
            start = min(block * share, GROUPS * rows)
            count = min(share, GROUPS * rows - start)
            if count:
                blocks_ref[start : start + count, :] = jnp.zeros((count, LANES), F32)

    code_copy.wait()

    def place(block, carry):
        def load(start):
            columns = range(start, min(start + 16, LANES))
            return [(code_ref[block, j], slot_ref[block, j]) for j in columns]

        ready = load(0)
        for start in range(16, LANES + 16, 16):
            coming = load(start)
            for code, slot in ready:
                block_ref[code] = slot
            ready = coming
        return carry

    lax.fori_loop(0, BLOCKS, place, 0)
    group = iota((8, LANES), 1) // WIDTH

    def merge(at, carry):
        for j in range(8):
            start = pl.multiple_of(at * 64 + j * 8, 8)
            value = zeros
            for k in range(GROUPS):
                value = jnp.where(group == k, blocks_ref[pl.ds(k * rows + start, 8), :], value)
            out_ref[pl.ds(start, 8), :] = value
        return carry

    lax.fori_loop(0, rows // 64, merge, 0)
    lane = iota((OWNERS, LANES), 1)
    leading = pl.ds(0, OWNERS, stride=ROWS)
    out_ref[leading, :] = jnp.where(lane >= COUNT_AT, flag_ref[...], out_ref[leading, :])


def solve(factor, scales, vector):
    forward = []
    for i in range(9):
        value = vector[i]
        for j in range(i):
            value = value - factor[i, j] * forward[j]
        forward.append(value * scales[i])
    result = [None] * 9
    for i in reversed(range(9)):
        value = forward[i]
        for j in range(i + 1, 9):
            value = value - factor[j, i] * result[j]
        result[i] = value * scales[i]
    return result


def hot_cameras(feature_ref, hot_ref, block):
    names = iota((LANES, LANES), 0)
    for r in range(8):
        camera = feature_ref[pl.ds(CAMERA_AT * SPAN + block * 8 + r, 1), :].astype(jnp.int32) - 1
        hot = jnp.where(names == (camera & (LANES - 1)), 1.0, 0.0).astype(BF16)
        hot_ref[:, block * PT_DEV + r * LANES : block * PT_DEV + (r + 1) * LANES] = hot


def features_of(feature_ref, f, block):
    start = f * SPAN + block * 8
    return feature_ref[start : start + 8, :]


def image_slots(vector, feature_ref, table_ref, image_ref, many):
    for j in range(9):
        for c in range(3):
            at = (3 * j + c) * 8
            table_ref[at : at + 8, :] = jnp.broadcast_to(vector[j][c : c + 1, :], (8, LANES))

    def one(block):
        camera = features_of(feature_ref, CAMERA_AT, block).astype(jnp.int32) - 1
        third = camera >> 7
        lane = camera & (LANES - 1)
        images = [jnp.zeros((8, LANES), F32)] * 2
        for j in range(9):
            found = [
                jnp.take_along_axis(
                    table_ref[(3 * j + c) * 8 : (3 * j + c + 1) * 8, :],
                    lane,
                    axis=1,
                    mode="promise_in_bounds",
                )
                for c in range(3)
            ]
            value = jnp.where(third == 1, found[1], jnp.where(third == 2, found[2], found[0]))
            for i in range(2):
                images[i] = images[i] + features_of(feature_ref, 9 * i + j, block) * value
        for i in range(2):
            start = i * LANES + block * 8
            image_ref[start : start + 8, :] = images[i]

    for block in range(FEW // 8):
        one(block)

    @pl.when(many)
    def _():
        for block in range(FEW // 8, SPAN // 8):
            one(block)


def keep_parts(part_ref, feature_ref, parts_ref, block, count):
    for r in range(8):
        lanes = slice(block * PT_DEV + r * LANES, block * PT_DEV + (r + 1) * LANES)
        camera = feature_ref[pl.ds(CAMERA_AT * SPAN + block * 8 + r, 1), :].astype(jnp.int32) - 1
        value = part_ref[pl.ds(r, count, stride=8), :]
        high = value.astype(BF16).astype(F32)
        both = jnp.concatenate([high, value - high], axis=0).astype(BF16)
        third = jnp.broadcast_to(camera >> 7, (16, LANES))
        for c in range(3):
            inside = jnp.where(third == c, 1.0, 0.0).astype(BF16)
            inside = jnp.concatenate([inside] * (count // 8), axis=0)
            parts_ref[2 * c * count : 2 * (c + 1) * count, lanes] = both * inside


def camera_sums(terms, parts_ref, hot_ref, part_ref, sum_ref, count, many):
    def block_sums(block):
        terms(block)
        lanes = slice(block * PT_DEV, (block + 1) * PT_DEV)
        return dot_lanes(parts_ref[:, lanes], hot_ref[:, lanes])

    sums = block_sums(0)
    for block in range(1, FEW // 8):
        sums = sums + block_sums(block)
    sum_ref[...] = sums

    @pl.when(many)
    def _():
        for block in range(FEW // 8, SPAN // 8):
            sum_ref[...] += block_sums(block)

    part_ref[...] = jnp.zeros(part_ref.shape, F32)
    for c in range(3):
        at = 2 * c * count
        part_ref[pl.ds(c, count, stride=8), :] = (
            sum_ref[at : at + count, :] + sum_ref[at + count : at + 2 * count, :]
        )


def turn_in(got_ref, i):
    return jnp.transpose(got_ref[pl.ds(i, OWNERS, stride=2), :])


def turn_out(image_ref, out_ref):
    for i in range(2):
        out_ref[pl.ds(i, OWNERS, stride=2), :] = jnp.transpose(
            image_ref[i * LANES : (i + 1) * LANES, :]
        )


def first_camera_kernel(got_ref, feature_ref, factor_ref, first_ref, out_ref, flag_ref, hot_ref, parts_ref, table_ref, image_ref, sum_ref, part_ref):
    image_ref[...] = jnp.zeros((2 * LANES, LANES), F32)
    feature_ref[...] = jnp.zeros(feature_ref.shape, F32)

    def take_row(q):
        turned = jnp.transpose(got_ref[pl.ds(q, OWNERS, stride=ROWS), :])
        for k in range(GROUPS):
            feature_ref[pl.ds(q * GROUPS + k, WIDTH, stride=SPAN), :] = turned[
                k * WIDTH : (k + 1) * WIDTH, :
            ]
        return turned

    turned = take_row(0)
    worst = jnp.max(turned[COUNT_AT + 1 : COUNT_AT + 2, :])
    flag_ref[0, 0] = jnp.where(worst > CAP, 1, 0)
    most = jnp.max(turned[COUNT_AT : COUNT_AT + 1, :])
    many = most > FEW
    few_rows = -(-FEW // GROUPS)
    for q in range(1, few_rows):
        take_row(q)

    @pl.when(many)
    def _():
        for q in range(few_rows, ROWS):
            take_row(q)

    part_ref[...] = jnp.zeros((ENTRIES * 8, LANES), F32)

    def gather_terms(block):
        hot_cameras(feature_ref, hot_ref, block)
        f = [features_of(feature_ref, at, block) for at in range(20)]
        for at, (j, k) in enumerate(block_pairs):
            part_ref[at * 8 : (at + 1) * 8, :] = f[j] * f[k] + f[9 + j] * f[9 + k]
        for j in range(9):
            part_ref[(45 + j) * 8 : (46 + j) * 8, :] = -(f[j] * f[18] + f[9 + j] * f[19])
        keep_parts(part_ref, feature_ref, parts_ref, block, ENTRIES)

    camera_sums(gather_terms, parts_ref, hot_ref, part_ref, sum_ref, ENTRIES, many)
    matrix = {}
    for at, (j, k) in enumerate(block_pairs):
        entry = part_ref[at * 8 : (at + 1) * 8, :]
        matrix[k, j] = entry + 1.0 if j == k else entry
    side = [part_ref[(45 + j) * 8 : (46 + j) * 8, :] for j in range(9)]
    factor, scales = {}, []
    for j in range(9):
        pivot = matrix[j, j]
        for m in range(j):
            pivot = pivot - factor[j, m] * factor[j, m]
        scales.append(1.0 / jnp.sqrt(pivot))
        for i in range(j + 1, 9):
            running = matrix[i, j]
            for m in range(j):
                running = running - factor[i, m] * factor[j, m]
            factor[i, j] = running * scales[j]
    for at, (j, k) in enumerate(block_pairs):
        factor_ref[at * 8 : (at + 1) * 8, :] = scales[j] if j == k else factor[k, j]
    first = solve(factor, scales, side)
    energy = side[0] * first[0]
    for j in range(1, 9):
        energy = energy + side[j] * first[j]
    for j in range(9):
        first_ref[j * 8 : (j + 1) * 8, :] = first[j]
    first_ref[72:80, :] = energy
    first_ref[80:88, :] = jnp.where(
        iota((8, LANES), 0) < 4,
        jnp.max(turned[COUNT_AT : COUNT_AT + 1, :], axis=1, keepdims=True),
        jnp.max(turned[COUNT_AT + 1 : COUNT_AT + 2, :], axis=1, keepdims=True),
    )
    image_slots(first, feature_ref, table_ref, image_ref, many)
    turn_out(image_ref, out_ref)


def either_span(flag_ref, work):
    many = jnp.max(flag_ref[0:8, :]) > FEW
    pl.when(many)(lambda: work(SPAN))
    pl.when(jnp.logical_not(many))(lambda: work(FEW))


def pull_slots(got_ref, route_ref, masked_ref, state_ref, root_ref, owned_ref, value_ref, pulled_ref, curve_ref, span, back):
    images = []
    for i in range(2):
        images.append(turn_in(got_ref, i)[0:span, :])
    high, low = two_parts(jnp.concatenate(images, axis=0))
    parts = jnp.concatenate([high, low], axis=1)
    ranks = iota((span, PT_DEV), 0)
    for s in range(TRACK):
        hot = owned_ref[s]
        got = dot(parts, jnp.concatenate([hot, hot], axis=0))
        here = ranks == route_ref[TRACK + s : TRACK + s + 1, :]
        for i in range(2):
            value_ref[i * TRACK + s : i * TRACK + s + 1, :] = jnp.sum(
                jnp.where(here, got[i * span : (i + 1) * span, :], 0.0), axis=0, keepdims=True
            )
    curve = jnp.zeros((TRACK, LANES), F32)
    for chunk in range(PT_DEV // LANES):
        lanes = slice(chunk * LANES, (chunk + 1) * LANES)
        point = [[masked_ref[3 * i + a, :, lanes] for a in range(3)] for i in range(2)]
        root = [root_ref[at * TRACK : (at + 1) * TRACK, lanes] for at in range(3)]
        image1 = value_ref[TRACK : 2 * TRACK, lanes] * root[2]
        image = [(value_ref[0:TRACK, lanes] - root[1] * image1) * root[0], image1]
        pulled = [over_tracks(point[0][a] * image[0] + point[1][a] * image[1]) for a in range(3)]
        inverse = [state_ref[at : at + 1, lanes] for at in range(6)]
        solved = times_inverse(inverse, pulled)
        for a in range(3):
            pulled_ref[a : a + 1, lanes] = pulled[a]
        result = [
            image[i] - (point[i][0] * solved[0] + point[i][1] * solved[1] + point[i][2] * solved[2])
            for i in range(2)
        ]
        if back:
            result0 = result[0] * root[0]
            value_ref[0:TRACK, lanes] = result0
            value_ref[TRACK : 2 * TRACK, lanes] = (result[1] - root[1] * result0) * root[2]
        else:
            curve = curve + image[0] * result[0] + image[1] * result[1]
    if not back:
        curve_ref[...] = curve


def first_point_kernel(got_ref, route_ref, masked_ref, state_ref, root_ref, flag_ref, owned_ref, pulled_ref, out_ref, value_ref, image_ref):
    image_ref[...] = jnp.zeros((2 * LANES, LANES), F32)

    def work(span):
        pull_slots(got_ref, route_ref, masked_ref, state_ref, root_ref, owned_ref, value_ref, pulled_ref, None, span, True)
        ranks = iota((span, PT_DEV), 0)
        sums = jnp.zeros((4 * span, OWNERS), F32)
        for s in range(TRACK):
            here = ranks == route_ref[TRACK + s : TRACK + s + 1, :]
            spread = []
            for i in range(2):
                value = value_ref[i * TRACK + s : i * TRACK + s + 1, :]
                spread.append(jnp.where(here, value, 0.0))
            high, low = two_parts(jnp.concatenate(spread, axis=0))
            sums = sums + dot_lanes(jnp.concatenate([high, low], axis=0), owned_ref[s])
        sums = sums[0 : 2 * span] + sums[2 * span :]
        for i in range(2):
            image_ref[i * LANES : i * LANES + span, :] = sums[i * span : (i + 1) * span, :]

    either_span(flag_ref, work)
    turn_out(image_ref, out_ref)


def second_point_kernel(got_ref, route_ref, masked_ref, state_ref, root_ref, flag_ref, owned_ref, pulled_ref, out_ref, scalar_ref, value_ref, curve_ref):
    def work(span):
        pull_slots(got_ref, route_ref, masked_ref, state_ref, root_ref, owned_ref, value_ref, pulled_ref, curve_ref, span, False)

    either_span(flag_ref, work)
    out_ref[...] = jnp.broadcast_to(total(curve_ref[...]), (OWNERS, LANES))
    scalar_ref[...] = jnp.broadcast_to(
        jnp.sum(got_ref[pl.ds(0, OWNERS, stride=2), :], axis=0, keepdims=True), (8, LANES)
    )


def second_camera_kernel(got_ref, feature_ref, factor_ref, first_ref, second_ref, out_ref, hot_ref, parts_ref, table_ref, image_ref, sum_ref, wide_ref):
    for i in range(2):
        image_ref[i * LANES : (i + 1) * LANES, :] = turn_in(got_ref, i)
    many = jnp.max(first_ref[80:84, :]) > FEW
    wide_ref[...] = jnp.zeros((LANES, LANES), F32)

    def gather_terms(block):
        hot_cameras(feature_ref, hot_ref, block)
        back = [
            image_ref[i * LANES + block * 8 : i * LANES + (block + 1) * 8, :] for i in range(2)
        ]
        for j in range(9):
            wide_ref[j * 8 : (j + 1) * 8, :] = (
                features_of(feature_ref, j, block) * back[0]
                + features_of(feature_ref, 9 + j, block) * back[1]
            )
        keep_parts(wide_ref, feature_ref, parts_ref, block, 16)

    camera_sums(gather_terms, parts_ref, hot_ref, wide_ref, sum_ref, 16, many)
    first = [first_ref[j * 8 : (j + 1) * 8, :] for j in range(9)]
    image = [first[j] + wide_ref[j * 8 : (j + 1) * 8, :] for j in range(9)]
    factor, scales = {}, []
    for at, (j, k) in enumerate(block_pairs):
        entry = factor_ref[at * 8 : (at + 1) * 8, :]
        if j == k:
            scales.append(entry)
        else:
            factor[k, j] = entry
    second = solve(factor, scales, image)
    for j in range(9):
        second_ref[j * 8 : (j + 1) * 8, :] = second[j]

    def inner(left, right):
        value = left[0] * right[0]
        for j in range(1, 9):
            value = value + left[j] * right[j]
        return value

    image_slots(second, feature_ref, table_ref, image_ref, many)
    scalars = [first_ref[72:80, :], inner(first, image), inner(image, second), inner(second, second)]
    for at, value in enumerate(scalars):
        image_ref[SPAN + at : SPAN + at + 1, :] = jnp.broadcast_to(total(value), (1, LANES))
    turn_out(image_ref, out_ref)


def finish_kernel(curve_ref, scalar_ref, first_ref, second_ref, state_ref, first_pulled_ref, second_pulled_ref, dense_camera, dense_point, camera_out, point_out, camera_ref, point_ref, camera_sem, point_sem):
    own = jnp.sum(curve_ref[...], axis=0, keepdims=True)[:, 0:1]
    energy, curvature, crossed, square = [
        scalar_ref[0:1, SPAN + at : SPAN + at + 1] for at in range(4)
    ]
    step_size = energy / curvature
    renewed = step_size * step_size * crossed - energy
    ratio = 1.0 + renewed / energy
    second_step = renewed / (
        ratio * ratio * curvature
        - 2.0 * step_size * ratio * crossed
        + step_size * step_size * (square + own)
    )
    first_weight = step_size + second_step * ratio
    second_weight = -second_step * step_size
    for c in range(3):
        camera_ref[:, c * LANES : (c + 1) * LANES] = (
            first_weight * first_ref[pl.ds(c, 9, stride=8), :]
            + second_weight * second_ref[pl.ds(c, 9, stride=8), :]
        )
    left = [
        state_ref[6 + a : 7 + a, :]
        - first_weight * first_pulled_ref[a : a + 1, :]
        - second_weight * second_pulled_ref[a : a + 1, :]
        for a in range(3)
    ]
    moved = times_inverse([state_ref[at : at + 1, :] for at in range(6)], left)
    for a in range(3):
        point_ref[a : a + 1, :] = moved[a]

    def send(camera, point):
        copies = [
            pltpu.make_async_copy(camera, camera_out, camera_sem),
            pltpu.make_async_copy(point, point_out, point_sem),
        ]
        for copy in copies:
            copy.start()
        for copy in copies:
            copy.wait()

    over = jnp.max(first_ref[84:88, :]) > CAP
    pl.when(over)(lambda: send(dense_camera, dense_point))
    pl.when(jnp.logical_not(over))(lambda: send(camera_ref, point_ref))


def call(kernel, outs, scratch, operands, in_scalar=0):
    specs = [
        pl.BlockSpec(memory_space=pltpu.SMEM if at < in_scalar else pltpu.VMEM)
        for at in range(len(operands))
    ]
    return pl.pallas_call(
        kernel,
        out_shape=[jax.ShapeDtypeStruct(shape, dtype) for shape, dtype in outs],
        in_specs=specs,
        out_specs=[
            pl.BlockSpec(memory_space=pltpu.SMEM if shape == (1, 1) else pltpu.VMEM)
            for shape, unused in outs
        ],
        scratch_shapes=[pltpu.VMEM(shape, dtype) for shape, dtype in scratch],
        compiler_params=PARAMS,
    )(*operands)


def exchange(rows):
    blocks = rows.reshape(OWNERS, 1, -1)
    blocks = lax.all_to_all(blocks, ("row", "col"), split_axis=0, concat_axis=0, tiled=True)
    return blocks.reshape(rows.shape)


def by_slots(camera_jacobian, point_jacobian, residuals, observed_camera, track_length):
    lengths = track_length.reshape(1, PT_DEV)
    in_vmem = [pl.BlockSpec(memory_space=pltpu.VMEM)]
    held = [(18, TRACK, PT_DEV), (6, TRACK, PT_DEV), (2, TRACK, PT_DEV)]
    outs = [
        ((OWNERS * ROWS, LANES), F32),
        ((2 * TRACK, PT_DEV), jnp.int32),
        ((16, PT_DEV), F32),
        ((3 * TRACK, PT_DEV), F32),
        ((OWNERS, LANES), F32),
        ((TRACK, OWNERS, PT_DEV), BF16),
        ((6, TRACK, PT_DEV), F32),
    ]
    sent, route, state, root, flag, owned, masked = pl.pallas_call(
        prepare_kernel,
        out_shape=[jax.ShapeDtypeStruct(shape, dtype) for shape, dtype in outs],
        in_specs=[pl.BlockSpec(memory_space=pl.ANY)] * 3 + in_vmem * 2,
        out_specs=in_vmem * len(outs),
        scratch_shapes=[pltpu.VMEM(shape, F32) for shape in held]
        + [
            pltpu.VMEM((WIDTH * BLOCKS, LANES), F32),
            pltpu.VMEM((BLOCKS, LANES), jnp.int32),
            pltpu.SMEM((BLOCKS, LANES), jnp.int32),
            pltpu.VMEM((BLOCKS, LANES, 1, LANES), F32),
            pltpu.VMEM((GROUPS * OWNERS * ROWS + 8, 1, LANES), F32),
        ]
        + [pltpu.SemaphoreType.DMA] * 4,
        compiler_params=PARAMS,
    )(camera_jacobian, point_jacobian, residuals, observed_camera, lengths)
    hot = ((LANES, SPAN * LANES), BF16)
    table = ((27 * 8, LANES), F32)
    image = ((2 * LANES, LANES), F32)
    pair = ((2 * OWNERS, LANES), F32)
    features, factor, first, out, overflow = call(
        first_camera_kernel,
        [((WIDTH * SPAN, LANES), F32), ((45 * 8, LANES), F32), ((88, LANES), F32), pair, ((1, 1), jnp.int32)],
        [hot, ((6 * ENTRIES, SPAN * LANES), BF16), table, image, ((6 * ENTRIES, LANES), F32), ((ENTRIES * 8, LANES), F32)],
        (exchange(sent),),
    )
    first_pulled, out = call(
        first_point_kernel,
        [((8, PT_DEV), F32), pair],
        [((2 * TRACK, PT_DEV), F32), image],
        (exchange(out), route, masked, state, root, flag, owned),
    )
    second, out = call(
        second_camera_kernel,
        [((72, LANES), F32), pair],
        [hot, ((96, SPAN * LANES), BF16), table, image, ((96, LANES), F32), ((LANES, LANES), F32)],
        (exchange(out), features, factor, first),
    )
    second_pulled, curve, scalars = call(
        second_point_kernel,
        [((8, PT_DEV), F32), ((OWNERS, LANES), F32), ((8, LANES), F32)],
        [((2 * TRACK, PT_DEV), F32), ((TRACK, LANES), F32)],
        (exchange(out), route, masked, state, root, flag, owned),
    )
    overflow, curve = lax.optimization_barrier((overflow, exchange(curve)))
    return overflow[0, 0], (curve, scalars, first, second, state, first_pulled, second_pulled)


def finish(*operands):
    shapes = [(9, CAM_DEV), (3, PT_DEV)]
    return tuple(
        pl.pallas_call(
            finish_kernel,
            out_shape=[jax.ShapeDtypeStruct(shape, F32) for shape in shapes],
            in_specs=[pl.BlockSpec(memory_space=pltpu.VMEM)] * len(operands),
            out_specs=[pl.BlockSpec(memory_space=pltpu.HBM)] * 2,
            scratch_shapes=[pltpu.VMEM(shape, F32) for shape in shapes]
            + [pltpu.SemaphoreType.DMA] * 2,
            compiler_params=PARAMS,
        )(*operands)
    )


damping = 1.0


def inverse_small(matrix):
    entries = [[matrix[row_at, col_at] for col_at in range(3)] for row_at in range(3)]
    cofactor = [
        [
            entries[(row_at + 1) % 3][(col_at + 1) % 3]
            * entries[(row_at + 2) % 3][(col_at + 2) % 3]
            - entries[(row_at + 1) % 3][(col_at + 2) % 3]
            * entries[(row_at + 2) % 3][(col_at + 1) % 3]
            for col_at in range(3)
        ]
        for row_at in range(3)
    ]
    determinant = (
        entries[0][0] * cofactor[0][0]
        + entries[0][1] * cofactor[0][1]
        + entries[0][2] * cofactor[0][2]
    )
    return jnp.stack(
        [
            jnp.stack([cofactor[col_at][row_at] / determinant for col_at in range(3)])
            for row_at in range(3)
        ]
    )


def block_inverse(matrix):
    factor = {}
    for col_at in range(9):
        pivot_value = matrix[col_at, col_at]
        for middle in range(col_at):
            pivot_value = pivot_value - factor[col_at, middle] * factor[col_at, middle]
        diagonal_root = jnp.sqrt(pivot_value)
        factor[col_at, col_at] = diagonal_root
        for row_at in range(col_at + 1, 9):
            running = matrix[row_at, col_at]
            for middle in range(col_at):
                running = running - factor[row_at, middle] * factor[col_at, middle]
            factor[row_at, col_at] = running / diagonal_root
    factor_inverse = {}
    for row_at in range(9):
        factor_inverse[row_at, row_at] = 1.0 / factor[row_at, row_at]
        for col_at in range(row_at):
            running = factor[row_at, col_at] * factor_inverse[col_at, col_at]
            for middle in range(col_at + 1, row_at):
                running = running + factor[row_at, middle] * factor_inverse[middle, col_at]
            factor_inverse[row_at, col_at] = -running / factor[row_at, row_at]
    result_rows = []
    for row_at in range(9):
        entries = []
        for col_at in range(9):
            running = (
                factor_inverse[max(row_at, col_at), row_at]
                * factor_inverse[max(row_at, col_at), col_at]
            )
            for middle in range(max(row_at, col_at) + 1, 9):
                running = running + factor_inverse[middle, row_at] * factor_inverse[middle, col_at]
            entries.append(running)
        result_rows.append(jnp.stack(entries))
    return jnp.stack(result_rows)


def assemble(packed):
    positions = {}
    for index_at, pair in enumerate(block_pairs):
        positions[pair[0], pair[1]] = index_at
        positions[pair[1], pair[0]] = index_at
    return jnp.stack(
        [
            jnp.stack(
                [
                    packed[positions[row_at, col_at]] + (damping if row_at == col_at else 0.0)
                    for col_at in range(9)
                ]
            )
            for row_at in range(9)
        ]
    )


def apply_blocks(inverse_blocks, vector):
    return jnp.sum(inverse_blocks * vector[None], axis=1)


def slot_basics(camera_jacobian, point_jacobian, residuals, track_length):
    tracks = camera_jacobian.shape[1]
    in_track = (jnp.arange(tracks, dtype=jnp.int32)[:, None] < track_length[None, :]).astype(
        jnp.float32
    )
    camera_blocks = camera_jacobian.reshape(2, 9, tracks, -1) * in_track
    point_blocks = point_jacobian.reshape(2, 3, tracks, -1) * in_track
    errors = residuals * in_track
    coupling = jnp.sum(camera_blocks[:, :, None] * point_blocks[:, None], axis=0)
    point_system = jnp.sum(point_blocks[:, :, None] * point_blocks[:, None], axis=(0, 3))
    point_system = point_system + damping * jnp.eye(3, dtype=jnp.float32)[:, :, None]
    point_inverse = inverse_small(point_system)
    point_gradient = -jnp.sum(point_blocks * errors[:, None], axis=(0, 2))
    return (camera_blocks, errors, coupling, point_inverse, point_gradient)


def camera_terms(camera_blocks, errors, coupling, point_inverse, point_gradient):
    solved = jnp.sum(point_inverse * point_gradient[None], axis=1)
    scaled = coupling[:, 0][:, None] * point_inverse[0][None, :, None, :]
    for middle in range(1, 3):
        scaled = scaled + coupling[:, middle][:, None] * point_inverse[middle][None, :, None, :]
    packed = []
    for leading, trailing in block_pairs:
        packed.append(
            jnp.sum(camera_blocks[:, leading] * camera_blocks[:, trailing], axis=0)
            - jnp.sum(scaled[leading] * coupling[trailing], axis=0)
        )
    right_side = -jnp.sum(camera_blocks * errors[:, None], axis=0) - jnp.sum(
        coupling * solved[None, :, None], axis=1
    )
    return jnp.concatenate([jnp.stack(packed), right_side], axis=0)


def slot_product(camera_blocks, coupling, point_inverse, gathered):
    projected = jnp.sum(camera_blocks * gathered[None], axis=1)
    pulled = jnp.sum(coupling * gathered[:, None], axis=(0, 2))
    solved = jnp.sum(point_inverse * pulled[None], axis=1)
    return jnp.sum(camera_blocks * projected[:, None], axis=0) - jnp.sum(
        coupling * solved[None, :, None], axis=1
    )


def by_dense(camera_jacobian, point_jacobian, residuals, observed_camera, track_length):
    camera_blocks, errors, coupling, point_inverse, point_gradient = slot_basics(
        camera_jacobian, point_jacobian, residuals, track_length
    )
    tracks, points = observed_camera.shape
    rows, cols = lax.axis_size("row"), lax.axis_size("col")
    cameras = CAM_DEV * rows * cols
    flat_cameras = observed_camera.reshape(-1)

    def into_cameras(values):
        width = values.shape[0]
        by_camera = (
            jnp.zeros((cameras, width), jnp.float32).at[flat_cameras].add(jnp.transpose(values))
        )
        return jnp.transpose(by_camera)

    def pick_slots(whole):
        slot_rows = jnp.transpose(whole)[flat_cameras]
        return jnp.transpose(slot_rows).reshape(9, tracks, points)

    def spread_out(value):
        copies = jnp.broadcast_to(value[:, None], (9, OWNERS, CAM_DEV)).reshape(9, cameras)
        return lax.all_to_all(copies, ("row", "col"), split_axis=1, concat_axis=1, tiled=True)

    term_values = camera_terms(
        camera_blocks, errors, coupling, point_inverse, point_gradient
    ).reshape(54, -1)
    local_terms = into_cameras(term_values).reshape(54, rows * cols, CAM_DEV)
    own_terms = jnp.sum(
        lax.all_to_all(local_terms, ("row", "col"), split_axis=1, concat_axis=1, tiled=True), axis=1
    )
    inverse_blocks = block_inverse(assemble(own_terms[:45]))
    right_side = own_terms[45:]

    first = apply_blocks(inverse_blocks, right_side)
    first_slots = pick_slots(spread_out(first))
    first_pulled = jnp.sum(coupling * first_slots[:, None], axis=(0, 2))
    contrib = slot_product(camera_blocks, coupling, point_inverse, first_slots)
    local_image = into_cameras(contrib.reshape(9, -1)).reshape(9, OWNERS, CAM_DEV)
    gathered_image = lax.all_to_all(
        local_image, ("row", "col"), split_axis=1, concat_axis=1, tiled=True
    )
    first_image = damping * first + jnp.sum(gathered_image, axis=1)

    second = apply_blocks(inverse_blocks, first_image)
    second_slots = pick_slots(spread_out(second))
    second_pulled = jnp.sum(coupling * second_slots[:, None], axis=(0, 2))
    projected = jnp.sum(camera_blocks * second_slots[None], axis=1)
    solved = jnp.sum(point_inverse * second_pulled[None], axis=1)
    own_sums = jnp.stack(
        [
            jnp.sum(right_side * first),
            jnp.sum(first * first_image),
            jnp.sum(first_image * second),
            jnp.sum(second * second)
            + jnp.sum(projected * projected)
            - jnp.sum(second_pulled * solved),
        ]
    )
    spread = jnp.broadcast_to(own_sums[None], (OWNERS, 4))
    energy, curvature, crossed, second_curvature = jnp.sum(exchange(spread), axis=0)
    step_size = energy / curvature
    renewed = step_size * step_size * crossed - energy
    ratio = 1.0 + renewed / energy
    second_step = renewed / (
        ratio * ratio * curvature
        - 2.0 * step_size * ratio * crossed
        + step_size * step_size * second_curvature
    )
    first_weight = step_size + second_step * ratio
    second_weight = -second_step * step_size
    camera_move = first_weight * first + second_weight * second
    pulled = first_weight * first_pulled + second_weight * second_pulled
    point_move = jnp.sum(point_inverse * (point_gradient - pulled)[None], axis=1)
    return (camera_move, point_move)


def on_device(camera_jacobian, point_jacobian, residuals, observed_camera, track_length):
    operands = (camera_jacobian, point_jacobian, residuals, observed_camera, track_length)
    overflow, kept = by_slots(*operands)
    dense = lax.cond(
        overflow > 0,
        lambda *given: by_dense(*given),
        lambda *given: (jnp.zeros((9, CAM_DEV), F32), jnp.zeros((3, PT_DEV), F32)),
        *operands,
    )
    return finish(*kept, *dense)


def solution(mesh):
    in_specs = (
        P(None, None, ("row", "col")),
        P(None, None, ("row", "col")),
        P(None, None, ("row", "col")),
        P(None, ("row", "col")),
        P(("row", "col")),
    )
    out_specs = (P(None, ("row", "col")), P(None, ("row", "col")))
    return jax.shard_map(
        on_device, mesh=mesh, in_specs=in_specs, out_specs=out_specs, check_vma=False
    )
```
